1024 devices in a mesh: row: 64 (over y, z_lo, core), col: 16 (over x, z_hi).
Axes of the slice: x: 4, y: 8, z: 16 (z_hi: 4, z_lo: 4; z = z_hi * 4 + z_lo), core: 2. Of those that a mesh axis runs over, the one named last changes fastest.
Arguments:
- populations: float32 [19, 8, 512, 2048], P(None, None, 'row', 'col'), may hold values from 0 to 0.6, as said below
- order_tensor: float32 [5, 8, 512, 2048], P(None, None, 'row', 'col'), may hold values from -0.8 to 0.8
Outputs:
- new_populations: float32 [19, 8, 512, 2048], P(None, None, 'row', 'col')
- new_order: float32 [5, 8, 512, 2048], P(None, None, 'row', 'col')
The draws below stay inside these ranges and needn't reach their ends.
Inputs may be any that keep to these rules, and one draw needn't show every extreme that they name: `populations`: each population lies between 0.3 and 1.7 times its lattice weight.
All inputs are finite; a program needn't handle non-finite values.
Results may differ from the reference program's by a relative error of at most 0.0001.
Values sent between devices are 32-bit elements; how exact they have to be, the bound alone decides.
No kernel may reach another device: no remote copies, remote signals or barrier semaphores. Data moves between devices by JAX's collectives and lax.ppermute only.
A program may use at most 32 MiB of HBM per device.

```python
import math
import jax
import jax.numpy as jnp
import numpy as np
from jax import lax

SUBSTEPS = 3
NX = 512
NY = 2048
NZ = 8


def draw_populations(key, part):
    key = jax.random.fold_in(key, 11)
    weights = jnp.array([1.0 / 3.0] + [1.0 / 18.0] * 6 + [1.0 / 36.0] * 12, jnp.float32)
    factor = jax.random.uniform(key, (19, NZ, NX, NY), jnp.float32, 0.6, 1.4)
    return weights[:, None, None, None] * factor


def draw_order_tensor(key, part):
    key = jax.random.fold_in(key, 23)
    return jnp.clip(0.2 * jax.random.normal(key, (5, NZ, NX, NY), jnp.float32), -0.8, 0.8)


def setup_inputs(seed: int = 0) -> dict:
    arg_keys = jax.random.split(jax.random.key(seed), 3)
    return {
        "populations": draw_populations(jax.random.fold_in(arg_keys[2], 71), 0),
        "order_tensor": draw_order_tensor(jax.random.fold_in(arg_keys[2], 71), 0),
    }


lattice = np.array([[0, 0, 0], [1, 0, 0], [-1, 0, 0], [0, 1, 0], [0, -1, 0], [0, 0, 1], [0, 0, -1],
                    [1, 1, 0], [-1, -1, 0], [1, -1, 0], [-1, 1, 0], [1, 0, 1], [-1, 0, -1], [1, 0, -1],
                    [-1, 0, 1], [0, 1, 1], [0, -1, -1], [0, 1, -1], [0, -1, 1]])
lattice_weights = np.array([1.0 / 3.0] + [1.0 / 18.0] * 6 + [1.0 / 36.0] * 12)
tau_rate = 1.25
a_zero = 0.1
gamma_bulk = 3.0
stiffness = 0.4
pitch_wave = math.pi / 8.0
mobility_dt = 0.3
levi_terms = ((0, 1, 2, 1.0), (1, 2, 0, 1.0), (2, 0, 1, 1.0), (0, 2, 1, -1.0), (2, 1, 0, -1.0), (1, 0, 2, -1.0))
index_pairs = ((0, 0), (0, 1), (0, 2), (1, 1), (1, 2))


def full_tensor(components):
    trace_part = -components[0] - components[3]
    return [[components[0], components[1], components[2]],
            [components[1], components[3], components[4]],
            [components[2], components[4], trace_part]]


def relax_step(center, laplace, gradient, velocity, want_force):
    tensor = full_tensor(center)
    slopes = [full_tensor(gradient[c]) for c in range(3)]
    square_sum = sum(tensor[a][b] * tensor[a][b] for a in range(3) for b in range(3))
    fields = []
    updated = []
    for k, (a, b) in enumerate(index_pairs):
        product = tensor[a][0] * tensor[0][b] + tensor[a][1] * tensor[1][b] + tensor[a][2] * tensor[2][b]
        chiral = jnp.zeros_like(product)
        for i, c, d, s in levi_terms:
            if i == a:
                chiral = chiral + s * slopes[c][d][b]
            if i == b:
                chiral = chiral + s * slopes[c][d][a]
        isotropic = square_sum / 3.0 if a == b else 0.0
        bulk_term = (a_zero * (gamma_bulk / 3.0 - 1.0) * tensor[a][b]
                     + a_zero * gamma_bulk * (product - isotropic)
                     - a_zero * gamma_bulk * square_sum * tensor[a][b])
        molecular = bulk_term + stiffness * (laplace[k] - 4.0 * pitch_wave ** 2 * tensor[a][b] - 2.0 * pitch_wave * chiral)
        fields.append(molecular)
        carried = velocity[0] * gradient[0][k] + velocity[1] * gradient[1][k] + velocity[2] * gradient[2][k]
        updated.append(center[k] + mobility_dt * molecular - carried)
    if not want_force:
        return updated, None
    field_full = full_tensor(fields)
    body_force = [sum(field_full[b][c] * slopes[a][b][c] for b in range(3) for c in range(3)) for a in range(3)]
    return updated, body_force


def stencil_terms(center, x_ahead, x_behind, y_ahead, y_behind):
    z_ahead = jnp.roll(center, -1, axis=0)
    z_behind = jnp.roll(center, 1, axis=0)
    laplace = x_ahead + x_behind + y_ahead + y_behind + z_ahead + z_behind - 6.0 * center
    gradient = [0.5 * (x_ahead - x_behind), 0.5 * (y_ahead - y_behind), 0.5 * (z_ahead - z_behind)]
    return laplace, gradient


def moments(populations):
    lattice_table = jnp.asarray(lattice, jnp.float32)
    density = jnp.sum(populations, axis=0)
    momentum = jnp.einsum("ia,izxy->azxy", lattice_table, populations, precision=lax.Precision.HIGHEST)
    return density, momentum


def collide(populations, density, momentum, body_force):
    lattice_table = jnp.asarray(lattice, jnp.float32)
    weight_column = jnp.asarray(lattice_weights, jnp.float32)[:, None, None, None]
    velocity = (momentum + 0.5 * body_force) / density[None]
    along_speed = jnp.einsum("ia,azxy->izxy", lattice_table, velocity, precision=lax.Precision.HIGHEST)
    along_force = jnp.einsum("ia,azxy->izxy", lattice_table, body_force, precision=lax.Precision.HIGHEST)
    speed_squared = jnp.sum(velocity * velocity, axis=0)
    speed_force = jnp.sum(velocity * body_force, axis=0)
    equilibrium = weight_column * density[None] * (1.0 + 3.0 * along_speed + 4.5 * along_speed * along_speed - 1.5 * speed_squared[None])
    source = weight_column * (3.0 * (along_force - speed_force[None]) + 9.0 * along_speed * along_force)
    return populations - tau_rate * (populations - equilibrium) + (1.0 - 0.5 * tau_rate) * source


def reference(populations, order_tensor):
    density, momentum = moments(populations)
    velocity = [momentum[a] / density for a in range(3)]
    components = [order_tensor[k] for k in range(5)]
    body_force = None
    for substep in range(SUBSTEPS):
        laplace = []
        per_component = []
        for k in range(5):
            field_now = components[k]
            lap_term, grad_term = stencil_terms(field_now, jnp.roll(field_now, -1, axis=1), jnp.roll(field_now, 1, axis=1),
                                                jnp.roll(field_now, -1, axis=2), jnp.roll(field_now, 1, axis=2))
            laplace.append(lap_term)
            per_component.append(grad_term)
        gradient = [[per_component[k][c] for k in range(5)] for c in range(3)]
        components, body_force = relax_step(components, laplace, gradient, velocity, substep == SUBSTEPS - 1)
    collided = collide(populations, density, momentum, jnp.stack(body_force))
    arrived = []
    for i in range(19):
        a, b, c = int(lattice[i][0]), int(lattice[i][1]), int(lattice[i][2])
        arrived.append(jnp.roll(collided[i], (c, a, b), axis=(0, 1, 2)))
    return jnp.stack(arrived), jnp.stack(components)
```

```python
import functools
import math

import jax
import jax.numpy as jnp
import numpy as np
from jax import lax
from jax.experimental import pallas as pl
from jax.experimental.pallas import tpu as pltpu
from jax.sharding import PartitionSpec as P

lattice = np.array(
    [
        [0, 0, 0],
        [1, 0, 0],
        [-1, 0, 0],
        [0, 1, 0],
        [0, -1, 0],
        [0, 0, 1],
        [0, 0, -1],
        [1, 1, 0],
        [-1, -1, 0],
        [1, -1, 0],
        [-1, 1, 0],
        [1, 0, 1],
        [-1, 0, -1],
        [1, 0, -1],
        [-1, 0, 1],
        [0, 1, 1],
        [0, -1, -1],
        [0, 1, -1],
        [0, -1, 1],
    ]
)
tau_rate = 1.25
a_zero = 0.1
gamma_bulk = 3.0
stiffness = 0.4
pitch_wave = math.pi / 8.0
mobility_dt = 0.3

x_up = [i for i in range(19) if lattice[i][0] == 1]
x_down = [i + 1 for i in x_up]
y_up = [i for i in range(19) if lattice[i][1] == 1]
y_down = [i for i in range(19) if lattice[i][1] == -1]

VEL, DEN, POP, FACE = 20, 29, 30, 35
SLOTS = 16
FIELDS = 28
f32 = jnp.float32


def lanes():
    return lax.broadcasted_iota(jnp.int32, (8, 128), 1)


def slots():
    return lax.rem(lanes(), SLOTS)


def roll_y(value, shift):
    shift = shift % 128
    return value if shift == 0 else pltpu.roll(value, shift, 1)


def roll_z(value, shift):
    shift = shift % 8
    return value if shift == 0 else pltpu.roll(value, shift, 0)


def is_even(axis):
    return lax.rem(lax.axis_index(axis), 2) == 0


def stencil(center, x_ahead, x_behind):
    y_ahead, y_behind = roll_y(center, -1), roll_y(center, 1)
    z_ahead, z_behind = roll_z(center, -1), roll_z(center, 1)
    around = (x_ahead + x_behind) + (y_ahead + y_behind) + (z_ahead + z_behind)
    return around, (x_ahead - x_behind, y_ahead - y_behind, z_ahead - z_behind)


def molecular_field(q, around, dx, dy, dz):
    q0, q1, q2, q3, q4 = q
    qzz = -(q0 + q3)
    s0, s1, s2, s3, s4 = q0 * q0, q1 * q1, q2 * q2, q3 * q3, q4 * q4
    square = s0 + s3 + qzz * qzz + 2.0 * (s1 + s2 + s4)
    third = square * (1.0 / 3.0)
    bulk = a_zero * gamma_bulk
    product = (
        s0 + s1 + s2 - third,
        q2 * q4 - q1 * qzz,
        q1 * q4 - q2 * q3,
        s1 + s3 + s4 - third,
        q1 * q2 - q4 * q0,
    )
    chiral = (
        2.0 * (dy[2] - dz[1]),
        (dy[4] - dx[2]) + (dz[0] - dz[3]),
        (dx[1] - dz[4]) - (2.0 * dy[0] + dy[3]),
        2.0 * (dz[1] - dx[4]),
        (dz[2] - dy[1]) + (dx[0] + 2.0 * dx[3]),
    )
    linear = a_zero * (gamma_bulk / 3.0 - 1.0) - stiffness * (4.0 * pitch_wave**2 + 6.0)
    factor = linear - bulk * square
    return [
        bulk * product[k]
        + factor * q[k]
        + stiffness * around[k]
        - (stiffness * pitch_wave) * chiral[k]
        for k in range(5)
    ]


def gather_stencil(load):
    q, around, dx, dy, dz = [], [], [], [], []
    for k in range(5):
        center, ahead, behind = load(k)
        total, (a, b, c) = stencil(center, ahead, behind)
        q.append(center)
        around.append(total)
        dx.append(a)
        dy.append(b)
        dz.append(c)
    return q, around, dx, dy, dz


def updated(q, field, dx, dy, dz, velocity):
    hx, hy, hz = (0.5 * v for v in velocity)
    return [
        q[k] + mobility_dt * field[k] - (hx * dx[k] + hy * dy[k] + hz * dz[k]) for k in range(5)
    ]


def force_of(field, dx, dy, dz):
    first = field[0] + 0.5 * field[3]
    second = field[3] + 0.5 * field[0]
    return [
        first * d[0] + second * d[3] + field[1] * d[1] + field[2] * d[2] + field[4] * d[4]
        for d in (dx, dy, dz)
    ]


def collide(which, load, density, velocity, force):
    half = 0.5 / density
    u = [velocity[a] + force[a] * half for a in range(3)]
    speed = u[0] * u[0] + u[1] * u[1] + u[2] * u[2]
    along = u[0] * force[0] + u[1] * force[1] + u[2] * force[2]
    keep = 1.0 - 0.5 * tau_rate
    base = (tau_rate * density) * (1.0 - 1.5 * speed) - (3.0 * keep) * along
    odd = [(3.0 * tau_rate) * density * u[a] + (3.0 * keep) * force[a] for a in range(3)]
    even = [(4.5 * tau_rate) * density * u[a] + (9.0 * keep) * force[a] for a in range(3)]

    def dot(c, vector):
        total = None
        for a in range(3):
            if c[a]:
                term = vector[a]
                if total is None:
                    total = term if c[a] > 0 else -term
                else:
                    total = total + term if c[a] > 0 else total - term
        return total

    rest = 1.0 - tau_rate
    done = set()
    for i in which:
        if i in done:
            continue
        if i == 0:
            yield 0, rest * load(0) + (1.0 / 3.0) * base
            continue
        low = i if i % 2 else i - 1
        c = [int(v) for v in lattice[low]]
        weight = 1.0 / 18.0 if low < 7 else 1.0 / 36.0
        first = weight * (base + dot(c, u) * dot(c, even))
        second = weight * dot(c, odd)
        for j, sign in ((low, 1), (low + 1, -1)):
            if j in which:
                done.add(j)
                yield j, rest * load(j) + (first + second if sign > 0 else first - second)


def moments_kernel(pop_ref, order_ref, base_ref, first_ref, second_ref):
    def row(x, carry):
        p = [pop_ref[i, pl.ds(x, 8, stride=8), :] for i in range(19)]
        density = p[0]
        for i in range(1, 19):
            density = density + p[i]
        inverse = 1.0 / density
        for a in range(3):
            plus = [p[i] for i in range(19) if lattice[i][a] == 1]
            minus = [p[i] for i in range(19) if lattice[i][a] == -1]
            momentum = functools.reduce(lambda s, t: s + t, plus) - functools.reduce(
                lambda s, t: s + t, minus
            )
            base_ref[5 + a, x] = momentum * inverse
        base_ref[8, x] = density
        for k in range(5):
            base_ref[k, x] = order_ref[k, pl.ds(x, 8, stride=8), :]
        return carry

    lax.fori_loop(0, 8, row, 0)
    even = is_even("row")
    for out, high in ((first_ref, even), (second_ref, jnp.logical_not(even))):

        @pl.when(high)
        def _():
            for k in range(5):
                out[4 * k : 4 * k + 4] = base_ref[k, 4:8]
            for a in range(3):
                out[VEL + 3 * a : VEL + 3 * a + 3] = base_ref[5 + a, 5:8]
            out[DEN] = base_ref[8, 7]
            for j, i in enumerate(x_up):
                out[POP + j] = pop_ref[i, pl.ds(7, 8, stride=8), :]

        @pl.when(jnp.logical_not(high))
        def _():
            for k in range(5):
                out[4 * k : 4 * k + 4] = base_ref[k, 0:4]
            for a in range(3):
                out[VEL + 3 * a : VEL + 3 * a + 3] = base_ref[5 + a, 0:3]
            out[DEN] = base_ref[8, 0]
            for j, i in enumerate(x_down):
                out[POP + j] = pop_ref[i, pl.ds(0, 8, stride=8), :]


def placed(value, row, into):
    q = row % 8
    lane = lanes()
    mask = jnp.logical_and(lane >= SLOTS * q, lane < SLOTS * q + SLOTS)
    return jnp.where(mask, roll_y(value, 8 + SLOTS * q), into)


def own_edges_kernel(base_ref, pop_ref, edge_ref):
    def pack(load, fill, field):
        low = high = jnp.full((8, 128), fill, f32)
        for x in range(4):
            low = placed(load(x), x + 4, low)
            high = placed(load(x + 4), x + 8, high)
        edge_ref[field, 0] = low
        edge_ref[field, 1] = high

    def base_field(f, carry):
        pack(lambda x: base_ref[f, x], 0.0, f)
        return carry

    def pop_field(i, carry):
        pack(lambda x: pop_ref[i, pl.ds(x, 8, stride=8), :], 0.0, 9 + i)
        return carry

    lax.fori_loop(0, 8, base_field, 0)
    pack(lambda x: base_ref[8, x], 1.0, 8)
    lax.fori_loop(0, 19, pop_field, 0)


def column_message_kernel(own_ref, recv_a, recv_b, edge_ref, first_ref, second_ref):
    even = is_even("row")
    slot = slots()

    def halo(j):
        a, b = recv_a[j], recv_b[j]
        return jnp.where(even, b, a), jnp.where(even, a, b)

    def widen(field, rows):
        low, high = own_ref[field, 0], own_ref[field, 1]
        for j_low, j_high, row_low, row_high in rows:
            if j_low == j_high:
                below, above = halo(j_low)
                low, high = placed(below, row_low, low), placed(above, row_high, high)
        edge_ref[field, 0] = low
        edge_ref[field, 1] = high

    for k in range(5):
        widen(k, [(4 * k + r, 4 * k + r, r, 12 + r) for r in range(4)])
    for a in range(3):
        widen(5 + a, [(VEL + 3 * a + r, VEL + 3 * a + r, 1 + r, 12 + r) for r in range(3)])
    widen(8, [(DEN, DEN, 3, 12)])
    for i in range(19):
        low, high = own_ref[9 + i, 0], own_ref[9 + i, 1]
        if i in x_up:
            low = placed(halo(POP + x_up.index(i))[0], 3, low)
        if i in x_down:
            high = placed(halo(POP + x_down.index(i))[1], 12, high)
        edge_ref[9 + i, 0] = low
        edge_ref[9 + i, 1] = high

    col_even = is_even("col")
    for h in range(2):
        for g, parts in enumerate(((0, 1, 2, 3), (4, 5, 6, 7))):
            to_left = to_right = jnp.zeros((8, 128), f32)
            for u, f in enumerate(parts):
                value = edge_ref[f, h]
                mask = jnp.logical_and(slot >= 4 * u, slot < 4 * u + 4)
                to_left = jnp.where(mask, roll_y(value, 4 * u - 8), to_left)
                to_right = jnp.where(mask, roll_y(value, 4 * u - 4), to_right)
            first_ref[2 * g + h] = jnp.where(col_even, to_right, to_left)
            second_ref[2 * g + h] = jnp.where(col_even, to_left, to_right)
        to_left = to_right = jnp.zeros((8, 128), f32)
        for s in range(6):
            left_field = 8 if s == 0 else 9 + y_down[s - 1]
            right_field = 8 if s == 0 else 9 + y_up[s - 1]
            to_left = jnp.where(slot == s, roll_y(edge_ref[left_field, h], s - 8), to_left)
            to_right = jnp.where(slot == s, roll_y(edge_ref[right_field, h], s - 7), to_right)
        first_ref[4 + h] = jnp.where(col_even, to_right, to_left)
        second_ref[4 + h] = jnp.where(col_even, to_left, to_right)


def main_kernel(
    base_ref, recv_a, recv_b, pop_ref, moved_ref, order_ref, q_zero, q_one, q_two, vel, den
):
    even = is_even("row")

    def halo(j):
        a, b = recv_a[j], recv_b[j]
        return jnp.where(even, b, a), jnp.where(even, a, b)

    for k in range(5):
        q_zero[k, 4:12] = base_ref[k]
        for r in range(4):
            q_zero[k, r], q_zero[k, 12 + r] = halo(4 * k + r)
    for a in range(3):
        vel[a, 3:11] = base_ref[5 + a]
        for r in range(3):
            vel[a, r], vel[a, 11 + r] = halo(VEL + 3 * a + r)
    den[0], den[9] = halo(DEN)

    def relax(source, target):
        def row(r, carry):
            q, around, dx, dy, dz = gather_stencil(
                lambda k: (source[k, r], source[k, r + 1], source[k, r - 1])
            )
            field = molecular_field(q, around, dx, dy, dz)
            new = updated(q, field, dx, dy, dz, [vel[a, r - 1] for a in range(3)])
            for k in range(5):
                target[k, r] = new[k]
            return carry

        return row

    lax.fori_loop(1, 15, relax(q_zero, q_one), 0)
    lax.fori_loop(2, 14, relax(q_one, q_two), 0)

    def last(x):
        q, around, dx, dy, dz = gather_stencil(
            lambda k: (q_two[k, x + 4], q_two[k, x + 5], q_two[k, x + 3])
        )
        field = molecular_field(q, around, dx, dy, dz)
        velocity = [vel[a, x + 3] for a in range(3)]
        return q, field, dx, dy, dz, velocity, force_of(field, dx, dy, dz)

    def stream(i, value, row):
        a, b, c = (int(v) for v in lattice[i])
        moved_ref[i, row + a] = roll_y(roll_z(value, c), b)

    def own_row(x, carry):
        q, field, dx, dy, dz, velocity, force = last(x)
        new = updated(q, field, dx, dy, dz, velocity)
        for k in range(5):
            order_ref[k, x] = new[k]
        for i, value in collide(
            range(19),
            lambda i: pop_ref[i, pl.ds(x, 8, stride=8), :],
            base_ref[8, x],
            velocity,
            force,
        ):
            stream(i, value, x + 1)
        return carry

    lax.fori_loop(0, 8, own_row, 0)
    for x, which, side in ((-1, x_up, 0), (8, x_down, 1)):
        _, _, _, _, _, velocity, force = last(x)
        for i, value in collide(
            which,
            lambda i, which=which, side=side: halo(POP + which.index(i))[side],
            den[9 * side],
            velocity,
            force,
        ):
            stream(i, value, x + 1)


def edge_kernel(
    edge_ref, recv_a, recv_b, moved_ref, order_ref, out_pop, out_order, strip, q_one, q_two, done
):
    even = is_even("col")
    slot, lane = slots(), lanes()

    def columns(j):
        a, b = recv_a[j], recv_b[j]
        return jnp.where(even, b, a), jnp.where(even, a, b)

    for h in range(2):
        for f in range(8):
            from_left, from_right = columns(2 * (f // 4) + h)
            u = f % 4
            own = edge_ref[f, h]
            strip[f, h] = jnp.where(slot < 4, roll_y(from_left, -4 * u), roll_y(own, -4))
            strip[f, 2 + h] = jnp.where(slot < 8, own, roll_y(from_right, 8 - 4 * u))
        from_left, from_right = columns(4 + h)
        for f in range(8, FIELDS):
            own = edge_ref[f, h]
            left, right = roll_y(own, -4), own
            if f == 8 or f - 9 in y_up:
                s = 0 if f == 8 else 1 + y_up.index(f - 9)
                left = jnp.where(slot == 3, roll_y(from_left, 3 - s), left)
            if f == 8 or f - 9 in y_down:
                s = 0 if f == 8 else 1 + y_down.index(f - 9)
                right = jnp.where(slot == 8, roll_y(from_right, 8 - s), right)
            strip[f, h] = left
            strip[f, 2 + h] = right

    def neighbours(source, unit):
        other = jnp.bitwise_xor(unit, 1)

        def load(k):
            me, that = source[k, unit], source[k, other]
            ahead = jnp.where(lane >= 112, roll_y(that, -16), roll_y(me, -16))
            behind = jnp.where(lane < 16, roll_y(that, 16), roll_y(me, 16))
            return me, ahead, behind

        return load

    def relax(source, target):
        def step(unit, carry):
            q, around, dx, dy, dz = gather_stencil(neighbours(source, unit))
            field = molecular_field(q, around, dx, dy, dz)
            new = updated(q, field, dx, dy, dz, [strip[5 + a, unit] for a in range(3)])
            for k in range(5):
                target[k, unit] = new[k]
            return carry

        return step

    lax.fori_loop(0, 4, relax(strip, q_one), 0)
    lax.fori_loop(0, 4, relax(q_one, q_two), 0)

    def last(unit, carry):
        q, around, dx, dy, dz = gather_stencil(neighbours(q_two, unit))
        field = molecular_field(q, around, dx, dy, dz)
        velocity = [strip[5 + a, unit] for a in range(3)]
        new = updated(q, field, dx, dy, dz, velocity)
        force = force_of(field, dx, dy, dz)
        for k in range(5):
            done[19 + k, unit] = new[k]
        for i, value in collide(
            range(19), lambda i: strip[9 + i, unit], strip[8, unit], velocity, force
        ):
            _, b, c = (int(v) for v in lattice[i])
            done[i, unit] = roll_y(roll_z(value, c), b)
        return carry

    lax.fori_loop(0, 4, last, 0)

    edge_lane = jnp.logical_or(lane < 4, lane >= 124)

    def merged(field, shift, x, value):
        row = x + 4 - shift
        h, q = row // 8, row % 8
        pair = halves[field][h]
        return jnp.where(edge_lane, roll_y(pair, -(SLOTS * q + 8)), value)

    halves = {}
    for f in range(24):
        halves[f] = [
            jnp.where(slot < 8, done[f, 2 + h], roll_y(done[f, h], 4)) for h in range(2)
        ]
        shift = int(lattice[f][0]) if f < 19 else 0
        for x in range(8):
            if f < 19:
                out_pop[f, pl.ds(x, 8, stride=8), :] = merged(f, shift, x, moved_ref[f, x + 1])
            else:
                out_order[f - 19, pl.ds(x, 8, stride=8), :] = merged(
                    f, shift, x, order_ref[f - 19, x]
                )


def call(kernel, out_shapes, scratch, flops, *args):
    whole = pl.BlockSpec(memory_space=pltpu.VMEM)
    return pl.pallas_call(
        kernel,
        out_shape=[jax.ShapeDtypeStruct(s, f32) for s in out_shapes],
        in_specs=[whole] * len(args),
        out_specs=[whole] * len(out_shapes),
        scratch_shapes=[pltpu.VMEM(s, f32) for s in scratch],
        cost_estimate=pl.CostEstimate(
            flops=flops,
            bytes_accessed=4 * sum(math.prod(s) for s in out_shapes) + sum(4 * a.size for a in args),
            transcendentals=0,
        ),
        compiler_params=pltpu.CompilerParams(vmem_limit_bytes=12 * 1024 * 1024),
    )(*args)


def swap(size, first):
    return [
        (i, (i + 1) % size if i % 2 == first else (i - 1) % size) for i in range(size)
    ]


def body(rows, cols, populations, order_tensor):
    pops = populations.reshape(19, 64, 128)
    order = order_tensor.reshape(5, 64, 128)
    face = (FACE, 8, 128)
    base, first, second = call(
        moments_kernel, [(9, 8, 8, 128), face, face], [], 2_000_000, pops, order
    )
    recv_a = lax.ppermute(first, "row", swap(rows, 0))
    recv_b = lax.ppermute(second, "row", swap(rows, 1))
    own_edges = call(
        own_edges_kernel, [(FIELDS, 2, 8, 128)], [], 2_000_000, base, pops
    )[0]
    side = (6, 8, 128)
    edges, left, right = call(
        column_message_kernel,
        [(FIELDS, 2, 8, 128), side, side],
        [],
        1_000_000,
        own_edges,
        recv_a,
        recv_b,
    )
    col_a = lax.ppermute(left, "col", swap(cols, 0))
    col_b = lax.ppermute(right, "col", swap(cols, 1))
    moved, relaxed = call(
        main_kernel,
        [(19, 10, 8, 128), (5, 8, 8, 128)],
        [(5, 16, 8, 128)] * 3 + [(3, 14, 8, 128), (10, 8, 128)],
        20_000_000,
        base,
        recv_a,
        recv_b,
        pops,
    )
    new_pops, new_order = call(
        edge_kernel,
        [(19, 64, 128), (5, 64, 128)],
        [(FIELDS, 4, 8, 128), (5, 4, 8, 128), (5, 4, 8, 128), (24, 4, 8, 128)],
        8_000_000,
        edges,
        col_a,
        col_b,
        moved,
        relaxed,
    )
    return new_pops.reshape(populations.shape), new_order.reshape(order_tensor.shape)


def solution(mesh):
    spec = P(None, None, "row", "col")
    return jax.shard_map(
        functools.partial(body, mesh.shape["row"], mesh.shape["col"]),
        mesh=mesh,
        in_specs=(spec, spec),
        out_specs=(spec, spec),
        check_vma=False,
    )
```

```python
import functools
import math

import jax
import jax.numpy as jnp
import numpy as np
from jax import lax
from jax.experimental import pallas as pl
from jax.experimental.pallas import tpu as pltpu
from jax.sharding import PartitionSpec as P

lattice = np.array(
    [
        [0, 0, 0],
        [1, 0, 0],
        [-1, 0, 0],
        [0, 1, 0],
        [0, -1, 0],
        [0, 0, 1],
        [0, 0, -1],
        [1, 1, 0],
        [-1, -1, 0],
        [1, -1, 0],
        [-1, 1, 0],
        [1, 0, 1],
        [-1, 0, -1],
        [1, 0, -1],
        [-1, 0, 1],
        [0, 1, 1],
        [0, -1, -1],
        [0, 1, -1],
        [0, -1, 1],
    ]
)
tau_rate = 1.25
a_zero = 0.1
gamma_bulk = 3.0
stiffness = 0.4
pitch_wave = math.pi / 8.0
mobility_dt = 0.3

x_up = [i for i in range(19) if lattice[i][0] == 1]
x_down = [i + 1 for i in x_up]
y_up = [i for i in range(19) if lattice[i][1] == 1]
y_down = [i for i in range(19) if lattice[i][1] == -1]

VEL, DEN, POP, FACE = 20, 29, 30, 35
SLOTS = 16
near = sorted(y_up + y_down)
far = [i for i in range(19) if i not in near]
NEAR, FAR = 9 + len(near), len(far)
MOVE_UNROLL, RELAX_UNROLL, EDGE_UNROLL = 4, 7, 2
f32 = jnp.float32


def lanes():
    return lax.broadcasted_iota(jnp.int32, (8, 128), 1)


def slots():
    return lax.rem(lanes(), SLOTS)


def roll_y(value, shift):
    shift = shift % 128
    return value if shift == 0 else pltpu.roll(value, shift, 1)


def roll_z(value, shift):
    shift = shift % 8
    return value if shift == 0 else pltpu.roll(value, shift, 0)


def is_even(axis):
    return lax.rem(lax.axis_index(axis), 2) == 0


def stencil(center, x_ahead, x_behind):
    y_ahead, y_behind = roll_y(center, -1), roll_y(center, 1)
    z_ahead, z_behind = roll_z(center, -1), roll_z(center, 1)
    around = (x_ahead + x_behind) + (y_ahead + y_behind) + (z_ahead + z_behind)
    return around, (x_ahead - x_behind, y_ahead - y_behind, z_ahead - z_behind)


def molecular_field(q, around, dx, dy, dz):
    q0, q1, q2, q3, q4 = q
    qzz = -(q0 + q3)
    s0, s1, s2, s3, s4 = q0 * q0, q1 * q1, q2 * q2, q3 * q3, q4 * q4
    square = s0 + s3 + qzz * qzz + 2.0 * (s1 + s2 + s4)
    third = square * (1.0 / 3.0)
    bulk = a_zero * gamma_bulk
    product = (
        s0 + s1 + s2 - third,
        q2 * q4 - q1 * qzz,
        q1 * q4 - q2 * q3,
        s1 + s3 + s4 - third,
        q1 * q2 - q4 * q0,
    )
    chiral = (
        2.0 * (dy[2] - dz[1]),
        (dy[4] - dx[2]) + (dz[0] - dz[3]),
        (dx[1] - dz[4]) - (2.0 * dy[0] + dy[3]),
        2.0 * (dz[1] - dx[4]),
        (dz[2] - dy[1]) + (dx[0] + 2.0 * dx[3]),
    )
    linear = a_zero * (gamma_bulk / 3.0 - 1.0) - stiffness * (4.0 * pitch_wave**2 + 6.0)
    factor = linear - bulk * square
    return [
        bulk * product[k]
        + factor * q[k]
        + stiffness * around[k]
        - (stiffness * pitch_wave) * chiral[k]
        for k in range(5)
    ]


def gather_stencil(load):
    q, around, dx, dy, dz = [], [], [], [], []
    for k in range(5):
        center, ahead, behind = load(k)
        total, (a, b, c) = stencil(center, ahead, behind)
        q.append(center)
        around.append(total)
        dx.append(a)
        dy.append(b)
        dz.append(c)
    return q, around, dx, dy, dz


def updated(q, field, dx, dy, dz, velocity):
    hx, hy, hz = (0.5 * v for v in velocity)
    return [
        q[k] + mobility_dt * field[k] - (hx * dx[k] + hy * dy[k] + hz * dz[k]) for k in range(5)
    ]


def force_of(field, dx, dy, dz):
    first = field[0] + 0.5 * field[3]
    second = field[3] + 0.5 * field[0]
    return [
        first * d[0] + second * d[3] + field[1] * d[1] + field[2] * d[2] + field[4] * d[4]
        for d in (dx, dy, dz)
    ]


def collide(which, load, density, velocity, force):
    half = 0.5 / density
    u = [velocity[a] + force[a] * half for a in range(3)]
    speed = u[0] * u[0] + u[1] * u[1] + u[2] * u[2]
    along = u[0] * force[0] + u[1] * force[1] + u[2] * force[2]
    keep = 1.0 - 0.5 * tau_rate
    base = (tau_rate * density) * (1.0 - 1.5 * speed) - (3.0 * keep) * along
    odd = [(3.0 * tau_rate) * density * u[a] + (3.0 * keep) * force[a] for a in range(3)]
    even = [(4.5 * tau_rate) * density * u[a] + (9.0 * keep) * force[a] for a in range(3)]

    def dot(c, vector):
        total = None
        for a in range(3):
            if c[a]:
                term = vector[a]
                if total is None:
                    total = term if c[a] > 0 else -term
                else:
                    total = total + term if c[a] > 0 else total - term
        return total

    rest = 1.0 - tau_rate
    done = set()
    for i in which:
        if i in done:
            continue
        if i == 0:
            yield 0, rest * load(0) + (1.0 / 3.0) * base
            continue
        low = i if i % 2 else i - 1
        c = [int(v) for v in lattice[low]]
        weight = 1.0 / 18.0 if low < 7 else 1.0 / 36.0
        first = weight * (base + dot(c, u) * dot(c, even))
        second = weight * dot(c, odd)
        for j, sign in ((low, 1), (low + 1, -1)):
            if j in which:
                done.add(j)
                yield j, rest * load(j) + (first + second if sign > 0 else first - second)


def moments_kernel(
    pop_hbm, order_hbm, base_ref, first_ref, second_ref, pop_ref, order_ref, sems
):
    copies = [
        pltpu.make_async_copy(order_hbm, order_ref, sems.at[0]),
        pltpu.make_async_copy(pop_hbm, pop_ref, sems.at[1]),
    ]
    for copy in copies:
        copy.start()
    for copy in copies:
        copy.wait()

    def row(x, carry):
        p = [pop_ref[i, pl.ds(x, 8, stride=8), :] for i in range(19)]
        density = p[0]
        for i in range(1, 19):
            density = density + p[i]
        inverse = 1.0 / density
        for a in range(3):
            plus = [p[i] for i in range(19) if lattice[i][a] == 1]
            minus = [p[i] for i in range(19) if lattice[i][a] == -1]
            momentum = functools.reduce(lambda s, t: s + t, plus) - functools.reduce(
                lambda s, t: s + t, minus
            )
            base_ref[5 + a, x] = momentum * inverse
        base_ref[8, x] = density
        for k in range(5):
            base_ref[k, x] = order_ref[k, pl.ds(x, 8, stride=8), :]
        return carry

    lax.fori_loop(0, 8, row, 0)
    even = is_even("row")
    for out, high in ((first_ref, even), (second_ref, jnp.logical_not(even))):

        @pl.when(high)
        def _():
            for k in range(5):
                out[4 * k : 4 * k + 4] = base_ref[k, 4:8]
            for a in range(3):
                out[VEL + 3 * a : VEL + 3 * a + 3] = base_ref[5 + a, 5:8]
            out[DEN] = base_ref[8, 7]
            for j, i in enumerate(x_up):
                out[POP + j] = pop_ref[i, pl.ds(7, 8, stride=8), :]

        @pl.when(jnp.logical_not(high))
        def _():
            for k in range(5):
                out[4 * k : 4 * k + 4] = base_ref[k, 0:4]
            for a in range(3):
                out[VEL + 3 * a : VEL + 3 * a + 3] = base_ref[5 + a, 0:3]
            out[DEN] = base_ref[8, 0]
            for j, i in enumerate(x_down):
                out[POP + j] = pop_ref[i, pl.ds(0, 8, stride=8), :]


def placed(value, row, into):
    q = row % 8
    lane = lanes()
    mask = jnp.logical_and(lane >= SLOTS * q, lane < SLOTS * q + SLOTS)
    return jnp.where(mask, roll_y(value, 8 + SLOTS * q), into)


def own_edges_kernel(base_ref, pop_ref, edge_ref):
    def pack(load, fill, field):
        low = high = jnp.full((8, 128), fill, f32)
        for x in range(4):
            low = placed(load(x), x + 4, low)
            high = placed(load(x + 4), x + 8, high)
        edge_ref[field, 0] = low
        edge_ref[field, 1] = high

    for f in range(9):
        pack(lambda x, f=f: base_ref[f, x], 1.0 if f == 8 else 0.0, f)
    for n, i in enumerate(near):
        pack(lambda x, i=i: pop_ref[i, pl.ds(x, 8, stride=8), :], 0.0, 9 + n)


def column_message_kernel(own_ref, recv_a, recv_b, edge_ref, first_ref, second_ref):
    even = is_even("row")
    slot = slots()

    def halo(j):
        a, b = recv_a[j], recv_b[j]
        return jnp.where(even, b, a), jnp.where(even, a, b)

    def widen(field, rows):
        low, high = own_ref[field, 0], own_ref[field, 1]
        for j, row_low, row_high in rows:
            below, above = halo(j)
            low, high = placed(below, row_low, low), placed(above, row_high, high)
        edge_ref[field, 0] = low
        edge_ref[field, 1] = high

    for k in range(5):
        widen(k, [(4 * k + r, r, 12 + r) for r in range(4)])
    for a in range(3):
        widen(5 + a, [(VEL + 3 * a + r, 1 + r, 12 + r) for r in range(3)])
    widen(8, [(DEN, 3, 12)])
    for n, i in enumerate(near):
        low, high = own_ref[9 + n, 0], own_ref[9 + n, 1]
        if i in x_up:
            low = placed(halo(POP + x_up.index(i))[0], 3, low)
        if i in x_down:
            high = placed(halo(POP + x_down.index(i))[1], 12, high)
        edge_ref[9 + n, 0] = low
        edge_ref[9 + n, 1] = high

    col_even = is_even("col")
    for h in range(2):
        for g, parts in enumerate(((0, 1, 2, 3), (4, 5, 6, 7))):
            to_left = to_right = jnp.zeros((8, 128), f32)
            for u, f in enumerate(parts):
                value = edge_ref[f, h]
                mask = jnp.logical_and(slot >= 4 * u, slot < 4 * u + 4)
                to_left = jnp.where(mask, roll_y(value, 4 * u - 8), to_left)
                to_right = jnp.where(mask, roll_y(value, 4 * u - 4), to_right)
            first_ref[2 * g + h] = jnp.where(col_even, to_right, to_left)
            second_ref[2 * g + h] = jnp.where(col_even, to_left, to_right)
        to_left = to_right = jnp.zeros((8, 128), f32)
        for s in range(6):
            left_field = 8 if s == 0 else 9 + near.index(y_down[s - 1])
            right_field = 8 if s == 0 else 9 + near.index(y_up[s - 1])
            to_left = jnp.where(slot == s, roll_y(edge_ref[left_field, h], s - 8), to_left)
            to_right = jnp.where(slot == s, roll_y(edge_ref[right_field, h], s - 7), to_right)
        first_ref[4 + h] = jnp.where(col_even, to_right, to_left)
        second_ref[4 + h] = jnp.where(col_even, to_left, to_right)


def main_kernel(
    base_ref,
    recv_a,
    recv_b,
    pop_ref,
    moved_ref,
    order_ref,
    far_ref,
    q_zero,
    q_one,
    q_two,
    vel,
    den,
):
    even = is_even("row")

    def halo(j):
        a, b = recv_a[j], recv_b[j]
        return jnp.where(even, b, a), jnp.where(even, a, b)

    for k in range(5):
        q_zero[k, 4:12] = base_ref[k]
        for r in range(4):
            q_zero[k, r], q_zero[k, 12 + r] = halo(4 * k + r)
    for a in range(3):
        vel[a, 3:11] = base_ref[5 + a]
        for r in range(3):
            vel[a, r], vel[a, 11 + r] = halo(VEL + 3 * a + r)
    den[0], den[9] = halo(DEN)

    def relax(source, target):
        def row(r, carry):
            q, around, dx, dy, dz = gather_stencil(
                lambda k: (source[k, r], source[k, r + 1], source[k, r - 1])
            )
            field = molecular_field(q, around, dx, dy, dz)
            new = updated(q, field, dx, dy, dz, [vel[a, r - 1] for a in range(3)])
            for k in range(5):
                target[k, r] = new[k]
            return carry

        return row

    lax.fori_loop(1, 15, relax(q_zero, q_one), 0, unroll=RELAX_UNROLL)
    lax.fori_loop(2, 14, relax(q_one, q_two), 0, unroll=6)

    def last(x):
        q, around, dx, dy, dz = gather_stencil(
            lambda k: (q_two[k, x + 4], q_two[k, x + 5], q_two[k, x + 3])
        )
        field = molecular_field(q, around, dx, dy, dz)
        velocity = [vel[a, x + 3] for a in range(3)]
        return q, field, dx, dy, dz, velocity, force_of(field, dx, dy, dz)

    def stream(i, value, row):
        a, b, c = (int(v) for v in lattice[i])
        moved_ref[i, row + a] = roll_y(roll_z(value, c), b)

    def own_row(x, carry):
        q, field, dx, dy, dz, velocity, force = last(x)
        new = updated(q, field, dx, dy, dz, velocity)
        for k in range(5):
            order_ref[k, x] = new[k]
        for i, value in collide(
            range(19),
            lambda i: pop_ref[i, pl.ds(x, 8, stride=8), :],
            base_ref[8, x],
            velocity,
            force,
        ):
            stream(i, value, x + 1)
        return carry

    lax.fori_loop(0, 8, own_row, 0, unroll=MOVE_UNROLL)

    for n, i in enumerate(far):
        low = high = jnp.zeros((8, 128), f32)
        for x in range(4):
            low = placed(pop_ref[i, pl.ds(x, 8, stride=8), :], x + 4, low)
            high = placed(pop_ref[i, pl.ds(x + 4, 8, stride=8), :], x + 8, high)
        if i in x_up:
            low = placed(halo(POP + x_up.index(i))[0], 3, low)
        if i in x_down:
            high = placed(halo(POP + x_down.index(i))[1], 12, high)
        far_ref[n, 0] = low
        far_ref[n, 1] = high

    for x, which, side in ((-1, x_up, 0), (8, x_down, 1)):
        _, _, _, _, _, velocity, force = last(x)
        for i, value in collide(
            which,
            lambda i, which=which, side=side: halo(POP + which.index(i))[side],
            den[9 * side],
            velocity,
            force,
        ):
            stream(i, value, x + 1)


def edge_kernel(
    edge_ref,
    far_ref,
    recv_a,
    recv_b,
    moved_ref,
    order_ref,
    out_pop,
    out_order,
    strip,
    q_one,
    q_two,
    done,
):
    even = is_even("col")
    slot, lane = slots(), lanes()

    def columns(j):
        a, b = recv_a[j], recv_b[j]
        return jnp.where(even, b, a), jnp.where(even, a, b)

    for h in range(2):
        for f in range(8):
            from_left, from_right = columns(2 * (f // 4) + h)
            u = f % 4
            own = edge_ref[f, h]
            strip[f, h] = jnp.where(slot < 4, roll_y(from_left, -4 * u), roll_y(own, -4))
            strip[f, 2 + h] = jnp.where(slot < 8, own, roll_y(from_right, 8 - 4 * u))
        from_left, from_right = columns(4 + h)
        for f in range(8, 28):
            i = f - 9
            if f == 8:
                own = edge_ref[8, h]
            elif i in near:
                own = edge_ref[9 + near.index(i), h]
            else:
                own = far_ref[far.index(i), h]
            left, right = roll_y(own, -4), own
            if f == 8 or i in y_up:
                s = 0 if f == 8 else 1 + y_up.index(i)
                left = jnp.where(slot == 3, roll_y(from_left, 3 - s), left)
            if f == 8 or i in y_down:
                s = 0 if f == 8 else 1 + y_down.index(i)
                right = jnp.where(slot == 8, roll_y(from_right, 8 - s), right)
            strip[f, h] = left
            strip[f, 2 + h] = right

    def neighbours(source, unit):
        other = unit ^ 1

        def load(k):
            me, that = source[k, unit], source[k, other]
            ahead = jnp.where(lane >= 112, roll_y(that, -16), roll_y(me, -16))
            behind = jnp.where(lane < 16, roll_y(that, 16), roll_y(me, 16))
            return me, ahead, behind

        return load

    def relax(source, target):
        def step(unit, carry):
            q, around, dx, dy, dz = gather_stencil(neighbours(source, unit))
            field = molecular_field(q, around, dx, dy, dz)
            new = updated(q, field, dx, dy, dz, [strip[5 + a, unit] for a in range(3)])
            for k in range(5):
                target[k, unit] = new[k]
            return carry

        return step

    lax.fori_loop(0, 4, relax(strip, q_one), 0, unroll=EDGE_UNROLL)
    lax.fori_loop(0, 4, relax(q_one, q_two), 0, unroll=EDGE_UNROLL)

    def last(unit, carry):
        q, around, dx, dy, dz = gather_stencil(neighbours(q_two, unit))
        field = molecular_field(q, around, dx, dy, dz)
        velocity = [strip[5 + a, unit] for a in range(3)]
        new = updated(q, field, dx, dy, dz, velocity)
        force = force_of(field, dx, dy, dz)
        for k in range(5):
            done[19 + k, unit] = new[k]
        for i, value in collide(
            range(19), lambda i: strip[9 + i, unit], strip[8, unit], velocity, force
        ):
            _, b, c = (int(v) for v in lattice[i])
            done[i, unit] = roll_y(roll_z(value, c), b)
        return carry

    lax.fori_loop(0, 4, last, 0, unroll=EDGE_UNROLL)

    edge_lane = jnp.logical_or(lane < 4, lane >= 124)

    def merged(field, shift, x, value):
        row = x + 4 - shift
        h, q = row // 8, row % 8
        pair = halves[field][h]
        return jnp.where(edge_lane, roll_y(pair, -(SLOTS * q + 8)), value)

    halves = {}
    for f in range(24):
        halves[f] = [
            jnp.where(slot < 8, done[f, 2 + h], roll_y(done[f, h], 4)) for h in range(2)
        ]
        shift = int(lattice[f][0]) if f < 19 else 0
        for x in range(8):
            if f < 19:
                out_pop[f, pl.ds(x, 8, stride=8), :] = merged(f, shift, x, moved_ref[f, x + 1])
            else:
                out_order[f - 19, pl.ds(x, 8, stride=8), :] = merged(
                    f, shift, x, order_ref[f - 19, x]
                )


def call(kernel, out_shapes, scratch, flops, *args, from_hbm=False):
    whole = pl.BlockSpec(memory_space=pltpu.VMEM)
    source = pl.BlockSpec(memory_space=pltpu.HBM) if from_hbm else whole
    return pl.pallas_call(
        kernel,
        out_shape=[jax.ShapeDtypeStruct(s, f32) for s in out_shapes],
        in_specs=[source] * len(args),
        out_specs=[whole] * len(out_shapes),
        scratch_shapes=[pltpu.VMEM(s, f32) if isinstance(s, tuple) else s for s in scratch],
        cost_estimate=pl.CostEstimate(
            flops=flops,
            bytes_accessed=4 * sum(math.prod(s) for s in out_shapes) + sum(4 * a.size for a in args),
            transcendentals=0,
        ),
        compiler_params=pltpu.CompilerParams(vmem_limit_bytes=12 * 1024 * 1024),
    )(*args)


def swap(size, first):
    return [
        (i, (i + 1) % size if i % 2 == first else (i - 1) % size) for i in range(size)
    ]


def body(rows, cols, populations, order_tensor):
    face, side = (FACE, 8, 128), (6, 8, 128)
    base, first, second, pops = call(
        moments_kernel,
        [(9, 8, 8, 128), face, face, (19, 64, 128)],
        [(5, 64, 128), pltpu.SemaphoreType.DMA((2,))],
        2_000_000,
        pltpu.with_memory_space_constraint(populations.reshape(19, 64, 128), pltpu.HBM),
        pltpu.with_memory_space_constraint(order_tensor.reshape(5, 64, 128), pltpu.HBM),
        from_hbm=True,
    )
    recv_b = lax.ppermute(second, "row", swap(rows, 1))
    recv_a = lax.ppermute(first, "row", swap(rows, 0))
    own_edges = call(own_edges_kernel, [(NEAR, 2, 8, 128)], [], 2_000_000, base, pops)[0]
    edges, left, right = call(
        column_message_kernel,
        [(NEAR, 2, 8, 128), side, side],
        [],
        1_000_000,
        own_edges,
        recv_a,
        recv_b,
    )
    col_a = lax.ppermute(left, "col", swap(cols, 0))
    col_b = lax.ppermute(right, "col", swap(cols, 1))
    moved, relaxed, far_edges = call(
        main_kernel,
        [(19, 10, 8, 128), (5, 8, 8, 128), (FAR, 2, 8, 128)],
        [(5, 16, 8, 128)] * 3 + [(3, 14, 8, 128), (10, 8, 128)],
        20_000_000,
        base,
        recv_a,
        recv_b,
        pops,
    )
    new_pops, new_order = call(
        edge_kernel,
        [(19, 64, 128), (5, 64, 128)],
        [(28, 4, 8, 128), (5, 4, 8, 128), (5, 4, 8, 128), (24, 4, 8, 128)],
        8_000_000,
        edges,
        far_edges,
        col_a,
        col_b,
        moved,
        relaxed,
    )
    return new_pops.reshape(populations.shape), new_order.reshape(order_tensor.shape)


def solution(mesh):
    spec = P(None, None, "row", "col")
    return jax.shard_map(
        functools.partial(body, mesh.shape["row"], mesh.shape["col"]),
        mesh=mesh,
        in_specs=(spec, spec),
        out_specs=(spec, spec),
        check_vma=False,
    )
```

```python
import functools
import math

import jax
import jax.numpy as jnp
import numpy as np
from jax import lax
from jax.experimental import pallas as pl
from jax.experimental.pallas import tpu as pltpu
from jax.sharding import PartitionSpec as P

lattice = np.array(
    [
        [0, 0, 0],
        [1, 0, 0],
        [-1, 0, 0],
        [0, 1, 0],
        [0, -1, 0],
        [0, 0, 1],
        [0, 0, -1],
        [1, 1, 0],
        [-1, -1, 0],
        [1, -1, 0],
        [-1, 1, 0],
        [1, 0, 1],
        [-1, 0, -1],
        [1, 0, -1],
        [-1, 0, 1],
        [0, 1, 1],
        [0, -1, -1],
        [0, 1, -1],
        [0, -1, 1],
    ]
)
tau_rate = 1.25
a_zero = 0.1
gamma_bulk = 3.0
stiffness = 0.4
pitch_wave = math.pi / 8.0
mobility_dt = 0.3

x_up = [i for i in range(19) if lattice[i][0] == 1]
x_down = [i + 1 for i in x_up]
y_up = [i for i in range(19) if lattice[i][1] == 1]
y_down = [i for i in range(19) if lattice[i][1] == -1]

VEL, DEN, POP, FACE = 20, 29, 30, 35
SLOTS = 16
near = sorted(y_up + y_down)
far = [i for i in range(19) if i not in near]
NEAR, FAR = 9 + len(near), len(far)
CHUNKS = (0, 7, 13)
f32 = jnp.float32


def lanes():
    return lax.broadcasted_iota(jnp.int32, (8, 128), 1)


def slots():
    return lax.rem(lanes(), SLOTS)


def roll_y(value, shift):
    shift = shift % 128
    return value if shift == 0 else pltpu.roll(value, shift, 1)


def roll_z(value, shift):
    shift = shift % 8
    return value if shift == 0 else pltpu.roll(value, shift, 0)


def is_even(axis):
    return lax.rem(lax.axis_index(axis), 2) == 0


def stencil(center, x_ahead, x_behind):
    y_ahead, y_behind = roll_y(center, -1), roll_y(center, 1)
    z_ahead, z_behind = roll_z(center, -1), roll_z(center, 1)
    around = (x_ahead + x_behind) + (y_ahead + y_behind) + (z_ahead + z_behind)
    return around, (x_ahead - x_behind, y_ahead - y_behind, z_ahead - z_behind)


def molecular_field(q, around, dx, dy, dz):
    q0, q1, q2, q3, q4 = q
    qzz = -(q0 + q3)
    s0, s1, s2, s3, s4 = q0 * q0, q1 * q1, q2 * q2, q3 * q3, q4 * q4
    square = s0 + s3 + qzz * qzz + 2.0 * (s1 + s2 + s4)
    third = square * (1.0 / 3.0)
    bulk = a_zero * gamma_bulk
    product = (
        s0 + s1 + s2 - third,
        q2 * q4 - q1 * qzz,
        q1 * q4 - q2 * q3,
        s1 + s3 + s4 - third,
        q1 * q2 - q4 * q0,
    )
    chiral = (
        2.0 * (dy[2] - dz[1]),
        (dy[4] - dx[2]) + (dz[0] - dz[3]),
        (dx[1] - dz[4]) - (2.0 * dy[0] + dy[3]),
        2.0 * (dz[1] - dx[4]),
        (dz[2] - dy[1]) + (dx[0] + 2.0 * dx[3]),
    )
    linear = a_zero * (gamma_bulk / 3.0 - 1.0) - stiffness * (4.0 * pitch_wave**2 + 6.0)
    factor = linear - bulk * square
    return [
        bulk * product[k]
        + factor * q[k]
        + stiffness * around[k]
        - (stiffness * pitch_wave) * chiral[k]
        for k in range(5)
    ]


def gather_stencil(load):
    q, around, dx, dy, dz = [], [], [], [], []
    for k in range(5):
        center, ahead, behind = load(k)
        total, (a, b, c) = stencil(center, ahead, behind)
        q.append(center)
        around.append(total)
        dx.append(a)
        dy.append(b)
        dz.append(c)
    return q, around, dx, dy, dz


def updated(q, field, dx, dy, dz, velocity):
    hx, hy, hz = (0.5 * v for v in velocity)
    return [
        q[k] + mobility_dt * field[k] - (hx * dx[k] + hy * dy[k] + hz * dz[k]) for k in range(5)
    ]


def force_of(field, dx, dy, dz):
    first = field[0] + 0.5 * field[3]
    second = field[3] + 0.5 * field[0]
    return [
        first * d[0] + second * d[3] + field[1] * d[1] + field[2] * d[2] + field[4] * d[4]
        for d in (dx, dy, dz)
    ]


def collide(which, load, density, velocity, force):
    half = 0.5 / density
    u = [velocity[a] + force[a] * half for a in range(3)]
    speed = u[0] * u[0] + u[1] * u[1] + u[2] * u[2]
    along = u[0] * force[0] + u[1] * force[1] + u[2] * force[2]
    keep = 1.0 - 0.5 * tau_rate
    base = (tau_rate * density) * (1.0 - 1.5 * speed) - (3.0 * keep) * along
    odd = [(3.0 * tau_rate) * density * u[a] + (3.0 * keep) * force[a] for a in range(3)]
    even = [(4.5 * tau_rate) * density * u[a] + (9.0 * keep) * force[a] for a in range(3)]

    def dot(c, vector):
        total = None
        for a in range(3):
            if c[a]:
                term = vector[a]
                if total is None:
                    total = term if c[a] > 0 else -term
                else:
                    total = total + term if c[a] > 0 else total - term
        return total

    rest = 1.0 - tau_rate
    done = set()
    for i in which:
        if i in done:
            continue
        if i == 0:
            yield 0, rest * load(0) + (1.0 / 3.0) * base
            continue
        low = i if i % 2 else i - 1
        c = [int(v) for v in lattice[low]]
        weight = 1.0 / 18.0 if low < 7 else 1.0 / 36.0
        first = weight * (base + dot(c, u) * dot(c, even))
        second = weight * dot(c, odd)
        for j, sign in ((low, 1), (low + 1, -1)):
            if j in which:
                done.add(j)
                yield j, rest * load(j) + (first + second if sign > 0 else first - second)


def moments_kernel(
    pop_hbm, order_hbm, base_ref, first_ref, second_ref, pop_ref, order_ref, sems
):
    copies = [
        pltpu.make_async_copy(order_hbm, order_ref, sems.at[0]),
        pltpu.make_async_copy(pop_hbm, pop_ref, sems.at[1]),
    ]
    for copy in copies:
        copy.start()
    for copy in copies:
        copy.wait()

    def row(x, carry):
        p = [pop_ref[i, pl.ds(x, 8, stride=8), :] for i in range(19)]
        density = p[0]
        for i in range(1, 19):
            density = density + p[i]
        inverse = 1.0 / density
        for a in range(3):
            plus = [p[i] for i in range(19) if lattice[i][a] == 1]
            minus = [p[i] for i in range(19) if lattice[i][a] == -1]
            momentum = functools.reduce(lambda s, t: s + t, plus) - functools.reduce(
                lambda s, t: s + t, minus
            )
            base_ref[5 + a, x] = momentum * inverse
        base_ref[8, x] = density
        for k in range(5):
            base_ref[k, x] = order_ref[k, pl.ds(x, 8, stride=8), :]
        return carry

    lax.fori_loop(0, 8, row, 0)
    even = is_even("row")
    for out, high in ((first_ref, even), (second_ref, jnp.logical_not(even))):

        @pl.when(high)
        def _():
            for k in range(5):
                out[4 * k : 4 * k + 4] = base_ref[k, 4:8]
            for a in range(3):
                out[VEL + 3 * a : VEL + 3 * a + 3] = base_ref[5 + a, 5:8]
            out[DEN] = base_ref[8, 7]
            for j, i in enumerate(x_up):
                out[POP + j] = pop_ref[i, pl.ds(7, 8, stride=8), :]

        @pl.when(jnp.logical_not(high))
        def _():
            for k in range(5):
                out[4 * k : 4 * k + 4] = base_ref[k, 0:4]
            for a in range(3):
                out[VEL + 3 * a : VEL + 3 * a + 3] = base_ref[5 + a, 0:3]
            out[DEN] = base_ref[8, 0]
            for j, i in enumerate(x_down):
                out[POP + j] = pop_ref[i, pl.ds(0, 8, stride=8), :]


def placed(value, row, into):
    q = row % 8
    lane = lanes()
    mask = jnp.logical_and(lane >= SLOTS * q, lane < SLOTS * q + SLOTS)
    return jnp.where(mask, roll_y(value, 8 + SLOTS * q), into)


def own_edges_kernel(base_ref, pop_ref, edge_ref):
    def pack(load, fill, field):
        low = high = jnp.full((8, 128), fill, f32)
        for x in range(4):
            low = placed(load(x), x + 4, low)
            high = placed(load(x + 4), x + 8, high)
        edge_ref[field, 0] = low
        edge_ref[field, 1] = high

    for f in range(9):
        pack(lambda x, f=f: base_ref[f, x], 1.0 if f == 8 else 0.0, f)
    for n, i in enumerate(near):
        pack(lambda x, i=i: pop_ref[i, pl.ds(x, 8, stride=8), :], 0.0, 9 + n)


def column_message_kernel(
    own_ref, recv_b, recv_a, edge_ref, first_ref, second_ref, third_ref
):
    even = is_even("row")
    slot = slots()

    def halo(j):
        a, b = recv_a[j], recv_b[j]
        return jnp.where(even, b, a), jnp.where(even, a, b)

    def widen(field, rows):
        low, high = own_ref[field, 0], own_ref[field, 1]
        for j, row_low, row_high in rows:
            below, above = halo(j)
            low, high = placed(below, row_low, low), placed(above, row_high, high)
        edge_ref[field, 0] = low
        edge_ref[field, 1] = high

    for k in range(5):
        widen(k, [(4 * k + r, r, 12 + r) for r in range(4)])
    for a in range(3):
        widen(5 + a, [(VEL + 3 * a + r, 1 + r, 12 + r) for r in range(3)])
    widen(8, [(DEN, 3, 12)])
    for n, i in enumerate(near):
        low, high = own_ref[9 + n, 0], own_ref[9 + n, 1]
        if i in x_up:
            low = placed(halo(POP + x_up.index(i))[0], 3, low)
        if i in x_down:
            high = placed(halo(POP + x_down.index(i))[1], 12, high)
        edge_ref[9 + n, 0] = low
        edge_ref[9 + n, 1] = high

    col_even = is_even("col")
    for h in range(2):
        for g, parts in enumerate(((0, 1, 2, 3), (4, 5, 6, 7))):
            to_left = to_right = jnp.zeros((8, 128), f32)
            for u, f in enumerate(parts):
                value = edge_ref[f, h]
                mask = jnp.logical_and(slot >= 4 * u, slot < 4 * u + 4)
                to_left = jnp.where(mask, roll_y(value, 4 * u - 8), to_left)
                to_right = jnp.where(mask, roll_y(value, 4 * u - 4), to_right)
            first_ref[2 * g + h] = third_ref[2 * g + h] = jnp.where(col_even, to_right, to_left)
            second_ref[2 * g + h] = jnp.where(col_even, to_left, to_right)
        to_left = to_right = jnp.zeros((8, 128), f32)
        for s in range(6):
            left_field = 8 if s == 0 else 9 + near.index(y_down[s - 1])
            right_field = 8 if s == 0 else 9 + near.index(y_up[s - 1])
            to_left = jnp.where(slot == s, roll_y(edge_ref[left_field, h], s - 8), to_left)
            to_right = jnp.where(slot == s, roll_y(edge_ref[right_field, h], s - 7), to_right)
        first_ref[4 + h] = third_ref[4 + h] = jnp.where(col_even, to_right, to_left)
        second_ref[4 + h] = jnp.where(col_even, to_left, to_right)


def main_kernel(
    base_ref,
    recv_b,
    recv_a,
    pop_ref,
    moved_ref,
    order_ref,
    far_ref,
    q_zero,
    q_one,
    q_two,
    vel,
    den,
):
    even = is_even("row")

    def halo(j):
        a, b = recv_a[j], recv_b[j]
        return jnp.where(even, b, a), jnp.where(even, a, b)

    for k in range(5):
        q_zero[k, 4:12] = base_ref[k]
        for r in range(4):
            q_zero[k, r], q_zero[k, 12 + r] = halo(4 * k + r)
    for a in range(3):
        vel[a, 3:11] = base_ref[5 + a]
        for r in range(3):
            vel[a, r], vel[a, 11 + r] = halo(VEL + 3 * a + r)
    den[0], den[9] = halo(DEN)

    def relax(source, target):
        def row(r, carry):
            q, around, dx, dy, dz = gather_stencil(
                lambda k: (source[k, r], source[k, r + 1], source[k, r - 1])
            )
            field = molecular_field(q, around, dx, dy, dz)
            new = updated(q, field, dx, dy, dz, [vel[a, r - 1] for a in range(3)])
            for k in range(5):
                target[k, r] = new[k]
            return carry

        return row

    lax.fori_loop(1, 15, relax(q_zero, q_one), 0, unroll=7)
    lax.fori_loop(2, 14, relax(q_one, q_two), 0, unroll=6)

    def last(x):
        q, around, dx, dy, dz = gather_stencil(
            lambda k: (q_two[k, x + 4], q_two[k, x + 5], q_two[k, x + 3])
        )
        field = molecular_field(q, around, dx, dy, dz)
        velocity = [vel[a, x + 3] for a in range(3)]
        return q, field, dx, dy, dz, velocity, force_of(field, dx, dy, dz)

    def stream(i, value, row):
        a, b, c = (int(v) for v in lattice[i])
        moved_ref[i, row + a] = roll_y(roll_z(value, c), b)

    def own_row(x, carry):
        q, field, dx, dy, dz, velocity, force = last(x)
        new = updated(q, field, dx, dy, dz, velocity)
        for k in range(5):
            order_ref[k, x] = new[k]
        for i, value in collide(
            range(19),
            lambda i: pop_ref[i, pl.ds(x, 8, stride=8), :],
            base_ref[8, x],
            velocity,
            force,
        ):
            stream(i, value, x + 1)
        return carry

    lax.fori_loop(0, 8, own_row, 0, unroll=4)

    for n, i in enumerate(far):
        low = high = jnp.zeros((8, 128), f32)
        for x in range(4):
            low = placed(pop_ref[i, pl.ds(x, 8, stride=8), :], x + 4, low)
            high = placed(pop_ref[i, pl.ds(x + 4, 8, stride=8), :], x + 8, high)
        if i in x_up:
            low = placed(halo(POP + x_up.index(i))[0], 3, low)
        if i in x_down:
            high = placed(halo(POP + x_down.index(i))[1], 12, high)
        far_ref[n, 0] = low
        far_ref[n, 1] = high

    for x, which, side in ((-1, x_up, 0), (8, x_down, 1)):
        _, _, _, _, _, velocity, force = last(x)
        for i, value in collide(
            which,
            lambda i, which=which, side=side: halo(POP + which.index(i))[side],
            den[9 * side],
            velocity,
            force,
        ):
            stream(i, value, x + 1)


def edge_kernel(
    edge_ref,
    far_ref,
    recv_first,
    recv_b,
    recv_last,
    moved_ref,
    order_ref,
    new_pop,
    new_order,
    strip,
    q_one,
    q_two,
    pop_out,
    order_out,
    sems,
):
    even = is_even("col")
    late = lax.rem(lax.axis_index("col"), 4) >= 2
    slot, lane = slots(), lanes()

    def columns(j):
        a, b = jnp.where(late, recv_last[j], recv_first[j]), recv_b[j]
        return jnp.where(even, b, a), jnp.where(even, a, b)

    for h in range(2):
        for f in range(8):
            from_left, from_right = columns(2 * (f // 4) + h)
            u = f % 4
            own = edge_ref[f, h]
            strip[f, h] = jnp.where(slot < 8, roll_y(from_left, 4 - 4 * u), own)
            strip[f, 2 + h] = jnp.where(slot < 8, own, roll_y(from_right, 8 - 4 * u))
        from_left, from_right = columns(4 + h)
        for f in range(8, 28):
            i = f - 9
            if f == 8:
                own = edge_ref[8, h]
            elif i in near:
                own = edge_ref[9 + near.index(i), h]
            else:
                own = far_ref[far.index(i), h]
            left = right = own
            if f == 8 or i in y_up:
                s = 0 if f == 8 else 1 + y_up.index(i)
                left = jnp.where(slot == 7, roll_y(from_left, 7 - s), left)
            if f == 8 or i in y_down:
                s = 0 if f == 8 else 1 + y_down.index(i)
                right = jnp.where(slot == 8, roll_y(from_right, 8 - s), right)
            strip[f, h] = left
            strip[f, 2 + h] = right

    def neighbours(source, unit):
        other = unit ^ 1

        def load(k):
            me, that = source[k, unit], source[k, other]
            ahead = jnp.where(lane >= 112, roll_y(that, -16), roll_y(me, -16))
            behind = jnp.where(lane < 16, roll_y(that, 16), roll_y(me, 16))
            return me, ahead, behind

        return load

    def relax(source, target):
        def step(unit, carry):
            q, around, dx, dy, dz = gather_stencil(neighbours(source, unit))
            field = molecular_field(q, around, dx, dy, dz)
            return updated(q, field, dx, dy, dz, [strip[5 + a, unit] for a in range(3)])

        results = [step(unit, 0) for unit in range(4)]
        for unit in range(4):
            for k in range(5):
                target[k, unit] = results[unit][k]

    relax(strip, q_one)
    relax(q_one, q_two)

    edge_lane = jnp.logical_or(lane < 4, lane >= 124)

    def merge(field, units, load, shift_x, shift_y, target):
        halves = [jnp.where(slot < 8 - shift_y, units[2 + h], units[h]) for h in range(2)]
        rows = []
        for x in range(8):
            row = x + 4 - shift_x
            pair = roll_y(halves[row // 8], shift_y - (SLOTS * (row % 8) + 8))
            rows.append(jnp.where(edge_lane, pair, load(x)))
        for x in range(8):
            target[field, pl.ds(x, 8, stride=8), :] = rows[x]

    copies = [pltpu.make_async_copy(order_out, new_order, sems.at[0])]
    bounds = CHUNKS + (19,)
    for n, first in enumerate(CHUNKS):
        rows = pl.ds(first, bounds[n + 1] - first)
        copies.append(pltpu.make_async_copy(pop_out.at[rows], new_pop.at[rows], sems.at[n + 1]))

    relaxed, moving = [], []
    for unit in range(4):
        q, around, dx, dy, dz = gather_stencil(neighbours(q_two, unit))
        field = molecular_field(q, around, dx, dy, dz)
        velocity = [strip[5 + a, unit] for a in range(3)]
        relaxed.append(updated(q, field, dx, dy, dz, velocity))
        force = force_of(field, dx, dy, dz)
        moving.append(
            collide(
                range(19),
                lambda i, unit=unit: strip[9 + i, unit],
                strip[8, unit],
                velocity,
                force,
            )
        )
    for k in range(5):
        merge(k, [new[k] for new in relaxed], lambda x, k=k: order_ref[k, x], 0, 0, order_out)
    copies[0].start()
    for items in zip(*moving):
        i = items[0][0]
        a, b, c = (int(v) for v in lattice[i])
        units = [roll_z(value, c) for _, value in items]
        merge(i, units, lambda x, i=i: moved_ref[i, x + 1], a, b, pop_out)
        if i + 1 in bounds:
            copies[bounds.index(i + 1)].start()
    for copy in copies:
        copy.wait()


def call(kernel, out_shapes, scratch, flops, *args, from_hbm=False, to_hbm=False):
    whole, outside = (pl.BlockSpec(memory_space=m) for m in (pltpu.VMEM, pltpu.HBM))
    return pl.pallas_call(
        kernel,
        out_shape=[jax.ShapeDtypeStruct(s, f32) for s in out_shapes],
        in_specs=[outside if from_hbm else whole] * len(args),
        out_specs=[outside if to_hbm else whole] * len(out_shapes),
        scratch_shapes=[pltpu.VMEM(s, f32) if isinstance(s, tuple) else s for s in scratch],
        cost_estimate=pl.CostEstimate(
            flops=flops,
            bytes_accessed=4 * sum(math.prod(s) for s in out_shapes) + sum(4 * a.size for a in args),
            transcendentals=0,
        ),
        compiler_params=pltpu.CompilerParams(vmem_limit_bytes=12 * 1024 * 1024),
    )(*args)


def swap(size, first):
    return [
        (i, (i + 1) % size if i % 2 == first else (i - 1) % size) for i in range(size)
    ]


def part(size, late):
    return [(i, i ^ 1) for i in range(size) if (i % 4 >= 2) == late]


def body(rows, cols, populations, order_tensor):
    face, side = (FACE, 8, 128), (6, 8, 128)
    base, first, second, pops = call(
        moments_kernel,
        [(9, 8, 8, 128), face, face, (19, 64, 128)],
        [(5, 64, 128), pltpu.SemaphoreType.DMA((2,))],
        2_000_000,
        pltpu.with_memory_space_constraint(populations.reshape(19, 64, 128), pltpu.HBM),
        pltpu.with_memory_space_constraint(order_tensor.reshape(5, 64, 128), pltpu.HBM),
        from_hbm=True,
    )
    recv_b = lax.ppermute(second, "row", swap(rows, 1))
    recv_a = lax.ppermute(first, "row", swap(rows, 0))
    own_edges = call(own_edges_kernel, [(NEAR, 2, 8, 128)], [], 2_000_000, base, pops)[0]
    edges, first, second, third = call(
        column_message_kernel,
        [(NEAR, 2, 8, 128), side, side, side],
        [],
        1_000_000,
        own_edges,
        recv_b,
        recv_a,
    )
    col_first = lax.ppermute(first, "col", part(cols, False))
    col_b = lax.ppermute(second, "col", swap(cols, 1))
    col_last = lax.ppermute(third, "col", part(cols, True))
    moved, relaxed, far_edges = call(
        main_kernel,
        [(19, 10, 8, 128), (5, 8, 8, 128), (FAR, 2, 8, 128)],
        [(5, 16, 8, 128)] * 3 + [(3, 14, 8, 128), (10, 8, 128)],
        20_000_000,
        base,
        recv_b,
        recv_a,
        pops,
    )
    new_pops, new_order = call(
        edge_kernel,
        [(19, 64, 128), (5, 64, 128)],
        [
            (28, 4, 8, 128),
            (5, 4, 8, 128),
            (5, 4, 8, 128),
            (19, 64, 128),
            (5, 64, 128),
            pltpu.SemaphoreType.DMA((len(CHUNKS) + 1,)),
        ],
        8_000_000,
        edges,
        far_edges,
        col_first,
        col_b,
        col_last,
        moved,
        relaxed,
        to_hbm=True,
    )
    return new_pops.reshape(populations.shape), new_order.reshape(order_tensor.shape)


def solution(mesh):
    spec = P(None, None, "row", "col")
    return jax.shard_map(
        functools.partial(body, mesh.shape["row"], mesh.shape["col"]),
        mesh=mesh,
        in_specs=(spec, spec),
        out_specs=(spec, spec),
        check_vma=False,
    )
```

```python
import functools
import math

import jax
import jax.numpy as jnp
import numpy as np
from jax import lax
from jax.experimental import pallas as pl
from jax.experimental.pallas import tpu as pltpu
from jax.sharding import PartitionSpec as P

lattice = np.array(
    [
        [0, 0, 0],
        [1, 0, 0],
        [-1, 0, 0],
        [0, 1, 0],
        [0, -1, 0],
        [0, 0, 1],
        [0, 0, -1],
        [1, 1, 0],
        [-1, -1, 0],
        [1, -1, 0],
        [-1, 1, 0],
        [1, 0, 1],
        [-1, 0, -1],
        [1, 0, -1],
        [-1, 0, 1],
        [0, 1, 1],
        [0, -1, -1],
        [0, 1, -1],
        [0, -1, 1],
    ]
)
tau_rate = 1.25
a_zero = 0.1
gamma_bulk = 3.0
stiffness = 0.4
pitch_wave = math.pi / 8.0
mobility_dt = 0.3

x_up = [i for i in range(19) if lattice[i][0] == 1]
x_down = [i + 1 for i in x_up]
y_up = [i for i in range(19) if lattice[i][1] == 1]
y_down = [i for i in range(19) if lattice[i][1] == -1]

VEL, DEN, POP, FACE = 20, 29, 30, 35
SLOTS = 16
near = sorted(y_up + y_down)
far = [i for i in range(19) if i not in near]
NEAR, FAR = 9 + len(near), len(far)
CHUNKS = (0, 7, 13)
f32 = jnp.float32


def lanes():
    return lax.broadcasted_iota(jnp.int32, (8, 128), 1)


def slots():
    return lax.rem(lanes(), SLOTS)


def roll_y(value, shift):
    shift = shift % 128
    return value if shift == 0 else pltpu.roll(value, shift, 1)


def roll_z(value, shift):
    shift = shift % 8
    return value if shift == 0 else pltpu.roll(value, shift, 0)


def is_even(axis):
    return lax.rem(lax.axis_index(axis), 2) == 0


def stencil(center, x_ahead, x_behind):
    y_ahead, y_behind = roll_y(center, -1), roll_y(center, 1)
    z_ahead, z_behind = roll_z(center, -1), roll_z(center, 1)
    around = (x_ahead + x_behind) + (y_ahead + y_behind) + (z_ahead + z_behind)
    return around, (x_ahead - x_behind, y_ahead - y_behind, z_ahead - z_behind)


def molecular_field(q, around, dx, dy, dz):
    q0, q1, q2, q3, q4 = q
    qzz = -(q0 + q3)
    s0, s1, s2, s3, s4 = q0 * q0, q1 * q1, q2 * q2, q3 * q3, q4 * q4
    square = s0 + s3 + qzz * qzz + 2.0 * (s1 + s2 + s4)
    third = square * (1.0 / 3.0)
    bulk = a_zero * gamma_bulk
    product = (
        s0 + s1 + s2 - third,
        q2 * q4 - q1 * qzz,
        q1 * q4 - q2 * q3,
        s1 + s3 + s4 - third,
        q1 * q2 - q4 * q0,
    )
    chiral = (
        2.0 * (dy[2] - dz[1]),
        (dy[4] - dx[2]) + (dz[0] - dz[3]),
        (dx[1] - dz[4]) - (2.0 * dy[0] + dy[3]),
        2.0 * (dz[1] - dx[4]),
        (dz[2] - dy[1]) + (dx[0] + 2.0 * dx[3]),
    )
    linear = a_zero * (gamma_bulk / 3.0 - 1.0) - stiffness * (4.0 * pitch_wave**2 + 6.0)
    factor = linear - bulk * square
    return [
        bulk * product[k]
        + factor * q[k]
        + stiffness * around[k]
        - (stiffness * pitch_wave) * chiral[k]
        for k in range(5)
    ]


def gather_stencil(load):
    q, around, dx, dy, dz = [], [], [], [], []
    for k in range(5):
        center, ahead, behind = load(k)
        total, (a, b, c) = stencil(center, ahead, behind)
        q.append(center)
        around.append(total)
        dx.append(a)
        dy.append(b)
        dz.append(c)
    return q, around, dx, dy, dz


def updated(q, field, dx, dy, dz, velocity):
    hx, hy, hz = (0.5 * v for v in velocity)
    return [
        q[k] + mobility_dt * field[k] - (hx * dx[k] + hy * dy[k] + hz * dz[k]) for k in range(5)
    ]


def force_of(field, dx, dy, dz):
    first = field[0] + 0.5 * field[3]
    second = field[3] + 0.5 * field[0]
    return [
        first * d[0] + second * d[3] + field[1] * d[1] + field[2] * d[2] + field[4] * d[4]
        for d in (dx, dy, dz)
    ]


def collide(which, load, density, velocity, force):
    half = 0.5 / density
    u = [velocity[a] + force[a] * half for a in range(3)]
    speed = u[0] * u[0] + u[1] * u[1] + u[2] * u[2]
    along = u[0] * force[0] + u[1] * force[1] + u[2] * force[2]
    keep = 1.0 - 0.5 * tau_rate
    base = (tau_rate * density) * (1.0 - 1.5 * speed) - (3.0 * keep) * along
    odd = [(3.0 * tau_rate) * density * u[a] + (3.0 * keep) * force[a] for a in range(3)]
    even = [(4.5 * tau_rate) * density * u[a] + (9.0 * keep) * force[a] for a in range(3)]

    def dot(c, vector):
        total = None
        for a in range(3):
            if c[a]:
                term = vector[a]
                if total is None:
                    total = term if c[a] > 0 else -term
                else:
                    total = total + term if c[a] > 0 else total - term
        return total

    rest = 1.0 - tau_rate
    done = set()
    for i in which:
        if i in done:
            continue
        if i == 0:
            yield 0, rest * load(0) + (1.0 / 3.0) * base
            continue
        low = i if i % 2 else i - 1
        c = [int(v) for v in lattice[low]]
        weight = 1.0 / 18.0 if low < 7 else 1.0 / 36.0
        first = weight * (base + dot(c, u) * dot(c, even))
        second = weight * dot(c, odd)
        for j, sign in ((low, 1), (low + 1, -1)):
            if j in which:
                done.add(j)
                yield j, rest * load(j) + (first + second if sign > 0 else first - second)


def moments_kernel(
    pop_hbm, order_hbm, base_ref, first_ref, second_ref, pop_ref, order_ref, sems
):
    copies = [
        pltpu.make_async_copy(order_hbm, order_ref, sems.at[0]),
        pltpu.make_async_copy(pop_hbm, pop_ref, sems.at[1]),
    ]
    for copy in copies:
        copy.start()
    for copy in copies:
        copy.wait()

    def row(x, carry):
        p = [pop_ref[i, pl.ds(x, 8, stride=8), :] for i in range(19)]
        density = p[0]
        for i in range(1, 19):
            density = density + p[i]
        inverse = 1.0 / density
        for a in range(3):
            plus = [p[i] for i in range(19) if lattice[i][a] == 1]
            minus = [p[i] for i in range(19) if lattice[i][a] == -1]
            momentum = functools.reduce(lambda s, t: s + t, plus) - functools.reduce(
                lambda s, t: s + t, minus
            )
            base_ref[5 + a, x] = momentum * inverse
        base_ref[8, x] = density
        for k in range(5):
            base_ref[k, x] = order_ref[k, pl.ds(x, 8, stride=8), :]
        return carry

    lax.fori_loop(0, 8, row, 0)
    even = is_even("row")
    for out, high in ((first_ref, even), (second_ref, jnp.logical_not(even))):

        @pl.when(high)
        def _():
            for k in range(5):
                out[4 * k : 4 * k + 4] = base_ref[k, 4:8]
            for a in range(3):
                out[VEL + 3 * a : VEL + 3 * a + 3] = base_ref[5 + a, 5:8]
            out[DEN] = base_ref[8, 7]
            for j, i in enumerate(x_up):
                out[POP + j] = pop_ref[i, pl.ds(7, 8, stride=8), :]

        @pl.when(jnp.logical_not(high))
        def _():
            for k in range(5):
                out[4 * k : 4 * k + 4] = base_ref[k, 0:4]
            for a in range(3):
                out[VEL + 3 * a : VEL + 3 * a + 3] = base_ref[5 + a, 0:3]
            out[DEN] = base_ref[8, 0]
            for j, i in enumerate(x_down):
                out[POP + j] = pop_ref[i, pl.ds(0, 8, stride=8), :]


def placed(value, row, into):
    q = row % 8
    lane = lanes()
    mask = jnp.logical_and(lane >= SLOTS * q, lane < SLOTS * q + SLOTS)
    return jnp.where(mask, roll_y(value, 8 + SLOTS * q), into)


def own_edges_kernel(base_ref, pop_ref, edge_ref):
    def pack(load, fill, field):
        low = high = jnp.full((8, 128), fill, f32)
        for x in range(4):
            low = placed(load(x), x + 4, low)
            high = placed(load(x + 4), x + 8, high)
        edge_ref[field, 0] = low
        edge_ref[field, 1] = high

    for f in range(9):
        pack(lambda x, f=f: base_ref[f, x], 1.0 if f == 8 else 0.0, f)
    for n, i in enumerate(near):
        pack(lambda x, i=i: pop_ref[i, pl.ds(x, 8, stride=8), :], 0.0, 9 + n)


def column_message_kernel(
    own_ref, recv_b, recv_a, edge_ref, first_ref, second_ref, third_ref, fourth_ref
):
    even = is_even("row")
    slot = slots()

    def halo(j):
        a, b = recv_a[j], recv_b[j]
        return jnp.where(even, b, a), jnp.where(even, a, b)

    def widen(field, rows):
        low, high = own_ref[field, 0], own_ref[field, 1]
        for j, row_low, row_high in rows:
            below, above = halo(j)
            low, high = placed(below, row_low, low), placed(above, row_high, high)
        edge_ref[field, 0] = low
        edge_ref[field, 1] = high

    for k in range(5):
        widen(k, [(4 * k + r, r, 12 + r) for r in range(4)])
    for a in range(3):
        widen(5 + a, [(VEL + 3 * a + r, 1 + r, 12 + r) for r in range(3)])
    widen(8, [(DEN, 3, 12)])
    for n, i in enumerate(near):
        low, high = own_ref[9 + n, 0], own_ref[9 + n, 1]
        if i in x_up:
            low = placed(halo(POP + x_up.index(i))[0], 3, low)
        if i in x_down:
            high = placed(halo(POP + x_down.index(i))[1], 12, high)
        edge_ref[9 + n, 0] = low
        edge_ref[9 + n, 1] = high

    col_even = is_even("col")
    for h in range(2):
        for g, parts in enumerate(((0, 1, 2, 3), (4, 5, 6, 7))):
            to_left = to_right = jnp.zeros((8, 128), f32)
            for u, f in enumerate(parts):
                value = edge_ref[f, h]
                mask = jnp.logical_and(slot >= 4 * u, slot < 4 * u + 4)
                to_left = jnp.where(mask, roll_y(value, 4 * u - 8), to_left)
                to_right = jnp.where(mask, roll_y(value, 4 * u - 4), to_right)
            first_ref[2 * g + h] = third_ref[2 * g + h] = jnp.where(col_even, to_right, to_left)
            second_ref[2 * g + h] = fourth_ref[2 * g + h] = jnp.where(col_even, to_left, to_right)
        to_left = to_right = jnp.zeros((8, 128), f32)
        for s in range(6):
            left_field = 8 if s == 0 else 9 + near.index(y_down[s - 1])
            right_field = 8 if s == 0 else 9 + near.index(y_up[s - 1])
            to_left = jnp.where(slot == s, roll_y(edge_ref[left_field, h], s - 8), to_left)
            to_right = jnp.where(slot == s, roll_y(edge_ref[right_field, h], s - 7), to_right)
        first_ref[4 + h] = third_ref[4 + h] = jnp.where(col_even, to_right, to_left)
        second_ref[4 + h] = fourth_ref[4 + h] = jnp.where(col_even, to_left, to_right)


def is_late():
    return lax.rem(lax.axis_index("col"), 4) >= 2


def early_main_kernel(base_ref, recv_b, recv_a, pop_ref, third_ref, fourth_ref, *rest):
    outputs, scratch = rest[:3], rest[5:]
    rest[3][...] = third_ref[...]
    rest[4][...] = fourth_ref[...]

    @pl.when(jnp.logical_not(is_late()))
    def _():
        main_block(base_ref, recv_b, recv_a, pop_ref, *outputs, *scratch)


def late_main_kernel(base_ref, recv_b, recv_a, pop_ref, *rest):
    done, outputs, scratch = rest[:3], rest[3:6], rest[6:]

    @pl.when(is_late())
    def _():
        main_block(base_ref, recv_b, recv_a, pop_ref, *outputs, *scratch)

    @pl.when(jnp.logical_not(is_late()))
    def _():
        for source, target in zip(done, outputs):
            target[...] = source[...]


def main_block(
    base_ref,
    recv_b,
    recv_a,
    pop_ref,
    moved_ref,
    order_ref,
    far_ref,
    q_zero,
    q_one,
    q_two,
    vel,
    den,
):
    even = is_even("row")

    def halo(j):
        a, b = recv_a[j], recv_b[j]
        return jnp.where(even, b, a), jnp.where(even, a, b)

    for k in range(5):
        q_zero[k, 4:12] = base_ref[k]
        for r in range(4):
            q_zero[k, r], q_zero[k, 12 + r] = halo(4 * k + r)
    for a in range(3):
        vel[a, 3:11] = base_ref[5 + a]
        for r in range(3):
            vel[a, r], vel[a, 11 + r] = halo(VEL + 3 * a + r)
    den[0], den[9] = halo(DEN)

    def relax(source, target):
        def row(r, carry):
            q, around, dx, dy, dz = gather_stencil(
                lambda k: (source[k, r], source[k, r + 1], source[k, r - 1])
            )
            field = molecular_field(q, around, dx, dy, dz)
            new = updated(q, field, dx, dy, dz, [vel[a, r - 1] for a in range(3)])
            for k in range(5):
                target[k, r] = new[k]
            return carry

        return row

    lax.fori_loop(1, 15, relax(q_zero, q_one), 0, unroll=7)
    lax.fori_loop(2, 14, relax(q_one, q_two), 0, unroll=6)

    def last(x):
        q, around, dx, dy, dz = gather_stencil(
            lambda k: (q_two[k, x + 4], q_two[k, x + 5], q_two[k, x + 3])
        )
        field = molecular_field(q, around, dx, dy, dz)
        velocity = [vel[a, x + 3] for a in range(3)]
        return q, field, dx, dy, dz, velocity, force_of(field, dx, dy, dz)

    def stream(i, value, row):
        a, b, c = (int(v) for v in lattice[i])
        moved_ref[i, row + a] = roll_y(roll_z(value, c), b)

    def own_row(x, carry):
        q, field, dx, dy, dz, velocity, force = last(x)
        new = updated(q, field, dx, dy, dz, velocity)
        for k in range(5):
            order_ref[k, x] = new[k]
        for i, value in collide(
            range(19),
            lambda i: pop_ref[i, pl.ds(x, 8, stride=8), :],
            base_ref[8, x],
            velocity,
            force,
        ):
            stream(i, value, x + 1)
        return carry

    lax.fori_loop(0, 8, own_row, 0, unroll=4)

    for n, i in enumerate(far):
        low = high = jnp.zeros((8, 128), f32)
        for x in range(4):
            low = placed(pop_ref[i, pl.ds(x, 8, stride=8), :], x + 4, low)
            high = placed(pop_ref[i, pl.ds(x + 4, 8, stride=8), :], x + 8, high)
        if i in x_up:
            low = placed(halo(POP + x_up.index(i))[0], 3, low)
        if i in x_down:
            high = placed(halo(POP + x_down.index(i))[1], 12, high)
        far_ref[n, 0] = low
        far_ref[n, 1] = high

    for x, which, side in ((-1, x_up, 0), (8, x_down, 1)):
        _, _, _, _, _, velocity, force = last(x)
        for i, value in collide(
            which,
            lambda i, which=which, side=side: halo(POP + which.index(i))[side],
            den[9 * side],
            velocity,
            force,
        ):
            stream(i, value, x + 1)


def edge_kernel(
    edge_ref,
    far_ref,
    recv_down,
    recv_first,
    recv_up,
    recv_last,
    moved_ref,
    order_ref,
    new_pop,
    new_order,
    strip,
    q_one,
    q_two,
    pop_out,
    order_out,
    sems,
):
    even = is_even("col")
    late = is_late()
    slot, lane = slots(), lanes()

    def columns(j):
        a = jnp.where(late, recv_last[j], recv_first[j])
        b = jnp.where(late, recv_up[j], recv_down[j])
        return jnp.where(even, b, a), jnp.where(even, a, b)

    for h in range(2):
        for f in range(8):
            from_left, from_right = columns(2 * (f // 4) + h)
            u = f % 4
            own = edge_ref[f, h]
            strip[f, h] = jnp.where(slot < 8, roll_y(from_left, 4 - 4 * u), own)
            strip[f, 2 + h] = jnp.where(slot < 8, own, roll_y(from_right, 8 - 4 * u))
        from_left, from_right = columns(4 + h)
        for f in range(8, 28):
            i = f - 9
            if f == 8:
                own = edge_ref[8, h]
            elif i in near:
                own = edge_ref[9 + near.index(i), h]
            else:
                own = far_ref[far.index(i), h]
            left = right = own
            if f == 8 or i in y_up:
                s = 0 if f == 8 else 1 + y_up.index(i)
                left = jnp.where(slot == 7, roll_y(from_left, 7 - s), left)
            if f == 8 or i in y_down:
                s = 0 if f == 8 else 1 + y_down.index(i)
                right = jnp.where(slot == 8, roll_y(from_right, 8 - s), right)
            strip[f, h] = left
            strip[f, 2 + h] = right

    def neighbours(source, unit):
        other = unit ^ 1

        def load(k):
            me, that = source[k, unit], source[k, other]
            ahead = jnp.where(lane >= 112, roll_y(that, -16), roll_y(me, -16))
            behind = jnp.where(lane < 16, roll_y(that, 16), roll_y(me, 16))
            return me, ahead, behind

        return load

    def relax(source, target):
        def step(unit, carry):
            q, around, dx, dy, dz = gather_stencil(neighbours(source, unit))
            field = molecular_field(q, around, dx, dy, dz)
            return updated(q, field, dx, dy, dz, [strip[5 + a, unit] for a in range(3)])

        results = [step(unit, 0) for unit in range(4)]
        for unit in range(4):
            for k in range(5):
                target[k, unit] = results[unit][k]

    relax(strip, q_one)
    relax(q_one, q_two)

    edge_lane = jnp.logical_or(lane < 4, lane >= 124)

    def merge(field, units, load, shift_x, shift_y, target):
        halves = [jnp.where(slot < 8 - shift_y, units[2 + h], units[h]) for h in range(2)]
        rows = []
        for x in range(8):
            row = x + 4 - shift_x
            pair = roll_y(halves[row // 8], shift_y - (SLOTS * (row % 8) + 8))
            rows.append(jnp.where(edge_lane, pair, load(x)))
        for x in range(8):
            target[field, pl.ds(x, 8, stride=8), :] = rows[x]

    copies = [pltpu.make_async_copy(order_out, new_order, sems.at[0])]
    bounds = CHUNKS + (19,)
    for n, first in enumerate(CHUNKS):
        rows = pl.ds(first, bounds[n + 1] - first)
        copies.append(pltpu.make_async_copy(pop_out.at[rows], new_pop.at[rows], sems.at[n + 1]))

    relaxed, moving = [], []
    for unit in range(4):
        q, around, dx, dy, dz = gather_stencil(neighbours(q_two, unit))
        field = molecular_field(q, around, dx, dy, dz)
        velocity = [strip[5 + a, unit] for a in range(3)]
        relaxed.append(updated(q, field, dx, dy, dz, velocity))
        force = force_of(field, dx, dy, dz)
        moving.append(
            collide(
                range(19),
                lambda i, unit=unit: strip[9 + i, unit],
                strip[8, unit],
                velocity,
                force,
            )
        )
    for k in range(5):
        merge(k, [new[k] for new in relaxed], lambda x, k=k: order_ref[k, x], 0, 0, order_out)
    copies[0].start()
    for items in zip(*moving):
        i = items[0][0]
        a, b, c = (int(v) for v in lattice[i])
        units = [roll_z(value, c) for _, value in items]
        merge(i, units, lambda x, i=i: moved_ref[i, x + 1], a, b, pop_out)
        if i + 1 in bounds:
            copies[bounds.index(i + 1)].start()
    for copy in copies:
        copy.wait()


def call(kernel, out_shapes, scratch, flops, *args, from_hbm=False, to_hbm=False):
    whole, outside = (pl.BlockSpec(memory_space=m) for m in (pltpu.VMEM, pltpu.HBM))
    return pl.pallas_call(
        kernel,
        out_shape=[jax.ShapeDtypeStruct(s, f32) for s in out_shapes],
        in_specs=[outside if from_hbm else whole] * len(args),
        out_specs=[outside if to_hbm else whole] * len(out_shapes),
        scratch_shapes=[pltpu.VMEM(s, f32) if isinstance(s, tuple) else s for s in scratch],
        cost_estimate=pl.CostEstimate(
            flops=flops,
            bytes_accessed=4 * sum(math.prod(s) for s in out_shapes) + sum(4 * a.size for a in args),
            transcendentals=0,
        ),
        compiler_params=pltpu.CompilerParams(vmem_limit_bytes=12 * 1024 * 1024),
    )(*args)


def swap(size, first):
    return [
        (i, (i + 1) % size if i % 2 == first else (i - 1) % size) for i in range(size)
    ]


def crossing(size):
    down = [(i, (i + 1) % size if i % 2 else i - 1) for i in range(size) if i % 4 >= 2]
    return down, [(target, source) for source, target in down]


def part(size, late):
    return [(i, i ^ 1) for i in range(size) if (i % 4 >= 2) == late]


def body(rows, cols, populations, order_tensor):
    face, side = (FACE, 8, 128), (6, 8, 128)
    base, first, second, pops = call(
        moments_kernel,
        [(9, 8, 8, 128), face, face, (19, 64, 128)],
        [(5, 64, 128), pltpu.SemaphoreType.DMA((2,))],
        2_000_000,
        pltpu.with_memory_space_constraint(populations.reshape(19, 64, 128), pltpu.HBM),
        pltpu.with_memory_space_constraint(order_tensor.reshape(5, 64, 128), pltpu.HBM),
        from_hbm=True,
    )
    recv_b = lax.ppermute(second, "row", swap(rows, 1))
    recv_a = lax.ppermute(first, "row", swap(rows, 0))
    own_edges = call(own_edges_kernel, [(NEAR, 2, 8, 128)], [], 2_000_000, base, pops)[0]
    edges, first, second, third, fourth = call(
        column_message_kernel,
        [(NEAR, 2, 8, 128), side, side, side, side],
        [],
        1_000_000,
        own_edges,
        recv_b,
        recv_a,
    )
    down, up = crossing(cols)
    recv_down = lax.ppermute(second, "col", down)
    recv_first = lax.ppermute(first, "col", part(cols, False))
    blocks = [(19, 10, 8, 128), (5, 8, 8, 128), (FAR, 2, 8, 128)]
    scratch = [(5, 16, 8, 128)] * 3 + [(3, 14, 8, 128), (10, 8, 128)]
    *half_done, third_again, fourth_again = call(
        early_main_kernel,
        [*blocks, side, side],
        scratch,
        20_000_000,
        base,
        recv_b,
        recv_a,
        pops,
        third,
        fourth,
    )
    recv_up = lax.ppermute(fourth_again, "col", up)
    recv_last = lax.ppermute(third_again, "col", part(cols, True))
    moved, relaxed, far_edges = call(
        late_main_kernel,
        blocks,
        scratch,
        20_000_000,
        base,
        recv_b,
        recv_a,
        pops,
        *half_done,
    )
    new_pops, new_order = call(
        edge_kernel,
        [(19, 64, 128), (5, 64, 128)],
        [
            (28, 4, 8, 128),
            (5, 4, 8, 128),
            (5, 4, 8, 128),
            (19, 64, 128),
            (5, 64, 128),
            pltpu.SemaphoreType.DMA((len(CHUNKS) + 1,)),
        ],
        8_000_000,
        edges,
        far_edges,
        recv_down,
        recv_first,
        recv_up,
        recv_last,
        moved,
        relaxed,
        to_hbm=True,
    )
    return new_pops.reshape(populations.shape), new_order.reshape(order_tensor.shape)


def solution(mesh):
    spec = P(None, None, "row", "col")
    return jax.shard_map(
        functools.partial(body, mesh.shape["row"], mesh.shape["col"]),
        mesh=mesh,
        in_specs=(spec, spec),
        out_specs=(spec, spec),
        check_vma=False,
    )
```

```python
import functools
import math

import jax
import jax.numpy as jnp
import numpy as np
from jax import lax
from jax.experimental import pallas as pl
from jax.experimental.pallas import tpu as pltpu
from jax.sharding import PartitionSpec as P

lattice = np.array(
    [
        [0, 0, 0],
        [1, 0, 0],
        [-1, 0, 0],
        [0, 1, 0],
        [0, -1, 0],
        [0, 0, 1],
        [0, 0, -1],
        [1, 1, 0],
        [-1, -1, 0],
        [1, -1, 0],
        [-1, 1, 0],
        [1, 0, 1],
        [-1, 0, -1],
        [1, 0, -1],
        [-1, 0, 1],
        [0, 1, 1],
        [0, -1, -1],
        [0, 1, -1],
        [0, -1, 1],
    ]
)
tau_rate = 1.25
a_zero = 0.1
gamma_bulk = 3.0
stiffness = 0.4
pitch_wave = math.pi / 8.0
mobility_dt = 0.3

x_up = [i for i in range(19) if lattice[i][0] == 1]
x_down = [i + 1 for i in x_up]
y_up = [i for i in range(19) if lattice[i][1] == 1]
y_down = [i for i in range(19) if lattice[i][1] == -1]

VEL, DEN, POP, FACE, PADDED = 20, 29, 30, 35, 42
CROSS_COST = 4_000_000_000
STRIPS = 6
SLOTS = 16
near = sorted(y_up + y_down)
far = [i for i in range(19) if i not in near]
NEAR, FAR = 9 + len(near), len(far)
CHUNKS = (0, 7, 13)
f32 = jnp.float32


def lanes():
    return lax.broadcasted_iota(jnp.int32, (8, 128), 1)


def slots():
    return lax.rem(lanes(), SLOTS)


def roll_y(value, shift):
    shift = shift % 128
    return value if shift == 0 else pltpu.roll(value, shift, 1)


def roll_z(value, shift):
    shift = shift % 8
    return value if shift == 0 else pltpu.roll(value, shift, 0)


def is_even(axis):
    return lax.rem(lax.axis_index(axis), 2) == 0


def stencil(center, x_ahead, x_behind):
    y_ahead, y_behind = roll_y(center, -1), roll_y(center, 1)
    z_ahead, z_behind = roll_z(center, -1), roll_z(center, 1)
    around = (x_ahead + x_behind) + (y_ahead + y_behind) + (z_ahead + z_behind)
    return around, (x_ahead - x_behind, y_ahead - y_behind, z_ahead - z_behind)


def molecular_field(q, around, dx, dy, dz):
    q0, q1, q2, q3, q4 = q
    qzz = -(q0 + q3)
    s0, s1, s2, s3, s4 = q0 * q0, q1 * q1, q2 * q2, q3 * q3, q4 * q4
    square = s0 + s3 + qzz * qzz + 2.0 * (s1 + s2 + s4)
    third = square * (1.0 / 3.0)
    bulk = a_zero * gamma_bulk
    product = (
        s0 + s1 + s2 - third,
        q2 * q4 - q1 * qzz,
        q1 * q4 - q2 * q3,
        s1 + s3 + s4 - third,
        q1 * q2 - q4 * q0,
    )
    chiral = (
        2.0 * (dy[2] - dz[1]),
        (dy[4] - dx[2]) + (dz[0] - dz[3]),
        (dx[1] - dz[4]) - (2.0 * dy[0] + dy[3]),
        2.0 * (dz[1] - dx[4]),
        (dz[2] - dy[1]) + (dx[0] + 2.0 * dx[3]),
    )
    linear = a_zero * (gamma_bulk / 3.0 - 1.0) - stiffness * (4.0 * pitch_wave**2 + 6.0)
    factor = linear - bulk * square
    return [
        bulk * product[k]
        + factor * q[k]
        + stiffness * around[k]
        - (stiffness * pitch_wave) * chiral[k]
        for k in range(5)
    ]


def gather_stencil(load):
    q, around, dx, dy, dz = [], [], [], [], []
    for k in range(5):
        center, ahead, behind = load(k)
        total, (a, b, c) = stencil(center, ahead, behind)
        q.append(center)
        around.append(total)
        dx.append(a)
        dy.append(b)
        dz.append(c)
    return q, around, dx, dy, dz


def updated(q, field, dx, dy, dz, velocity):
    hx, hy, hz = (0.5 * v for v in velocity)
    return [
        q[k] + mobility_dt * field[k] - (hx * dx[k] + hy * dy[k] + hz * dz[k]) for k in range(5)
    ]


def force_of(field, dx, dy, dz):
    first = field[0] + 0.5 * field[3]
    second = field[3] + 0.5 * field[0]
    return [
        first * d[0] + second * d[3] + field[1] * d[1] + field[2] * d[2] + field[4] * d[4]
        for d in (dx, dy, dz)
    ]


def collide(which, load, density, velocity, force):
    half = 0.5 / density
    u = [velocity[a] + force[a] * half for a in range(3)]
    speed = u[0] * u[0] + u[1] * u[1] + u[2] * u[2]
    along = u[0] * force[0] + u[1] * force[1] + u[2] * force[2]
    keep = 1.0 - 0.5 * tau_rate
    base = (tau_rate * density) * (1.0 - 1.5 * speed) - (3.0 * keep) * along
    odd = [(3.0 * tau_rate) * density * u[a] + (3.0 * keep) * force[a] for a in range(3)]
    even = [(4.5 * tau_rate) * density * u[a] + (9.0 * keep) * force[a] for a in range(3)]

    def dot(c, vector):
        total = None
        for a in range(3):
            if c[a]:
                term = vector[a]
                if total is None:
                    total = term if c[a] > 0 else -term
                else:
                    total = total + term if c[a] > 0 else total - term
        return total

    rest = 1.0 - tau_rate
    done = set()
    for i in which:
        if i in done:
            continue
        if i == 0:
            yield 0, rest * load(0) + (1.0 / 3.0) * base
            continue
        low = i if i % 2 else i - 1
        c = [int(v) for v in lattice[low]]
        weight = 1.0 / 18.0 if low < 7 else 1.0 / 36.0
        first = weight * (base + dot(c, u) * dot(c, even))
        second = weight * dot(c, odd)
        for j, sign in ((low, 1), (low + 1, -1)):
            if j in which:
                done.add(j)
                yield j, rest * load(j) + (first + second if sign > 0 else first - second)


def placed(value, row, into):
    q = row % 8
    lane = lanes()
    mask = jnp.logical_and(lane >= SLOTS * q, lane < SLOTS * q + SLOTS)
    return jnp.where(mask, roll_y(value, 8 + SLOTS * q), into)


def moments_kernel(
    pop_hbm,
    order_hbm,
    base_ref,
    edge_ref,
    strip_ref,
    pop_ref,
    order_ref,
    sems,
):
    copies = [
        pltpu.make_async_copy(order_hbm, order_ref, sems.at[0]),
        pltpu.make_async_copy(pop_hbm, pop_ref, sems.at[1]),
    ]
    for copy in copies:
        copy.start()
    for copy in copies:
        copy.wait()

    def pop(i, x):
        return pop_ref[i, pl.ds(x, 8, stride=8), :]

    for x in range(8):
        p = [pop(i, x) for i in range(19)]
        density = p[0]
        for i in range(1, 19):
            density = density + p[i]
        inverse = 1.0 / density
        for a in range(3):
            plus = [p[i] for i in range(19) if lattice[i][a] == 1]
            minus = [p[i] for i in range(19) if lattice[i][a] == -1]
            momentum = functools.reduce(lambda s, t: s + t, plus) - functools.reduce(
                lambda s, t: s + t, minus
            )
            base_ref[5 + a, x] = momentum * inverse
        base_ref[8, x] = density
        for k in range(5):
            base_ref[k, x] = order_ref[k, pl.ds(x, 8, stride=8), :]

    def pack(load, fill, field):
        low = high = jnp.full((8, 128), fill, f32)
        for x in range(4):
            low = placed(load(x), x + 4, low)
            high = placed(load(x + 4), x + 8, high)
        edge_ref[field, 0] = low
        edge_ref[field, 1] = high

    for f in range(9):
        pack(lambda x, f=f: base_ref[f, x], 1.0 if f == 8 else 0.0, f)
    for n, i in enumerate(near):
        pack(lambda x, i=i: pop(i, x), 0.0, 9 + n)

    even = is_even("row")
    for side, chosen in ((0, even), (1, jnp.logical_not(even))):

        @pl.when(chosen)
        def _():
            pack_strips(edge_ref, side, strip_ref)


def rows_kernel(base_ref, edge_ref, pop_ref, first_ref, second_ref):
    even = is_even("row")
    second_ref[FACE:] = jnp.zeros((PADDED - FACE, 8, 128), f32)
    for rows, high in ((first_ref, even), (second_ref, jnp.logical_not(even))):
        for side, chosen in ((1, high), (0, jnp.logical_not(high))):

            @pl.when(chosen)
            def _():
                if rows is first_ref:
                    pack_strips(edge_ref, side, rows.at[FACE:])
                for k in range(5):
                    rows[4 * k : 4 * k + 4] = base_ref[k, 4 * side : 4 * side + 4]
                for a in range(3):
                    rows[VEL + 3 * a : VEL + 3 * a + 3] = base_ref[5 + a, 5 * side : 5 * side + 3]
                rows[DEN] = base_ref[8, 7 * side]
                for j, i in enumerate(x_up if side else x_down):
                    rows[POP + j] = pop_ref[i, pl.ds(7 * side, 8, stride=8), :]


def pack_strips(edge_ref, side, target):
    fields = list(range(9)) + corner_fields(side)
    mine = lanes() < 64 if side else lanes() >= 64
    for n in range(0, len(fields), 2):
        value = edge_ref[fields[n], side]
        if n + 1 < len(fields):
            value = jnp.where(mine, value, roll_y(edge_ref[fields[n + 1], side], 64))
        target[n // 2] = value


def corner_fields(side):
    return [9 + near.index(i) for i in (x_up if side else x_down) if i in near]


def widen(edge_ref, strips, below, out_ref):
    left_half = lanes() < 64
    fields = list(range(9)) + corner_fields(1 if below else 0)
    half = 0 if below else 1
    for n, f in enumerate(fields):
        value = roll_y(strips[n // 2], 64 * (n % 2))
        keep = left_half if below else jnp.logical_not(left_half)
        out_ref[f, half] = jnp.where(keep, value, edge_ref[f, half])


def cross_chip_kernel(own_ref, strip_ref, edge_ref):
    even = is_even("row")
    edge_ref[...] = own_ref[...]

    @pl.when(even)
    def _():
        widen(own_ref, strip_ref, True, edge_ref)

    @pl.when(jnp.logical_not(even))
    def _():
        widen(own_ref, strip_ref, False, edge_ref)


def column_message_kernel(
    half_ref, first_row_ref, edge_ref, first_ref, second_ref, third_ref, fourth_ref
):
    even = is_even("row")
    slot = slots()
    edge_ref[...] = half_ref[...]

    @pl.when(even)
    def _():
        widen(half_ref, first_row_ref.at[FACE:], False, edge_ref)

    @pl.when(jnp.logical_not(even))
    def _():
        widen(half_ref, first_row_ref.at[FACE:], True, edge_ref)

    col_even = is_even("col")
    for h in range(2):
        for g, parts in enumerate(((0, 1, 2, 3), (4, 5, 6, 7))):
            to_left = to_right = jnp.zeros((8, 128), f32)
            for u, f in enumerate(parts):
                value = edge_ref[f, h]
                mask = jnp.logical_and(slot >= 4 * u, slot < 4 * u + 4)
                to_left = jnp.where(mask, roll_y(value, 4 * u - 8), to_left)
                to_right = jnp.where(mask, roll_y(value, 4 * u - 4), to_right)
            first_ref[2 * g + h] = third_ref[2 * g + h] = jnp.where(col_even, to_right, to_left)
            second_ref[2 * g + h] = fourth_ref[2 * g + h] = jnp.where(col_even, to_left, to_right)
        to_left = to_right = jnp.zeros((8, 128), f32)
        for s in range(6):
            left_field = 8 if s == 0 else 9 + near.index(y_down[s - 1])
            right_field = 8 if s == 0 else 9 + near.index(y_up[s - 1])
            to_left = jnp.where(slot == s, roll_y(edge_ref[left_field, h], s - 8), to_left)
            to_right = jnp.where(slot == s, roll_y(edge_ref[right_field, h], s - 7), to_right)
        first_ref[4 + h] = third_ref[4 + h] = jnp.where(col_even, to_right, to_left)
        second_ref[4 + h] = fourth_ref[4 + h] = jnp.where(col_even, to_left, to_right)


def is_late():
    return lax.rem(lax.axis_index("col"), 4) >= 2


def early_main_kernel(base_ref, recv_b, recv_a, pop_ref, third_ref, fourth_ref, *rest):
    outputs, scratch = rest[:3], rest[5:]
    rest[3][...] = third_ref[...]
    rest[4][...] = fourth_ref[...]

    @pl.when(jnp.logical_not(is_late()))
    def _():
        main_block(base_ref, recv_b, recv_a, pop_ref, *outputs, *scratch)


def late_main_kernel(base_ref, recv_b, recv_a, pop_ref, *rest):
    done, outputs, scratch = rest[:3], rest[3:6], rest[6:]

    @pl.when(is_late())
    def _():
        main_block(base_ref, recv_b, recv_a, pop_ref, *outputs, *scratch)

    @pl.when(jnp.logical_not(is_late()))
    def _():
        for source, target in zip(done, outputs):
            target[...] = source[...]


def main_block(
    base_ref,
    recv_b,
    recv_a,
    pop_ref,
    moved_ref,
    order_ref,
    far_ref,
    q_zero,
    q_one,
    q_two,
    vel,
    den,
):
    even = is_even("row")

    def halo(j):
        a, b = recv_a[j], recv_b[j]
        return jnp.where(even, b, a), jnp.where(even, a, b)

    for k in range(5):
        q_zero[k, 4:12] = base_ref[k]
        for r in range(4):
            q_zero[k, r], q_zero[k, 12 + r] = halo(4 * k + r)
    for a in range(3):
        vel[a, 3:11] = base_ref[5 + a]
        for r in range(3):
            vel[a, r], vel[a, 11 + r] = halo(VEL + 3 * a + r)
    den[0], den[9] = halo(DEN)

    def relax(source, target):
        def row(r, carry):
            q, around, dx, dy, dz = gather_stencil(
                lambda k: (source[k, r], source[k, r + 1], source[k, r - 1])
            )
            field = molecular_field(q, around, dx, dy, dz)
            new = updated(q, field, dx, dy, dz, [vel[a, r - 1] for a in range(3)])
            for k in range(5):
                target[k, r] = new[k]
            return carry

        return row

    lax.fori_loop(1, 15, relax(q_zero, q_one), 0, unroll=7)
    lax.fori_loop(2, 14, relax(q_one, q_two), 0, unroll=6)

    def last(x):
        q, around, dx, dy, dz = gather_stencil(
            lambda k: (q_two[k, x + 4], q_two[k, x + 5], q_two[k, x + 3])
        )
        field = molecular_field(q, around, dx, dy, dz)
        velocity = [vel[a, x + 3] for a in range(3)]
        return q, field, dx, dy, dz, velocity, force_of(field, dx, dy, dz)

    def stream(i, value, row):
        a, b, c = (int(v) for v in lattice[i])
        moved_ref[i, row + a] = roll_y(roll_z(value, c), b)

    def own_row(x, carry):
        q, field, dx, dy, dz, velocity, force = last(x)
        new = updated(q, field, dx, dy, dz, velocity)
        for k in range(5):
            order_ref[k, x] = new[k]
        for i, value in collide(
            range(19),
            lambda i: pop_ref[i, pl.ds(x, 8, stride=8), :],
            base_ref[8, x],
            velocity,
            force,
        ):
            stream(i, value, x + 1)
        return carry

    lax.fori_loop(0, 8, own_row, 0, unroll=4)

    for n, i in enumerate(far):
        low = high = jnp.zeros((8, 128), f32)
        for x in range(4):
            low = placed(pop_ref[i, pl.ds(x, 8, stride=8), :], x + 4, low)
            high = placed(pop_ref[i, pl.ds(x + 4, 8, stride=8), :], x + 8, high)
        if i in x_up:
            low = placed(halo(POP + x_up.index(i))[0], 3, low)
        if i in x_down:
            high = placed(halo(POP + x_down.index(i))[1], 12, high)
        far_ref[n, 0] = low
        far_ref[n, 1] = high

    for x, which, side in ((-1, x_up, 0), (8, x_down, 1)):
        _, _, _, _, _, velocity, force = last(x)
        for i, value in collide(
            which,
            lambda i, which=which, side=side: halo(POP + which.index(i))[side],
            den[9 * side],
            velocity,
            force,
        ):
            stream(i, value, x + 1)


def edge_kernel(
    edge_ref,
    far_ref,
    recv_down,
    recv_first,
    recv_up,
    recv_last,
    moved_ref,
    order_ref,
    new_pop,
    new_order,
    strip,
    q_one,
    q_two,
    pop_out,
    order_out,
    sems,
):
    even = is_even("col")
    late = is_late()
    slot, lane = slots(), lanes()

    def columns(j):
        a = jnp.where(late, recv_last[j], recv_first[j])
        b = jnp.where(late, recv_up[j], recv_down[j])
        return jnp.where(even, b, a), jnp.where(even, a, b)

    for h in range(2):
        for f in range(8):
            from_left, from_right = columns(2 * (f // 4) + h)
            u = f % 4
            own = edge_ref[f, h]
            strip[f, h] = jnp.where(slot < 8, roll_y(from_left, 4 - 4 * u), own)
            strip[f, 2 + h] = jnp.where(slot < 8, own, roll_y(from_right, 8 - 4 * u))
        from_left, from_right = columns(4 + h)
        for f in range(8, 28):
            i = f - 9
            if f == 8:
                own = edge_ref[8, h]
            elif i in near:
                own = edge_ref[9 + near.index(i), h]
            else:
                own = far_ref[far.index(i), h]
            left = right = own
            if f == 8 or i in y_up:
                s = 0 if f == 8 else 1 + y_up.index(i)
                left = jnp.where(slot == 7, roll_y(from_left, 7 - s), left)
            if f == 8 or i in y_down:
                s = 0 if f == 8 else 1 + y_down.index(i)
                right = jnp.where(slot == 8, roll_y(from_right, 8 - s), right)
            strip[f, h] = left
            strip[f, 2 + h] = right

    def neighbours(source, unit):
        other = unit ^ 1

        def load(k):
            me, that = source[k, unit], source[k, other]
            ahead = jnp.where(lane >= 112, roll_y(that, -16), roll_y(me, -16))
            behind = jnp.where(lane < 16, roll_y(that, 16), roll_y(me, 16))
            return me, ahead, behind

        return load

    def relax(source, target):
        def step(unit, carry):
            q, around, dx, dy, dz = gather_stencil(neighbours(source, unit))
            field = molecular_field(q, around, dx, dy, dz)
            return updated(q, field, dx, dy, dz, [strip[5 + a, unit] for a in range(3)])

        results = [step(unit, 0) for unit in range(4)]
        for unit in range(4):
            for k in range(5):
                target[k, unit] = results[unit][k]

    relax(strip, q_one)
    relax(q_one, q_two)

    edge_lane = jnp.logical_or(lane < 4, lane >= 124)

    def merge(field, units, load, shift_x, shift_y, target):
        halves = [jnp.where(slot < 8 - shift_y, units[2 + h], units[h]) for h in range(2)]
        rows = []
        for x in range(8):
            row = x + 4 - shift_x
            pair = roll_y(halves[row // 8], shift_y - (SLOTS * (row % 8) + 8))
            rows.append(jnp.where(edge_lane, pair, load(x)))
        for x in range(8):
            target[field, pl.ds(x, 8, stride=8), :] = rows[x]

    copies = [pltpu.make_async_copy(order_out, new_order, sems.at[0])]
    bounds = CHUNKS + (19,)
    for n, first in enumerate(CHUNKS):
        rows = pl.ds(first, bounds[n + 1] - first)
        copies.append(pltpu.make_async_copy(pop_out.at[rows], new_pop.at[rows], sems.at[n + 1]))

    relaxed, moving = [], []
    for unit in range(4):
        q, around, dx, dy, dz = gather_stencil(neighbours(q_two, unit))
        field = molecular_field(q, around, dx, dy, dz)
        velocity = [strip[5 + a, unit] for a in range(3)]
        relaxed.append(updated(q, field, dx, dy, dz, velocity))
        force = force_of(field, dx, dy, dz)
        moving.append(
            collide(
                range(19),
                lambda i, unit=unit: strip[9 + i, unit],
                strip[8, unit],
                velocity,
                force,
            )
        )
    for k in range(5):
        merge(k, [new[k] for new in relaxed], lambda x, k=k: order_ref[k, x], 0, 0, order_out)
    copies[0].start()
    for items in zip(*moving):
        i = items[0][0]
        a, b, c = (int(v) for v in lattice[i])
        units = [roll_z(value, c) for _, value in items]
        merge(i, units, lambda x, i=i: moved_ref[i, x + 1], a, b, pop_out)
        if i + 1 in bounds:
            copies[bounds.index(i + 1)].start()
    for copy in copies:
        copy.wait()


def call(kernel, out_shapes, scratch, flops, *args, from_hbm=False, to_hbm=False):
    whole, outside = (pl.BlockSpec(memory_space=m) for m in (pltpu.VMEM, pltpu.HBM))
    return pl.pallas_call(
        kernel,
        out_shape=[jax.ShapeDtypeStruct(s, f32) for s in out_shapes],
        in_specs=[outside if from_hbm else whole] * len(args),
        out_specs=[outside if to_hbm else whole] * len(out_shapes),
        scratch_shapes=[pltpu.VMEM(s, f32) if isinstance(s, tuple) else s for s in scratch],
        cost_estimate=pl.CostEstimate(
            flops=flops,
            bytes_accessed=4 * sum(math.prod(s) for s in out_shapes) + sum(4 * a.size for a in args),
            transcendentals=0,
        ),
        compiler_params=pltpu.CompilerParams(vmem_limit_bytes=12 * 1024 * 1024),
    )(*args)


def swap(size, first):
    return [
        (i, (i + 1) % size if i % 2 == first else (i - 1) % size) for i in range(size)
    ]


def crossing(size):
    down = [(i, (i + 1) % size if i % 2 else i - 1) for i in range(size) if i % 4 >= 2]
    return down, [(target, source) for source, target in down]


def part(size, late):
    return [(i, i ^ 1) for i in range(size) if (i % 4 >= 2) == late]


def body(rows, cols, populations, order_tensor):
    side = (6, 8, 128)
    base, own_edges, strips, pops = call(
        moments_kernel,
        [(9, 8, 8, 128), (NEAR, 2, 8, 128), (STRIPS, 8, 128), (19, 64, 128)],
        [(5, 64, 128), pltpu.SemaphoreType.DMA((2,))],
        2_000_000,
        pltpu.with_memory_space_constraint(populations.reshape(19, 64, 128), pltpu.HBM),
        pltpu.with_memory_space_constraint(order_tensor.reshape(5, 64, 128), pltpu.HBM),
        from_hbm=True,
    )
    recv_strip = lax.ppermute(strips, "row", swap(rows, 1))
    first_rows, second_rows = call(
        rows_kernel, [(FACE + STRIPS, 8, 128), (PADDED, 8, 128)], [], 1_000_000, base, own_edges, pops
    )
    recv_a = lax.ppermute(first_rows, "row", swap(rows, 0))
    recv_b = lax.ppermute(second_rows, "row", swap(rows, 1))
    half_edges = call(
        cross_chip_kernel, [(NEAR, 2, 8, 128)], [], CROSS_COST, own_edges, recv_strip
    )[0]
    edges, first, second, third, fourth = call(
        column_message_kernel,
        [(NEAR, 2, 8, 128), side, side, side, side],
        [],
        1_000_000,
        half_edges,
        recv_a,
    )
    down, up = crossing(cols)
    recv_down = lax.ppermute(second, "col", down)
    recv_first = lax.ppermute(first, "col", part(cols, False))
    blocks = [(19, 10, 8, 128), (5, 8, 8, 128), (FAR, 2, 8, 128)]
    scratch = [(5, 16, 8, 128)] * 3 + [(3, 14, 8, 128), (10, 8, 128)]
    *half_done, third_again, fourth_again = call(
        early_main_kernel,
        [*blocks, side, side],
        scratch,
        20_000_000,
        base,
        recv_b,
        recv_a,
        pops,
        third,
        fourth,
    )
    recv_up = lax.ppermute(fourth_again, "col", up)
    recv_last = lax.ppermute(third_again, "col", part(cols, True))
    moved, relaxed, far_edges = call(
        late_main_kernel,
        blocks,
        scratch,
        20_000_000,
        base,
        recv_b,
        recv_a,
        pops,
        *half_done,
    )
    new_pops, new_order = call(
        edge_kernel,
        [(19, 64, 128), (5, 64, 128)],
        [
            (28, 4, 8, 128),
            (5, 4, 8, 128),
            (5, 4, 8, 128),
            (19, 64, 128),
            (5, 64, 128),
            pltpu.SemaphoreType.DMA((len(CHUNKS) + 1,)),
        ],
        8_000_000,
        edges,
        far_edges,
        recv_down,
        recv_first,
        recv_up,
        recv_last,
        moved,
        relaxed,
        to_hbm=True,
    )
    return new_pops.reshape(populations.shape), new_order.reshape(order_tensor.shape)


def solution(mesh):
    spec = P(None, None, "row", "col")
    return jax.shard_map(
        functools.partial(body, mesh.shape["row"], mesh.shape["col"]),
        mesh=mesh,
        in_specs=(spec, spec),
        out_specs=(spec, spec),
        check_vma=False,
    )
```

```python
import functools
import math

import jax
import jax.numpy as jnp
import numpy as np
from jax import lax
from jax.experimental import pallas as pl
from jax.experimental.pallas import tpu as pltpu
from jax.sharding import PartitionSpec as P

lattice = np.array(
    [
        [0, 0, 0],
        [1, 0, 0],
        [-1, 0, 0],
        [0, 1, 0],
        [0, -1, 0],
        [0, 0, 1],
        [0, 0, -1],
        [1, 1, 0],
        [-1, -1, 0],
        [1, -1, 0],
        [-1, 1, 0],
        [1, 0, 1],
        [-1, 0, -1],
        [1, 0, -1],
        [-1, 0, 1],
        [0, 1, 1],
        [0, -1, -1],
        [0, 1, -1],
        [0, -1, 1],
    ]
)
tau_rate = 1.25
a_zero = 0.1
gamma_bulk = 3.0
stiffness = 0.4
pitch_wave = math.pi / 8.0
mobility_dt = 0.3

x_up = [i for i in range(19) if lattice[i][0] == 1]
x_down = [i + 1 for i in x_up]
y_up = [i for i in range(19) if lattice[i][1] == 1]
y_down = [i for i in range(19) if lattice[i][1] == -1]

VEL, DEN, POP, FACE = 20, 29, 30, 35
SLOTS = 16
near = sorted(y_up + y_down)
far = [i for i in range(19) if i not in near]
NEAR, FAR = 9 + len(near), len(far)
CHUNKS = (0, 7, 13)
f32 = jnp.float32


def lanes():
    return lax.broadcasted_iota(jnp.int32, (8, 128), 1)


def slots():
    return lax.rem(lanes(), SLOTS)


def roll_y(value, shift):
    shift = shift % 128
    return value if shift == 0 else pltpu.roll(value, shift, 1)


def roll_z(value, shift):
    shift = shift % 8
    return value if shift == 0 else pltpu.roll(value, shift, 0)


def is_even(axis):
    return lax.rem(lax.axis_index(axis), 2) == 0


def stencil(center, x_ahead, x_behind):
    y_ahead, y_behind = roll_y(center, -1), roll_y(center, 1)
    z_ahead, z_behind = roll_z(center, -1), roll_z(center, 1)
    around = (x_ahead + x_behind) + (y_ahead + y_behind) + (z_ahead + z_behind)
    return around, (x_ahead - x_behind, y_ahead - y_behind, z_ahead - z_behind)


def molecular_field(q, around, dx, dy, dz):
    q0, q1, q2, q3, q4 = q
    qzz = -(q0 + q3)
    s0, s1, s2, s3, s4 = q0 * q0, q1 * q1, q2 * q2, q3 * q3, q4 * q4
    square = s0 + s3 + qzz * qzz + 2.0 * (s1 + s2 + s4)
    third = square * (1.0 / 3.0)
    bulk = a_zero * gamma_bulk
    product = (
        s0 + s1 + s2 - third,
        q2 * q4 - q1 * qzz,
        q1 * q4 - q2 * q3,
        s1 + s3 + s4 - third,
        q1 * q2 - q4 * q0,
    )
    chiral = (
        2.0 * (dy[2] - dz[1]),
        (dy[4] - dx[2]) + (dz[0] - dz[3]),
        (dx[1] - dz[4]) - (2.0 * dy[0] + dy[3]),
        2.0 * (dz[1] - dx[4]),
        (dz[2] - dy[1]) + (dx[0] + 2.0 * dx[3]),
    )
    linear = a_zero * (gamma_bulk / 3.0 - 1.0) - stiffness * (4.0 * pitch_wave**2 + 6.0)
    factor = linear - bulk * square
    return [
        bulk * product[k]
        + factor * q[k]
        + stiffness * around[k]
        - (stiffness * pitch_wave) * chiral[k]
        for k in range(5)
    ]


def gather_stencil(load):
    q, around, dx, dy, dz = [], [], [], [], []
    for k in range(5):
        center, ahead, behind = load(k)
        total, (a, b, c) = stencil(center, ahead, behind)
        q.append(center)
        around.append(total)
        dx.append(a)
        dy.append(b)
        dz.append(c)
    return q, around, dx, dy, dz


def updated(q, field, dx, dy, dz, velocity):
    hx, hy, hz = (0.5 * v for v in velocity)
    return [
        q[k] + mobility_dt * field[k] - (hx * dx[k] + hy * dy[k] + hz * dz[k]) for k in range(5)
    ]


def force_of(field, dx, dy, dz):
    first = field[0] + 0.5 * field[3]
    second = field[3] + 0.5 * field[0]
    return [
        first * d[0] + second * d[3] + field[1] * d[1] + field[2] * d[2] + field[4] * d[4]
        for d in (dx, dy, dz)
    ]


def collide(which, load, density, velocity, force):
    half = 0.5 / density
    u = [velocity[a] + force[a] * half for a in range(3)]
    speed = u[0] * u[0] + u[1] * u[1] + u[2] * u[2]
    along = u[0] * force[0] + u[1] * force[1] + u[2] * force[2]
    keep = 1.0 - 0.5 * tau_rate
    base = (tau_rate * density) * (1.0 - 1.5 * speed) - (3.0 * keep) * along
    odd = [(3.0 * tau_rate) * density * u[a] + (3.0 * keep) * force[a] for a in range(3)]
    even = [(4.5 * tau_rate) * density * u[a] + (9.0 * keep) * force[a] for a in range(3)]

    def dot(c, vector):
        total = None
        for a in range(3):
            if c[a]:
                term = vector[a]
                if total is None:
                    total = term if c[a] > 0 else -term
                else:
                    total = total + term if c[a] > 0 else total - term
        return total

    rest = 1.0 - tau_rate
    done = set()
    for i in which:
        if i in done:
            continue
        if i == 0:
            yield 0, rest * load(0) + (1.0 / 3.0) * base
            continue
        low = i if i % 2 else i - 1
        c = [int(v) for v in lattice[low]]
        weight = 1.0 / 18.0 if low < 7 else 1.0 / 36.0
        first = weight * (base + dot(c, u) * dot(c, even))
        second = weight * dot(c, odd)
        for j, sign in ((low, 1), (low + 1, -1)):
            if j in which:
                done.add(j)
                yield j, rest * load(j) + (first + second if sign > 0 else first - second)


def moments_kernel(
    pop_hbm, order_hbm, base_ref, first_ref, second_ref, pop_ref, order_ref, sems
):
    copies = [
        pltpu.make_async_copy(order_hbm, order_ref, sems.at[0]),
        pltpu.make_async_copy(pop_hbm, pop_ref, sems.at[1]),
    ]
    for copy in copies:
        copy.start()
    for copy in copies:
        copy.wait()

    def row(x, carry):
        p = [pop_ref[i, pl.ds(x, 8, stride=8), :] for i in range(19)]
        density = p[0]
        for i in range(1, 19):
            density = density + p[i]
        inverse = 1.0 / density
        for a in range(3):
            plus = [p[i] for i in range(19) if lattice[i][a] == 1]
            minus = [p[i] for i in range(19) if lattice[i][a] == -1]
            momentum = functools.reduce(lambda s, t: s + t, plus) - functools.reduce(
                lambda s, t: s + t, minus
            )
            base_ref[5 + a, x] = momentum * inverse
        base_ref[8, x] = density
        for k in range(5):
            base_ref[k, x] = order_ref[k, pl.ds(x, 8, stride=8), :]
        return carry

    lax.fori_loop(0, 8, row, 0, unroll=8)
    even = is_even("row")
    for out, high in ((first_ref, even), (second_ref, jnp.logical_not(even))):

        @pl.when(high)
        def _():
            for k in range(5):
                out[4 * k : 4 * k + 4] = base_ref[k, 4:8]
            for a in range(3):
                out[VEL + 3 * a : VEL + 3 * a + 3] = base_ref[5 + a, 5:8]
            out[DEN] = base_ref[8, 7]
            for j, i in enumerate(x_up):
                out[POP + j] = pop_ref[i, pl.ds(7, 8, stride=8), :]

        @pl.when(jnp.logical_not(high))
        def _():
            for k in range(5):
                out[4 * k : 4 * k + 4] = base_ref[k, 0:4]
            for a in range(3):
                out[VEL + 3 * a : VEL + 3 * a + 3] = base_ref[5 + a, 0:3]
            out[DEN] = base_ref[8, 0]
            for j, i in enumerate(x_down):
                out[POP + j] = pop_ref[i, pl.ds(0, 8, stride=8), :]


def placed(value, row, into):
    q = row % 8
    lane = lanes()
    mask = jnp.logical_and(lane >= SLOTS * q, lane < SLOTS * q + SLOTS)
    return jnp.where(mask, roll_y(value, 8 + SLOTS * q), into)


def own_edges_kernel(base_ref, pop_ref, edge_ref):
    def pack(load, fill, field):
        low = high = jnp.full((8, 128), fill, f32)
        for x in range(4):
            low = placed(load(x), x + 4, low)
            high = placed(load(x + 4), x + 8, high)
        edge_ref[field, 0] = low
        edge_ref[field, 1] = high

    for f in range(9):
        pack(lambda x, f=f: base_ref[f, x], 1.0 if f == 8 else 0.0, f)
    for n, i in enumerate(near):
        pack(lambda x, i=i: pop_ref[i, pl.ds(x, 8, stride=8), :], 0.0, 9 + n)


def column_message_kernel(
    own_ref, recv_b, recv_a, edge_ref, first_ref, second_ref, third_ref, fourth_ref
):
    even = is_even("row")
    slot = slots()

    def halo(j):
        a, b = recv_a[j], recv_b[j]
        return jnp.where(even, b, a), jnp.where(even, a, b)

    def widen(field, rows):
        low, high = own_ref[field, 0], own_ref[field, 1]
        for j, row_low, row_high in rows:
            below, above = halo(j)
            low, high = placed(below, row_low, low), placed(above, row_high, high)
        edge_ref[field, 0] = low
        edge_ref[field, 1] = high

    for k in range(5):
        widen(k, [(4 * k + r, r, 12 + r) for r in range(4)])
    for a in range(3):
        widen(5 + a, [(VEL + 3 * a + r, 1 + r, 12 + r) for r in range(3)])
    widen(8, [(DEN, 3, 12)])
    for n, i in enumerate(near):
        low, high = own_ref[9 + n, 0], own_ref[9 + n, 1]
        if i in x_up:
            low = placed(halo(POP + x_up.index(i))[0], 3, low)
        if i in x_down:
            high = placed(halo(POP + x_down.index(i))[1], 12, high)
        edge_ref[9 + n, 0] = low
        edge_ref[9 + n, 1] = high

    col_even = is_even("col")
    for h in range(2):
        for g, parts in enumerate(((0, 1, 2, 3), (4, 5, 6, 7))):
            to_left = to_right = jnp.zeros((8, 128), f32)
            for u, f in enumerate(parts):
                value = edge_ref[f, h]
                mask = jnp.logical_and(slot >= 4 * u, slot < 4 * u + 4)
                to_left = jnp.where(mask, roll_y(value, 4 * u - 8), to_left)
                to_right = jnp.where(mask, roll_y(value, 4 * u - 4), to_right)
            first_ref[2 * g + h] = third_ref[2 * g + h] = jnp.where(col_even, to_right, to_left)
            second_ref[2 * g + h] = fourth_ref[2 * g + h] = jnp.where(col_even, to_left, to_right)
        to_left = to_right = jnp.zeros((8, 128), f32)
        for s in range(6):
            left_field = 8 if s == 0 else 9 + near.index(y_down[s - 1])
            right_field = 8 if s == 0 else 9 + near.index(y_up[s - 1])
            to_left = jnp.where(slot == s, roll_y(edge_ref[left_field, h], s - 8), to_left)
            to_right = jnp.where(slot == s, roll_y(edge_ref[right_field, h], s - 7), to_right)
        first_ref[4 + h] = third_ref[4 + h] = jnp.where(col_even, to_right, to_left)
        second_ref[4 + h] = fourth_ref[4 + h] = jnp.where(col_even, to_left, to_right)


def is_late():
    return lax.rem(lax.axis_index("col"), 4) >= 2


def early_main_kernel(base_ref, recv_b, recv_a, pop_ref, third_ref, fourth_ref, _, *rest):
    outputs, scratch = rest[:3], rest[5:]
    rest[3][...] = third_ref[...]
    rest[4][...] = fourth_ref[...]

    @pl.when(jnp.logical_not(is_late()))
    def _():
        main_block(base_ref, recv_b, recv_a, pop_ref, *outputs, *scratch)


def late_main_kernel(base_ref, recv_b, recv_a, pop_ref, *rest):
    done, outputs, scratch = rest[:3], rest[3:6], rest[6:]

    @pl.when(is_late())
    def _():
        main_block(base_ref, recv_b, recv_a, pop_ref, *outputs, *scratch)

    @pl.when(jnp.logical_not(is_late()))
    def _():
        for source, target in zip(done, outputs):
            target[...] = source[...]


def main_block(
    base_ref,
    recv_b,
    recv_a,
    pop_ref,
    moved_ref,
    order_ref,
    far_ref,
    q_zero,
    q_one,
    q_two,
    vel,
    den,
):
    even = is_even("row")

    def halo(j):
        a, b = recv_a[j], recv_b[j]
        return jnp.where(even, b, a), jnp.where(even, a, b)

    for k in range(5):
        q_zero[k, 4:12] = base_ref[k]
        for r in range(4):
            q_zero[k, r], q_zero[k, 12 + r] = halo(4 * k + r)
    for a in range(3):
        vel[a, 3:11] = base_ref[5 + a]
        for r in range(3):
            vel[a, r], vel[a, 11 + r] = halo(VEL + 3 * a + r)
    den[0], den[9] = halo(DEN)

    def relax(source, target):
        def row(r, carry):
            q, around, dx, dy, dz = gather_stencil(
                lambda k: (source[k, r], source[k, r + 1], source[k, r - 1])
            )
            field = molecular_field(q, around, dx, dy, dz)
            new = updated(q, field, dx, dy, dz, [vel[a, r - 1] for a in range(3)])
            for k in range(5):
                target[k, r] = new[k]
            return carry

        return row

    lax.fori_loop(1, 15, relax(q_zero, q_one), 0, unroll=7)
    lax.fori_loop(2, 14, relax(q_one, q_two), 0, unroll=6)

    def last(x):
        q, around, dx, dy, dz = gather_stencil(
            lambda k: (q_two[k, x + 4], q_two[k, x + 5], q_two[k, x + 3])
        )
        field = molecular_field(q, around, dx, dy, dz)
        velocity = [vel[a, x + 3] for a in range(3)]
        return q, field, dx, dy, dz, velocity, force_of(field, dx, dy, dz)

    def stream(i, value, row):
        a, b, c = (int(v) for v in lattice[i])
        moved_ref[i, row + a] = roll_y(roll_z(value, c), b)

    def own_row(x, carry):
        q, field, dx, dy, dz, velocity, force = last(x)
        new = updated(q, field, dx, dy, dz, velocity)
        for k in range(5):
            order_ref[k, x] = new[k]
        for i, value in collide(
            range(19),
            lambda i: pop_ref[i, pl.ds(x, 8, stride=8), :],
            base_ref[8, x],
            velocity,
            force,
        ):
            stream(i, value, x + 1)
        return carry

    lax.fori_loop(0, 8, own_row, 0, unroll=4)

    for n, i in enumerate(far):
        low = high = jnp.zeros((8, 128), f32)
        for x in range(4):
            low = placed(pop_ref[i, pl.ds(x, 8, stride=8), :], x + 4, low)
            high = placed(pop_ref[i, pl.ds(x + 4, 8, stride=8), :], x + 8, high)
        if i in x_up:
            low = placed(halo(POP + x_up.index(i))[0], 3, low)
        if i in x_down:
            high = placed(halo(POP + x_down.index(i))[1], 12, high)
        far_ref[n, 0] = low
        far_ref[n, 1] = high

    for x, which, side in ((-1, x_up, 0), (8, x_down, 1)):
        _, _, _, _, _, velocity, force = last(x)
        for i, value in collide(
            which,
            lambda i, which=which, side=side: halo(POP + which.index(i))[side],
            den[9 * side],
            velocity,
            force,
        ):
            stream(i, value, x + 1)


def edge_kernel(
    edge_ref,
    far_ref,
    recv_down,
    recv_first,
    recv_up,
    recv_last,
    moved_ref,
    order_ref,
    new_pop,
    new_order,
    strip,
    q_one,
    q_two,
    pop_out,
    order_out,
    sems,
):
    even = is_even("col")
    late = is_late()
    slot, lane = slots(), lanes()

    def columns(j):
        a = jnp.where(late, recv_last[j], recv_first[j])
        b = jnp.where(late, recv_up[j], recv_down[j])
        return jnp.where(even, b, a), jnp.where(even, a, b)

    for h in range(2):
        for f in range(8):
            from_left, from_right = columns(2 * (f // 4) + h)
            u = f % 4
            own = edge_ref[f, h]
            strip[f, h] = jnp.where(slot < 8, roll_y(from_left, 4 - 4 * u), own)
            strip[f, 2 + h] = jnp.where(slot < 8, own, roll_y(from_right, 8 - 4 * u))
        from_left, from_right = columns(4 + h)
        for f in range(8, 28):
            i = f - 9
            if f == 8:
                own = edge_ref[8, h]
            elif i in near:
                own = edge_ref[9 + near.index(i), h]
            else:
                own = far_ref[far.index(i), h]
            left = right = own
            if f == 8 or i in y_up:
                s = 0 if f == 8 else 1 + y_up.index(i)
                left = jnp.where(slot == 7, roll_y(from_left, 7 - s), left)
            if f == 8 or i in y_down:
                s = 0 if f == 8 else 1 + y_down.index(i)
                right = jnp.where(slot == 8, roll_y(from_right, 8 - s), right)
            strip[f, h] = left
            strip[f, 2 + h] = right

    def neighbours(source, unit):
        other = unit ^ 1

        def load(k):
            me, that = source[k, unit], source[k, other]
            ahead = jnp.where(lane >= 112, roll_y(that, -16), roll_y(me, -16))
            behind = jnp.where(lane < 16, roll_y(that, 16), roll_y(me, 16))
            return me, ahead, behind

        return load

    def relax(source, target):
        def step(unit, carry):
            q, around, dx, dy, dz = gather_stencil(neighbours(source, unit))
            field = molecular_field(q, around, dx, dy, dz)
            return updated(q, field, dx, dy, dz, [strip[5 + a, unit] for a in range(3)])

        results = [step(unit, 0) for unit in range(4)]
        for unit in range(4):
            for k in range(5):
                target[k, unit] = results[unit][k]

    relax(strip, q_one)
    relax(q_one, q_two)

    edge_lane = jnp.logical_or(lane < 4, lane >= 124)

    def merge(field, units, load, shift_x, shift_y, target):
        halves = [jnp.where(slot < 8 - shift_y, units[2 + h], units[h]) for h in range(2)]
        rows = []
        for x in range(8):
            row = x + 4 - shift_x
            pair = roll_y(halves[row // 8], shift_y - (SLOTS * (row % 8) + 8))
            rows.append(jnp.where(edge_lane, pair, load(x)))
        for x in range(8):
            target[field, pl.ds(x, 8, stride=8), :] = rows[x]

    copies = [pltpu.make_async_copy(order_out, new_order, sems.at[0])]
    bounds = CHUNKS + (19,)
    for n, first in enumerate(CHUNKS):
        rows = pl.ds(first, bounds[n + 1] - first)
        copies.append(pltpu.make_async_copy(pop_out.at[rows], new_pop.at[rows], sems.at[n + 1]))

    relaxed, moving = [], []
    for unit in range(4):
        q, around, dx, dy, dz = gather_stencil(neighbours(q_two, unit))
        field = molecular_field(q, around, dx, dy, dz)
        velocity = [strip[5 + a, unit] for a in range(3)]
        relaxed.append(updated(q, field, dx, dy, dz, velocity))
        force = force_of(field, dx, dy, dz)
        moving.append(
            collide(
                range(19),
                lambda i, unit=unit: strip[9 + i, unit],
                strip[8, unit],
                velocity,
                force,
            )
        )
    for k in range(5):
        merge(k, [new[k] for new in relaxed], lambda x, k=k: order_ref[k, x], 0, 0, order_out)
    copies[0].start()
    for items in zip(*moving):
        i = items[0][0]
        a, b, c = (int(v) for v in lattice[i])
        units = [roll_z(value, c) for _, value in items]
        merge(i, units, lambda x, i=i: moved_ref[i, x + 1], a, b, pop_out)
        if i + 1 in bounds:
            copies[bounds.index(i + 1)].start()
    for copy in copies:
        copy.wait()


def call(kernel, out_shapes, scratch, flops, *args, from_hbm=False, to_hbm=False):
    whole, outside = (pl.BlockSpec(memory_space=m) for m in (pltpu.VMEM, pltpu.HBM))
    return pl.pallas_call(
        kernel,
        out_shape=[jax.ShapeDtypeStruct(s, f32) for s in out_shapes],
        in_specs=[outside if from_hbm else whole] * len(args),
        out_specs=[outside if to_hbm else whole] * len(out_shapes),
        scratch_shapes=[pltpu.VMEM(s, f32) if isinstance(s, tuple) else s for s in scratch],
        cost_estimate=pl.CostEstimate(
            flops=flops,
            bytes_accessed=4 * sum(math.prod(s) for s in out_shapes) + sum(4 * a.size for a in args),
            transcendentals=0,
        ),
        compiler_params=pltpu.CompilerParams(vmem_limit_bytes=12 * 1024 * 1024),
    )(*args)


def swap(size, first):
    return [
        (i, (i + 1) % size if i % 2 == first else (i - 1) % size) for i in range(size)
    ]


def crossing(size):
    down = [(i, (i + 1) % size if i % 2 else i - 1) for i in range(size) if i % 4 >= 2]
    return down, [(target, source) for source, target in down]


def part(size, late):
    return [(i, i ^ 1) for i in range(size) if (i % 4 >= 2) == late]


def body(rows, cols, populations, order_tensor):
    face, side = (FACE, 8, 128), (6, 8, 128)
    base, first, second, pops = call(
        moments_kernel,
        [(9, 8, 8, 128), face, face, (19, 64, 128)],
        [(5, 64, 128), pltpu.SemaphoreType.DMA((2,))],
        2_000_000,
        pltpu.with_memory_space_constraint(populations.reshape(19, 64, 128), pltpu.HBM),
        pltpu.with_memory_space_constraint(order_tensor.reshape(5, 64, 128), pltpu.HBM),
        from_hbm=True,
    )
    recv_b = lax.ppermute(second, "row", swap(rows, 1))
    recv_a = lax.ppermute(first, "row", swap(rows, 0))
    own_edges = call(own_edges_kernel, [(NEAR, 2, 8, 128)], [], 2_000_000, base, pops)[0]
    edges, first, second, third, fourth = call(
        column_message_kernel,
        [(NEAR, 2, 8, 128), side, side, side, side],
        [],
        1_000_000,
        own_edges,
        recv_b,
        recv_a,
    )
    down, up = crossing(cols)
    recv_down = lax.ppermute(second, "col", down)
    late = lax.rem(lax.axis_index("col"), 4) >= 2
    recv_first = lax.cond(
        late, lambda m: m, lambda m: lax.ppermute(m, "col", part(cols, False)), first
    )
    blocks = [(19, 10, 8, 128), (5, 8, 8, 128), (FAR, 2, 8, 128)]
    scratch = [(5, 16, 8, 128)] * 3 + [(3, 14, 8, 128), (10, 8, 128)]
    *half_done, third_again, fourth_again = call(
        early_main_kernel,
        [*blocks, side, side],
        scratch,
        20_000_000,
        base,
        recv_b,
        recv_a,
        pops,
        third,
        fourth,
        recv_first,
    )
    recv_up = lax.ppermute(fourth_again, "col", up)
    recv_last = lax.cond(
        late, lambda m: lax.ppermute(m, "col", part(cols, True)), lambda m: m, third_again
    )
    moved, relaxed, far_edges = call(
        late_main_kernel,
        blocks,
        scratch,
        20_000_000,
        base,
        recv_b,
        recv_a,
        pops,
        *half_done,
    )
    new_pops, new_order = call(
        edge_kernel,
        [(19, 64, 128), (5, 64, 128)],
        [
            (28, 4, 8, 128),
            (5, 4, 8, 128),
            (5, 4, 8, 128),
            (19, 64, 128),
            (5, 64, 128),
            pltpu.SemaphoreType.DMA((len(CHUNKS) + 1,)),
        ],
        8_000_000,
        edges,
        far_edges,
        recv_down,
        recv_first,
        recv_up,
        recv_last,
        moved,
        relaxed,
        to_hbm=True,
    )
    return new_pops.reshape(populations.shape), new_order.reshape(order_tensor.shape)


def solution(mesh):
    spec = P(None, None, "row", "col")
    return jax.shard_map(
        functools.partial(body, mesh.shape["row"], mesh.shape["col"]),
        mesh=mesh,
        in_specs=(spec, spec),
        out_specs=(spec, spec),
        check_vma=False,
    )
```

```python
import functools
import math

import jax
import jax.numpy as jnp
import numpy as np
from jax import lax
from jax.experimental import pallas as pl
from jax.experimental.pallas import tpu as pltpu
from jax.sharding import PartitionSpec as P

lattice = np.array(
    [
        [0, 0, 0],
        [1, 0, 0],
        [-1, 0, 0],
        [0, 1, 0],
        [0, -1, 0],
        [0, 0, 1],
        [0, 0, -1],
        [1, 1, 0],
        [-1, -1, 0],
        [1, -1, 0],
        [-1, 1, 0],
        [1, 0, 1],
        [-1, 0, -1],
        [1, 0, -1],
        [-1, 0, 1],
        [0, 1, 1],
        [0, -1, -1],
        [0, 1, -1],
        [0, -1, 1],
    ]
)
tau_rate = 1.25
a_zero = 0.1
gamma_bulk = 3.0
stiffness = 0.4
pitch_wave = math.pi / 8.0
mobility_dt = 0.3

x_up = [i for i in range(19) if lattice[i][0] == 1]
x_down = [i + 1 for i in x_up]
y_up = [i for i in range(19) if lattice[i][1] == 1]
y_down = [i for i in range(19) if lattice[i][1] == -1]

VEL, DEN, POP, FACE = 20, 29, 30, 35
SLOTS = 16
near = sorted(y_up + y_down)
far = [i for i in range(19) if i not in near]
NEAR, FAR = 9 + len(near), len(far)
CHUNKS = (0, 7, 13)
f32 = jnp.float32


def lanes():
    return lax.broadcasted_iota(jnp.int32, (8, 128), 1)


def slots():
    return lax.rem(lanes(), SLOTS)


def roll_y(value, shift):
    shift = shift % 128
    return value if shift == 0 else pltpu.roll(value, shift, 1)


def roll_z(value, shift):
    shift = shift % 8
    return value if shift == 0 else pltpu.roll(value, shift, 0)


def is_even(axis):
    return lax.rem(lax.axis_index(axis), 2) == 0


def stencil(center, x_ahead, x_behind):
    y_ahead, y_behind = roll_y(center, -1), roll_y(center, 1)
    z_ahead, z_behind = roll_z(center, -1), roll_z(center, 1)
    around = (x_ahead + x_behind) + (y_ahead + y_behind) + (z_ahead + z_behind)
    return around, (x_ahead - x_behind, y_ahead - y_behind, z_ahead - z_behind)


def molecular_field(q, around, dx, dy, dz):
    q0, q1, q2, q3, q4 = q
    qzz = -(q0 + q3)
    s0, s1, s2, s3, s4 = q0 * q0, q1 * q1, q2 * q2, q3 * q3, q4 * q4
    square = s0 + s3 + qzz * qzz + 2.0 * (s1 + s2 + s4)
    third = square * (1.0 / 3.0)
    bulk = a_zero * gamma_bulk
    product = (
        s0 + s1 + s2 - third,
        q2 * q4 - q1 * qzz,
        q1 * q4 - q2 * q3,
        s1 + s3 + s4 - third,
        q1 * q2 - q4 * q0,
    )
    chiral = (
        2.0 * (dy[2] - dz[1]),
        (dy[4] - dx[2]) + (dz[0] - dz[3]),
        (dx[1] - dz[4]) - (2.0 * dy[0] + dy[3]),
        2.0 * (dz[1] - dx[4]),
        (dz[2] - dy[1]) + (dx[0] + 2.0 * dx[3]),
    )
    linear = a_zero * (gamma_bulk / 3.0 - 1.0) - stiffness * (4.0 * pitch_wave**2 + 6.0)
    factor = linear - bulk * square
    return [
        bulk * product[k]
        + factor * q[k]
        + stiffness * around[k]
        - (stiffness * pitch_wave) * chiral[k]
        for k in range(5)
    ]


def gather_stencil(load):
    q, around, dx, dy, dz = [], [], [], [], []
    for k in range(5):
        center, ahead, behind = load(k)
        total, (a, b, c) = stencil(center, ahead, behind)
        q.append(center)
        around.append(total)
        dx.append(a)
        dy.append(b)
        dz.append(c)
    return q, around, dx, dy, dz


def updated(q, field, dx, dy, dz, velocity):
    hx, hy, hz = (0.5 * v for v in velocity)
    return [
        q[k] + mobility_dt * field[k] - (hx * dx[k] + hy * dy[k] + hz * dz[k]) for k in range(5)
    ]


def force_of(field, dx, dy, dz):
    first = field[0] + 0.5 * field[3]
    second = field[3] + 0.5 * field[0]
    return [
        first * d[0] + second * d[3] + field[1] * d[1] + field[2] * d[2] + field[4] * d[4]
        for d in (dx, dy, dz)
    ]


def collide(which, load, density, velocity, force):
    half = 0.5 / density
    u = [velocity[a] + force[a] * half for a in range(3)]
    speed = u[0] * u[0] + u[1] * u[1] + u[2] * u[2]
    along = u[0] * force[0] + u[1] * force[1] + u[2] * force[2]
    keep = 1.0 - 0.5 * tau_rate
    base = (tau_rate * density) * (1.0 - 1.5 * speed) - (3.0 * keep) * along
    odd = [(3.0 * tau_rate) * density * u[a] + (3.0 * keep) * force[a] for a in range(3)]
    even = [(4.5 * tau_rate) * density * u[a] + (9.0 * keep) * force[a] for a in range(3)]

    def dot(c, vector):
        total = None
        for a in range(3):
            if c[a]:
                term = vector[a]
                if total is None:
                    total = term if c[a] > 0 else -term
                else:
                    total = total + term if c[a] > 0 else total - term
        return total

    rest = 1.0 - tau_rate
    done = set()
    for i in which:
        if i in done:
            continue
        if i == 0:
            yield 0, rest * load(0) + (1.0 / 3.0) * base
            continue
        low = i if i % 2 else i - 1
        c = [int(v) for v in lattice[low]]
        weight = 1.0 / 18.0 if low < 7 else 1.0 / 36.0
        first = weight * (base + dot(c, u) * dot(c, even))
        second = weight * dot(c, odd)
        for j, sign in ((low, 1), (low + 1, -1)):
            if j in which:
                done.add(j)
                yield j, rest * load(j) + (first + second if sign > 0 else first - second)


def moments_kernel(
    pop_hbm, order_hbm, base_ref, first_ref, second_ref, pop_ref, order_ref, sems
):
    copies = [
        pltpu.make_async_copy(order_hbm, order_ref, sems.at[0]),
        pltpu.make_async_copy(pop_hbm, pop_ref, sems.at[1]),
    ]
    for copy in copies:
        copy.start()
    for copy in copies:
        copy.wait()

    def row(x, carry):
        p = [pop_ref[i, pl.ds(x, 8, stride=8), :] for i in range(19)]
        density = p[0]
        for i in range(1, 19):
            density = density + p[i]
        inverse = 1.0 / density
        for a in range(3):
            plus = [p[i] for i in range(19) if lattice[i][a] == 1]
            minus = [p[i] for i in range(19) if lattice[i][a] == -1]
            momentum = functools.reduce(lambda s, t: s + t, plus) - functools.reduce(
                lambda s, t: s + t, minus
            )
            base_ref[5 + a, x] = momentum * inverse
        base_ref[8, x] = density
        for k in range(5):
            base_ref[k, x] = order_ref[k, pl.ds(x, 8, stride=8), :]
        return carry

    lax.fori_loop(0, 8, row, 0, unroll=8)
    even = is_even("row")
    for out, high in ((first_ref, even), (second_ref, jnp.logical_not(even))):

        @pl.when(high)
        def _():
            for k in range(5):
                out[4 * k : 4 * k + 4] = base_ref[k, 4:8]
            for a in range(3):
                out[VEL + 3 * a : VEL + 3 * a + 3] = base_ref[5 + a, 5:8]
            out[DEN] = base_ref[8, 7]
            for j, i in enumerate(x_up):
                out[POP + j] = pop_ref[i, pl.ds(7, 8, stride=8), :]

        @pl.when(jnp.logical_not(high))
        def _():
            for k in range(5):
                out[4 * k : 4 * k + 4] = base_ref[k, 0:4]
            for a in range(3):
                out[VEL + 3 * a : VEL + 3 * a + 3] = base_ref[5 + a, 0:3]
            out[DEN] = base_ref[8, 0]
            for j, i in enumerate(x_down):
                out[POP + j] = pop_ref[i, pl.ds(0, 8, stride=8), :]


def placed(value, row, into):
    q = row % 8
    lane = lanes()
    mask = jnp.logical_and(lane >= SLOTS * q, lane < SLOTS * q + SLOTS)
    return jnp.where(mask, roll_y(value, 8 + SLOTS * q), into)


def own_edges_kernel(base_ref, pop_ref, edge_ref):
    def pack(load, fill, field):
        low = high = jnp.full((8, 128), fill, f32)
        for x in range(4):
            low = placed(load(x), x + 4, low)
            high = placed(load(x + 4), x + 8, high)
        edge_ref[field, 0] = low
        edge_ref[field, 1] = high

    for f in range(9):
        pack(lambda x, f=f: base_ref[f, x], 1.0 if f == 8 else 0.0, f)
    for n, i in enumerate(near):
        pack(lambda x, i=i: pop_ref[i, pl.ds(x, 8, stride=8), :], 0.0, 9 + n)


def column_message_kernel(
    own_ref, recv_b, recv_a, edge_ref, first_ref, second_ref, third_ref, fourth_ref
):
    even = is_even("row")
    slot = slots()

    def halo(j):
        a, b = recv_a[j], recv_b[j]
        return jnp.where(even, b, a), jnp.where(even, a, b)

    def widen(field, rows):
        low, high = own_ref[field, 0], own_ref[field, 1]
        for j, row_low, row_high in rows:
            below, above = halo(j)
            low, high = placed(below, row_low, low), placed(above, row_high, high)
        edge_ref[field, 0] = low
        edge_ref[field, 1] = high

    for k in range(5):
        widen(k, [(4 * k + r, r, 12 + r) for r in range(4)])
    for a in range(3):
        widen(5 + a, [(VEL + 3 * a + r, 1 + r, 12 + r) for r in range(3)])
    widen(8, [(DEN, 3, 12)])
    for n, i in enumerate(near):
        low, high = own_ref[9 + n, 0], own_ref[9 + n, 1]
        if i in x_up:
            low = placed(halo(POP + x_up.index(i))[0], 3, low)
        if i in x_down:
            high = placed(halo(POP + x_down.index(i))[1], 12, high)
        edge_ref[9 + n, 0] = low
        edge_ref[9 + n, 1] = high

    col_even = is_even("col")
    for h in range(2):
        for g, parts in enumerate(((0, 1, 2, 3), (4, 5, 6, 7))):
            to_left = to_right = jnp.zeros((8, 128), f32)
            for u, f in enumerate(parts):
                value = edge_ref[f, h]
                mask = jnp.logical_and(slot >= 4 * u, slot < 4 * u + 4)
                to_left = jnp.where(mask, roll_y(value, 4 * u - 8), to_left)
                to_right = jnp.where(mask, roll_y(value, 4 * u - 4), to_right)
            first_ref[2 * g + h] = third_ref[2 * g + h] = jnp.where(col_even, to_right, to_left)
            second_ref[2 * g + h] = fourth_ref[2 * g + h] = jnp.where(col_even, to_left, to_right)
        to_left = to_right = jnp.zeros((8, 128), f32)
        for s in range(6):
            left_field = 8 if s == 0 else 9 + near.index(y_down[s - 1])
            right_field = 8 if s == 0 else 9 + near.index(y_up[s - 1])
            to_left = jnp.where(slot == s, roll_y(edge_ref[left_field, h], s - 8), to_left)
            to_right = jnp.where(slot == s, roll_y(edge_ref[right_field, h], s - 7), to_right)
        first_ref[4 + h] = third_ref[4 + h] = jnp.where(col_even, to_right, to_left)
        second_ref[4 + h] = fourth_ref[4 + h] = jnp.where(col_even, to_left, to_right)


def is_late():
    return lax.rem(lax.axis_index("col"), 4) >= 2


def early_main_kernel(base_ref, recv_b, recv_a, pop_ref, third_ref, fourth_ref, _, *rest):
    outputs, scratch = rest[:3], rest[5:]
    rest[3][...] = third_ref[...]
    rest[4][...] = fourth_ref[...]

    @pl.when(jnp.logical_not(is_late()))
    def _():
        main_block(base_ref, recv_b, recv_a, pop_ref, *outputs, *scratch)


def late_main_kernel(base_ref, recv_b, recv_a, pop_ref, *rest):
    done, outputs, scratch = rest[:3], rest[3:6], rest[6:]

    @pl.when(is_late())
    def _():
        main_block(base_ref, recv_b, recv_a, pop_ref, *outputs, *scratch)

    @pl.when(jnp.logical_not(is_late()))
    def _():
        for source, target in zip(done, outputs):
            target[...] = source[...]


def main_block(
    base_ref,
    recv_b,
    recv_a,
    pop_ref,
    moved_ref,
    order_ref,
    far_ref,
    q_zero,
    q_one,
    q_two,
    vel,
    den,
):
    even = is_even("row")

    def halo(j):
        a, b = recv_a[j], recv_b[j]
        return jnp.where(even, b, a), jnp.where(even, a, b)

    for k in range(5):
        q_zero[k, 4:12] = base_ref[k]
        for r in range(4):
            q_zero[k, r], q_zero[k, 12 + r] = halo(4 * k + r)
    for a in range(3):
        vel[a, 3:11] = base_ref[5 + a]
        for r in range(3):
            vel[a, r], vel[a, 11 + r] = halo(VEL + 3 * a + r)
    den[0], den[9] = halo(DEN)

    def relax(source, target):
        def row(r, carry):
            q, around, dx, dy, dz = gather_stencil(
                lambda k: (source[k, r], source[k, r + 1], source[k, r - 1])
            )
            field = molecular_field(q, around, dx, dy, dz)
            new = updated(q, field, dx, dy, dz, [vel[a, r - 1] for a in range(3)])
            for k in range(5):
                target[k, r] = new[k]
            return carry

        return row

    lax.fori_loop(1, 15, relax(q_zero, q_one), 0, unroll=7)
    lax.fori_loop(2, 14, relax(q_one, q_two), 0, unroll=6)

    def last(x):
        q, around, dx, dy, dz = gather_stencil(
            lambda k: (q_two[k, x + 4], q_two[k, x + 5], q_two[k, x + 3])
        )
        field = molecular_field(q, around, dx, dy, dz)
        velocity = [vel[a, x + 3] for a in range(3)]
        return q, field, dx, dy, dz, velocity, force_of(field, dx, dy, dz)

    def stream(i, value, row):
        a, b, c = (int(v) for v in lattice[i])
        moved_ref[i, row + a] = roll_y(roll_z(value, c), b)

    def own_row(x, carry):
        q, field, dx, dy, dz, velocity, force = last(x)
        new = updated(q, field, dx, dy, dz, velocity)
        for k in range(5):
            order_ref[k, x] = new[k]
        for i, value in collide(
            range(19),
            lambda i: pop_ref[i, pl.ds(x, 8, stride=8), :],
            base_ref[8, x],
            velocity,
            force,
        ):
            stream(i, value, x + 1)
        return carry

    lax.fori_loop(0, 8, own_row, 0, unroll=4)

    for n, i in enumerate(far):
        low = high = jnp.zeros((8, 128), f32)
        for x in range(4):
            low = placed(pop_ref[i, pl.ds(x, 8, stride=8), :], x + 4, low)
            high = placed(pop_ref[i, pl.ds(x + 4, 8, stride=8), :], x + 8, high)
        if i in x_up:
            low = placed(halo(POP + x_up.index(i))[0], 3, low)
        if i in x_down:
            high = placed(halo(POP + x_down.index(i))[1], 12, high)
        far_ref[n, 0] = low
        far_ref[n, 1] = high

    for x, which, side in ((-1, x_up, 0), (8, x_down, 1)):
        _, _, _, _, _, velocity, force = last(x)
        for i, value in collide(
            which,
            lambda i, which=which, side=side: halo(POP + which.index(i))[side],
            den[9 * side],
            velocity,
            force,
        ):
            stream(i, value, x + 1)


def early_edge_kernel(edge_ref, far_ref, recv_down, recv_first, moved_ref, order_ref, *rest):
    @pl.when(jnp.logical_not(is_late()))
    def _():
        edge_block(edge_ref, far_ref, recv_down, recv_first, moved_ref, order_ref, *rest)


def late_edge_kernel(edge_ref, far_ref, recv_up, recv_last, moved_ref, order_ref, *rest):
    @pl.when(is_late())
    def _():
        edge_block(edge_ref, far_ref, recv_up, recv_last, moved_ref, order_ref, *rest[2:])


def edge_block(
    edge_ref,
    far_ref,
    recv_b,
    recv_a,
    moved_ref,
    order_ref,
    new_pop,
    new_order,
    strip,
    q_one,
    q_two,
    pop_out,
    order_out,
    sems,
):
    even = is_even("col")
    slot, lane = slots(), lanes()

    def columns(j):
        a, b = recv_a[j], recv_b[j]
        return jnp.where(even, b, a), jnp.where(even, a, b)

    for h in range(2):
        for f in range(8):
            from_left, from_right = columns(2 * (f // 4) + h)
            u = f % 4
            own = edge_ref[f, h]
            strip[f, h] = jnp.where(slot < 8, roll_y(from_left, 4 - 4 * u), own)
            strip[f, 2 + h] = jnp.where(slot < 8, own, roll_y(from_right, 8 - 4 * u))
        from_left, from_right = columns(4 + h)
        for f in range(8, 28):
            i = f - 9
            if f == 8:
                own = edge_ref[8, h]
            elif i in near:
                own = edge_ref[9 + near.index(i), h]
            else:
                own = far_ref[far.index(i), h]
            left = right = own
            if f == 8 or i in y_up:
                s = 0 if f == 8 else 1 + y_up.index(i)
                left = jnp.where(slot == 7, roll_y(from_left, 7 - s), left)
            if f == 8 or i in y_down:
                s = 0 if f == 8 else 1 + y_down.index(i)
                right = jnp.where(slot == 8, roll_y(from_right, 8 - s), right)
            strip[f, h] = left
            strip[f, 2 + h] = right

    def neighbours(source, unit):
        other = unit ^ 1

        def load(k):
            me, that = source[k, unit], source[k, other]
            ahead = jnp.where(lane >= 112, roll_y(that, -16), roll_y(me, -16))
            behind = jnp.where(lane < 16, roll_y(that, 16), roll_y(me, 16))
            return me, ahead, behind

        return load

    def relax(source, target):
        def step(unit, carry):
            q, around, dx, dy, dz = gather_stencil(neighbours(source, unit))
            field = molecular_field(q, around, dx, dy, dz)
            return updated(q, field, dx, dy, dz, [strip[5 + a, unit] for a in range(3)])

        results = [step(unit, 0) for unit in range(4)]
        for unit in range(4):
            for k in range(5):
                target[k, unit] = results[unit][k]

    relax(strip, q_one)
    relax(q_one, q_two)

    edge_lane = jnp.logical_or(lane < 4, lane >= 124)

    def merge(field, units, load, shift_x, shift_y, target):
        halves = [jnp.where(slot < 8 - shift_y, units[2 + h], units[h]) for h in range(2)]
        rows = []
        for x in range(8):
            row = x + 4 - shift_x
            pair = roll_y(halves[row // 8], shift_y - (SLOTS * (row % 8) + 8))
            rows.append(jnp.where(edge_lane, pair, load(x)))
        for x in range(8):
            target[field, pl.ds(x, 8, stride=8), :] = rows[x]

    copies = [pltpu.make_async_copy(order_out, new_order, sems.at[0])]
    bounds = CHUNKS + (19,)
    for n, first in enumerate(CHUNKS):
        rows = pl.ds(first, bounds[n + 1] - first)
        copies.append(pltpu.make_async_copy(pop_out.at[rows], new_pop.at[rows], sems.at[n + 1]))

    relaxed, moving = [], []
    for unit in range(4):
        q, around, dx, dy, dz = gather_stencil(neighbours(q_two, unit))
        field = molecular_field(q, around, dx, dy, dz)
        velocity = [strip[5 + a, unit] for a in range(3)]
        relaxed.append(updated(q, field, dx, dy, dz, velocity))
        force = force_of(field, dx, dy, dz)
        moving.append(
            collide(
                range(19),
                lambda i, unit=unit: strip[9 + i, unit],
                strip[8, unit],
                velocity,
                force,
            )
        )
    for k in range(5):
        merge(k, [new[k] for new in relaxed], lambda x, k=k: order_ref[k, x], 0, 0, order_out)
    copies[0].start()
    for items in zip(*moving):
        i = items[0][0]
        a, b, c = (int(v) for v in lattice[i])
        units = [roll_z(value, c) for _, value in items]
        merge(i, units, lambda x, i=i: moved_ref[i, x + 1], a, b, pop_out)
        if i + 1 in bounds:
            copies[bounds.index(i + 1)].start()
    for copy in copies:
        copy.wait()


def call(kernel, out_shapes, scratch, flops, *args, hbm_args=(), to_hbm=False, aliases=None):
    whole, outside = (pl.BlockSpec(memory_space=m) for m in (pltpu.VMEM, pltpu.HBM))
    return pl.pallas_call(
        kernel,
        out_shape=[jax.ShapeDtypeStruct(s, f32) for s in out_shapes],
        in_specs=[outside if n in hbm_args else whole for n in range(len(args))],
        out_specs=[outside if to_hbm else whole] * len(out_shapes),
        scratch_shapes=[pltpu.VMEM(s, f32) if isinstance(s, tuple) else s for s in scratch],
        cost_estimate=pl.CostEstimate(
            flops=flops,
            bytes_accessed=4 * sum(math.prod(s) for s in out_shapes) + sum(4 * a.size for a in args),
            transcendentals=0,
        ),
        input_output_aliases=aliases or {},
        compiler_params=pltpu.CompilerParams(vmem_limit_bytes=12 * 1024 * 1024),
    )(*args)


def swap(size, first):
    return [
        (i, (i + 1) % size if i % 2 == first else (i - 1) % size) for i in range(size)
    ]


def crossing(size):
    down = [(i, (i + 1) % size if i % 2 else i - 1) for i in range(size) if i % 4 >= 2]
    return down, [(target, source) for source, target in down]


def part(size, late):
    return [(i, i ^ 1) for i in range(size) if (i % 4 >= 2) == late]


def body(rows, cols, populations, order_tensor):
    face, side = (FACE, 8, 128), (6, 8, 128)
    base, first, second, pops = call(
        moments_kernel,
        [(9, 8, 8, 128), face, face, (19, 64, 128)],
        [(5, 64, 128), pltpu.SemaphoreType.DMA((2,))],
        2_000_000,
        pltpu.with_memory_space_constraint(populations.reshape(19, 64, 128), pltpu.HBM),
        pltpu.with_memory_space_constraint(order_tensor.reshape(5, 64, 128), pltpu.HBM),
        hbm_args=(0, 1),
    )
    recv_b = lax.ppermute(second, "row", swap(rows, 1))
    recv_a = lax.ppermute(first, "row", swap(rows, 0))
    own_edges = call(own_edges_kernel, [(NEAR, 2, 8, 128)], [], 2_000_000, base, pops)[0]
    edges, first, second, third, fourth = call(
        column_message_kernel,
        [(NEAR, 2, 8, 128), side, side, side, side],
        [],
        1_000_000,
        own_edges,
        recv_b,
        recv_a,
    )
    down, up = crossing(cols)
    recv_down = lax.ppermute(second, "col", down)
    late = lax.rem(lax.axis_index("col"), 4) >= 2
    recv_first = lax.cond(
        late, lambda m: m, lambda m: lax.ppermute(m, "col", part(cols, False)), first
    )
    blocks = [(19, 10, 8, 128), (5, 8, 8, 128), (FAR, 2, 8, 128)]
    scratch = [(5, 16, 8, 128)] * 3 + [(3, 14, 8, 128), (10, 8, 128)]
    *half_done, third_again, fourth_again = call(
        early_main_kernel,
        [*blocks, side, side],
        scratch,
        20_000_000,
        base,
        recv_b,
        recv_a,
        pops,
        third,
        fourth,
        recv_first,
    )
    recv_up = lax.ppermute(fourth_again, "col", up)
    recv_last = lax.cond(
        late, lambda m: lax.ppermute(m, "col", part(cols, True)), lambda m: m, third_again
    )
    moved, relaxed, far_edges = call(
        late_main_kernel,
        blocks,
        scratch,
        20_000_000,
        base,
        recv_b,
        recv_a,
        pops,
        *half_done,
    )
    results = [(19, 64, 128), (5, 64, 128)]
    scratch = [
        (28, 4, 8, 128),
        (5, 4, 8, 128),
        (5, 4, 8, 128),
        *results,
        pltpu.SemaphoreType.DMA((len(CHUNKS) + 1,)),
    ]
    half_done = call(
        early_edge_kernel,
        results,
        scratch,
        8_000_000,
        edges,
        far_edges,
        recv_down,
        recv_first,
        moved,
        relaxed,
        to_hbm=True,
    )
    new_pops, new_order = call(
        late_edge_kernel,
        results,
        scratch,
        8_000_000,
        edges,
        far_edges,
        recv_up,
        recv_last,
        moved,
        relaxed,
        *half_done,
        hbm_args=(6, 7),
        to_hbm=True,
        aliases={6: 0, 7: 1},
    )
    return new_pops.reshape(populations.shape), new_order.reshape(order_tensor.shape)


def solution(mesh):
    spec = P(None, None, "row", "col")
    return jax.shard_map(
        functools.partial(body, mesh.shape["row"], mesh.shape["col"]),
        mesh=mesh,
        in_specs=(spec, spec),
        out_specs=(spec, spec),
        check_vma=False,
    )
```

```python
import functools
import math

import jax
import jax.numpy as jnp
import numpy as np
from jax import lax
from jax.experimental import pallas as pl
from jax.experimental.pallas import tpu as pltpu
from jax.sharding import PartitionSpec as P

lattice = np.array(
    [
        [0, 0, 0],
        [1, 0, 0],
        [-1, 0, 0],
        [0, 1, 0],
        [0, -1, 0],
        [0, 0, 1],
        [0, 0, -1],
        [1, 1, 0],
        [-1, -1, 0],
        [1, -1, 0],
        [-1, 1, 0],
        [1, 0, 1],
        [-1, 0, -1],
        [1, 0, -1],
        [-1, 0, 1],
        [0, 1, 1],
        [0, -1, -1],
        [0, 1, -1],
        [0, -1, 1],
    ]
)
tau_rate = 1.25
a_zero = 0.1
gamma_bulk = 3.0
stiffness = 0.4
pitch_wave = math.pi / 8.0
mobility_dt = 0.3

x_up = [i for i in range(19) if lattice[i][0] == 1]
x_down = [i + 1 for i in x_up]
y_up = [i for i in range(19) if lattice[i][1] == 1]
y_down = [i for i in range(19) if lattice[i][1] == -1]

VEL, DEN, POP, FACE = 20, 29, 30, 35
STRIPS = 6
SLOTS = 16
near = sorted(y_up + y_down)
far = [i for i in range(19) if i not in near]
NEAR, FAR = 9 + len(near), len(far)
CHUNKS = (0, 7, 13)
f32 = jnp.float32


def lanes():
    return lax.broadcasted_iota(jnp.int32, (8, 128), 1)


def slots():
    return lax.rem(lanes(), SLOTS)


def roll_y(value, shift):
    shift = shift % 128
    return value if shift == 0 else pltpu.roll(value, shift, 1)


def roll_z(value, shift):
    shift = shift % 8
    return value if shift == 0 else pltpu.roll(value, shift, 0)


def is_even(axis):
    return lax.rem(lax.axis_index(axis), 2) == 0


def stencil(center, x_ahead, x_behind):
    y_ahead, y_behind = roll_y(center, -1), roll_y(center, 1)
    z_ahead, z_behind = roll_z(center, -1), roll_z(center, 1)
    around = (x_ahead + x_behind) + (y_ahead + y_behind) + (z_ahead + z_behind)
    return around, (x_ahead - x_behind, y_ahead - y_behind, z_ahead - z_behind)


def molecular_field(q, around, dx, dy, dz):
    q0, q1, q2, q3, q4 = q
    qzz = -(q0 + q3)
    s0, s1, s2, s3, s4 = q0 * q0, q1 * q1, q2 * q2, q3 * q3, q4 * q4
    square = s0 + s3 + qzz * qzz + 2.0 * (s1 + s2 + s4)
    third = square * (1.0 / 3.0)
    bulk = a_zero * gamma_bulk
    product = (
        s0 + s1 + s2 - third,
        q2 * q4 - q1 * qzz,
        q1 * q4 - q2 * q3,
        s1 + s3 + s4 - third,
        q1 * q2 - q4 * q0,
    )
    chiral = (
        2.0 * (dy[2] - dz[1]),
        (dy[4] - dx[2]) + (dz[0] - dz[3]),
        (dx[1] - dz[4]) - (2.0 * dy[0] + dy[3]),
        2.0 * (dz[1] - dx[4]),
        (dz[2] - dy[1]) + (dx[0] + 2.0 * dx[3]),
    )
    linear = a_zero * (gamma_bulk / 3.0 - 1.0) - stiffness * (4.0 * pitch_wave**2 + 6.0)
    factor = linear - bulk * square
    return [
        bulk * product[k]
        + factor * q[k]
        + stiffness * around[k]
        - (stiffness * pitch_wave) * chiral[k]
        for k in range(5)
    ]


def gather_stencil(load):
    q, around, dx, dy, dz = [], [], [], [], []
    for k in range(5):
        center, ahead, behind = load(k)
        total, (a, b, c) = stencil(center, ahead, behind)
        q.append(center)
        around.append(total)
        dx.append(a)
        dy.append(b)
        dz.append(c)
    return q, around, dx, dy, dz


def updated(q, field, dx, dy, dz, velocity):
    hx, hy, hz = (0.5 * v for v in velocity)
    return [
        q[k] + mobility_dt * field[k] - (hx * dx[k] + hy * dy[k] + hz * dz[k]) for k in range(5)
    ]


def force_of(field, dx, dy, dz):
    first = field[0] + 0.5 * field[3]
    second = field[3] + 0.5 * field[0]
    return [
        first * d[0] + second * d[3] + field[1] * d[1] + field[2] * d[2] + field[4] * d[4]
        for d in (dx, dy, dz)
    ]


def collide(which, load, density, velocity, force):
    half = 0.5 / density
    u = [velocity[a] + force[a] * half for a in range(3)]
    speed = u[0] * u[0] + u[1] * u[1] + u[2] * u[2]
    along = u[0] * force[0] + u[1] * force[1] + u[2] * force[2]
    keep = 1.0 - 0.5 * tau_rate
    base = (tau_rate * density) * (1.0 - 1.5 * speed) - (3.0 * keep) * along
    odd = [(3.0 * tau_rate) * density * u[a] + (3.0 * keep) * force[a] for a in range(3)]
    even = [(4.5 * tau_rate) * density * u[a] + (9.0 * keep) * force[a] for a in range(3)]

    def dot(c, vector):
        total = None
        for a in range(3):
            if c[a]:
                term = vector[a]
                if total is None:
                    total = term if c[a] > 0 else -term
                else:
                    total = total + term if c[a] > 0 else total - term
        return total

    rest = 1.0 - tau_rate
    done = set()
    for i in which:
        if i in done:
            continue
        if i == 0:
            yield 0, rest * load(0) + (1.0 / 3.0) * base
            continue
        low = i if i % 2 else i - 1
        c = [int(v) for v in lattice[low]]
        weight = 1.0 / 18.0 if low < 7 else 1.0 / 36.0
        first = weight * (base + dot(c, u) * dot(c, even))
        second = weight * dot(c, odd)
        for j, sign in ((low, 1), (low + 1, -1)):
            if j in which:
                done.add(j)
                yield j, rest * load(j) + (first + second if sign > 0 else first - second)


def placed(value, row, into):
    q = row % 8
    lane = lanes()
    mask = jnp.logical_and(lane >= SLOTS * q, lane < SLOTS * q + SLOTS)
    return jnp.where(mask, roll_y(value, 8 + SLOTS * q), into)


def is_late():
    return lax.rem(lax.axis_index("col"), 4) >= 2


def moments_kernel(
    pop_hbm, order_hbm, base_ref, edge_ref, first_ref, second_ref, first_strip, second_strip, pop_ref, order_ref, sems
):
    copies = [
        pltpu.make_async_copy(order_hbm, order_ref, sems.at[0]),
        pltpu.make_async_copy(pop_hbm, pop_ref, sems.at[1]),
    ]
    for copy in copies:
        copy.start()
    for copy in copies:
        copy.wait()

    def row(x, carry):
        p = [pop_ref[i, pl.ds(x, 8, stride=8), :] for i in range(19)]
        density = p[0]
        for i in range(1, 19):
            density = density + p[i]
        inverse = 1.0 / density
        for a in range(3):
            plus = [p[i] for i in range(19) if lattice[i][a] == 1]
            minus = [p[i] for i in range(19) if lattice[i][a] == -1]
            momentum = functools.reduce(lambda s, t: s + t, plus) - functools.reduce(
                lambda s, t: s + t, minus
            )
            base_ref[5 + a, x] = momentum * inverse
        base_ref[8, x] = density
        for k in range(5):
            base_ref[k, x] = order_ref[k, pl.ds(x, 8, stride=8), :]
        return carry

    lax.fori_loop(0, 8, row, 0, unroll=8)
    def pack(load, fill, field):
        low = high = jnp.full((8, 128), fill, f32)
        for x in range(4):
            low = placed(load(x), x + 4, low)
            high = placed(load(x + 4), x + 8, high)
        edge_ref[field, 0] = low
        edge_ref[field, 1] = high

    for f in range(9):
        pack(lambda x, f=f: base_ref[f, x], 1.0 if f == 8 else 0.0, f)
    for n, i in enumerate(near):
        pack(lambda x, i=i: pop_ref[i, pl.ds(x, 8, stride=8), :], 0.0, 9 + n)

    even = is_even("row")
    for out, high in ((first_ref, even), (second_ref, jnp.logical_not(even))):

        @pl.when(high)
        def _():
            for k in range(5):
                out[4 * k : 4 * k + 4] = base_ref[k, 4:8]
            for a in range(3):
                out[VEL + 3 * a : VEL + 3 * a + 3] = base_ref[5 + a, 5:8]
            out[DEN] = base_ref[8, 7]
            for j, i in enumerate(x_up):
                out[POP + j] = pop_ref[i, pl.ds(7, 8, stride=8), :]

        @pl.when(jnp.logical_not(high))
        def _():
            for k in range(5):
                out[4 * k : 4 * k + 4] = base_ref[k, 0:4]
            for a in range(3):
                out[VEL + 3 * a : VEL + 3 * a + 3] = base_ref[5 + a, 0:3]
            out[DEN] = base_ref[8, 0]
            for j, i in enumerate(x_down):
                out[POP + j] = pop_ref[i, pl.ds(0, 8, stride=8), :]

    left_half = lanes() < 64
    for out, high in ((first_strip, even), (second_strip, jnp.logical_not(even))):
        for side, chosen in ((1, high), (0, jnp.logical_not(high))):

            @pl.when(chosen)
            def _():
                fields = list(range(9)) + corner_fields(side)
                mine = left_half if side else jnp.logical_not(left_half)
                for n in range(0, len(fields), 2):
                    value = edge_ref[fields[n], side]
                    if n + 1 < len(fields):
                        other = roll_y(edge_ref[fields[n + 1], side], 64)
                        value = jnp.where(mine, value, other)
                    out[n // 2] = value


def corner_fields(side):
    return [9 + near.index(i) for i in (x_up if side else x_down) if i in near]


def column_message_kernel(
    own_ref,
    recv_b,
    recv_a,
    strip_b,
    strip_a,
    edge_ref,
    first_ref,
    second_ref,
    third_ref,
    fourth_ref,
):
    even = is_even("row")
    slot = slots()

    def halo(j):
        a, b = recv_a[j], recv_b[j]
        return jnp.where(even, b, a), jnp.where(even, a, b)

    @pl.when(jnp.logical_not(is_late()))
    def _():
        def widen(field, rows):
            low, high = own_ref[field, 0], own_ref[field, 1]
            for j, row_low, row_high in rows:
                below, above = halo(j)
                low, high = placed(below, row_low, low), placed(above, row_high, high)
            edge_ref[field, 0] = low
            edge_ref[field, 1] = high

        for k in range(5):
            widen(k, [(4 * k + r, r, 12 + r) for r in range(4)])
        for a in range(3):
            widen(5 + a, [(VEL + 3 * a + r, 1 + r, 12 + r) for r in range(3)])
        widen(8, [(DEN, 3, 12)])
        for n, i in enumerate(near):
            low, high = own_ref[9 + n, 0], own_ref[9 + n, 1]
            if i in x_up:
                low = placed(halo(POP + x_up.index(i))[0], 3, low)
            if i in x_down:
                high = placed(halo(POP + x_down.index(i))[1], 12, high)
            edge_ref[9 + n, 0] = low
            edge_ref[9 + n, 1] = high

    @pl.when(is_late())
    def _():
        left_half = lanes() < 64
        below = [jnp.where(even, strip_b[n], strip_a[n]) for n in range(STRIPS)]
        above = [jnp.where(even, strip_a[n], strip_b[n]) for n in range(STRIPS)]
        for f in range(NEAR):
            for half, vectors, keep in (
                (0, below, left_half),
                (1, above, jnp.logical_not(left_half)),
            ):
                fields = list(range(9)) + corner_fields(1 - half)
                value = own_ref[f, half]
                if f in fields:
                    n = fields.index(f)
                    value = jnp.where(keep, roll_y(vectors[n // 2], 64 * (n % 2)), value)
                edge_ref[f, half] = value

    col_even = is_even("col")
    for h in range(2):
        for g, parts in enumerate(((0, 1, 2, 3), (4, 5, 6, 7))):
            to_left = to_right = jnp.zeros((8, 128), f32)
            for u, f in enumerate(parts):
                value = edge_ref[f, h]
                mask = jnp.logical_and(slot >= 4 * u, slot < 4 * u + 4)
                to_left = jnp.where(mask, roll_y(value, 4 * u - 8), to_left)
                to_right = jnp.where(mask, roll_y(value, 4 * u - 4), to_right)
            first_ref[2 * g + h] = third_ref[2 * g + h] = jnp.where(col_even, to_right, to_left)
            second_ref[2 * g + h] = fourth_ref[2 * g + h] = jnp.where(col_even, to_left, to_right)
        to_left = to_right = jnp.zeros((8, 128), f32)
        for s in range(6):
            left_field = 8 if s == 0 else 9 + near.index(y_down[s - 1])
            right_field = 8 if s == 0 else 9 + near.index(y_up[s - 1])
            to_left = jnp.where(slot == s, roll_y(edge_ref[left_field, h], s - 8), to_left)
            to_right = jnp.where(slot == s, roll_y(edge_ref[right_field, h], s - 7), to_right)
        first_ref[4 + h] = third_ref[4 + h] = jnp.where(col_even, to_right, to_left)
        second_ref[4 + h] = fourth_ref[4 + h] = jnp.where(col_even, to_left, to_right)


def early_main_kernel(base_ref, recv_b, recv_a, pop_ref, third_ref, fourth_ref, _, *rest):
    outputs, scratch = rest[:3], rest[5:]
    rest[3][...] = third_ref[...]
    rest[4][...] = fourth_ref[...]

    @pl.when(jnp.logical_not(is_late()))
    def _():
        main_block(base_ref, recv_b, recv_a, pop_ref, *outputs, *scratch)


def late_main_kernel(base_ref, recv_b, recv_a, pop_ref, *rest):
    done, outputs, scratch = rest[:3], rest[3:6], rest[6:]

    @pl.when(is_late())
    def _():
        main_block(base_ref, recv_b, recv_a, pop_ref, *outputs, *scratch)

    @pl.when(jnp.logical_not(is_late()))
    def _():
        for source, target in zip(done, outputs):
            target[...] = source[...]


def main_block(
    base_ref,
    recv_b,
    recv_a,
    pop_ref,
    moved_ref,
    order_ref,
    far_ref,
    q_zero,
    q_one,
    q_two,
    vel,
    den,
):
    even = is_even("row")

    def halo(j):
        a, b = recv_a[j], recv_b[j]
        return jnp.where(even, b, a), jnp.where(even, a, b)

    for k in range(5):
        q_zero[k, 4:12] = base_ref[k]
        for r in range(4):
            q_zero[k, r], q_zero[k, 12 + r] = halo(4 * k + r)
    for a in range(3):
        vel[a, 3:11] = base_ref[5 + a]
        for r in range(3):
            vel[a, r], vel[a, 11 + r] = halo(VEL + 3 * a + r)
    den[0], den[9] = halo(DEN)

    def relax(source, target):
        def row(r, carry):
            q, around, dx, dy, dz = gather_stencil(
                lambda k: (source[k, r], source[k, r + 1], source[k, r - 1])
            )
            field = molecular_field(q, around, dx, dy, dz)
            new = updated(q, field, dx, dy, dz, [vel[a, r - 1] for a in range(3)])
            for k in range(5):
                target[k, r] = new[k]
            return carry

        return row

    lax.fori_loop(1, 15, relax(q_zero, q_one), 0, unroll=7)
    lax.fori_loop(2, 14, relax(q_one, q_two), 0, unroll=6)

    def last(x):
        q, around, dx, dy, dz = gather_stencil(
            lambda k: (q_two[k, x + 4], q_two[k, x + 5], q_two[k, x + 3])
        )
        field = molecular_field(q, around, dx, dy, dz)
        velocity = [vel[a, x + 3] for a in range(3)]
        return q, field, dx, dy, dz, velocity, force_of(field, dx, dy, dz)

    def stream(i, value, row):
        a, b, c = (int(v) for v in lattice[i])
        moved_ref[i, row + a] = roll_y(roll_z(value, c), b)

    def own_row(x, carry):
        q, field, dx, dy, dz, velocity, force = last(x)
        new = updated(q, field, dx, dy, dz, velocity)
        for k in range(5):
            order_ref[k, x] = new[k]
        for i, value in collide(
            range(19),
            lambda i: pop_ref[i, pl.ds(x, 8, stride=8), :],
            base_ref[8, x],
            velocity,
            force,
        ):
            stream(i, value, x + 1)
        return carry

    lax.fori_loop(0, 8, own_row, 0, unroll=4)

    for n, i in enumerate(far):
        low = high = jnp.zeros((8, 128), f32)
        for x in range(4):
            low = placed(pop_ref[i, pl.ds(x, 8, stride=8), :], x + 4, low)
            high = placed(pop_ref[i, pl.ds(x + 4, 8, stride=8), :], x + 8, high)
        if i in x_up:
            low = placed(halo(POP + x_up.index(i))[0], 3, low)
        if i in x_down:
            high = placed(halo(POP + x_down.index(i))[1], 12, high)
        far_ref[n, 0] = low
        far_ref[n, 1] = high

    for x, which, side in ((-1, x_up, 0), (8, x_down, 1)):
        _, _, _, _, _, velocity, force = last(x)
        for i, value in collide(
            which,
            lambda i, which=which, side=side: halo(POP + which.index(i))[side],
            den[9 * side],
            velocity,
            force,
        ):
            stream(i, value, x + 1)


def early_edge_kernel(edge_ref, far_ref, recv_down, recv_first, moved_ref, order_ref, *rest):
    @pl.when(jnp.logical_not(is_late()))
    def _():
        edge_block(edge_ref, far_ref, recv_down, recv_first, moved_ref, order_ref, *rest)


def late_edge_kernel(edge_ref, far_ref, recv_up, recv_last, moved_ref, order_ref, *rest):
    @pl.when(is_late())
    def _():
        edge_block(edge_ref, far_ref, recv_up, recv_last, moved_ref, order_ref, *rest[2:])


def edge_block(
    edge_ref,
    far_ref,
    recv_b,
    recv_a,
    moved_ref,
    order_ref,
    new_pop,
    new_order,
    strip,
    q_one,
    q_two,
    pop_out,
    order_out,
    sems,
):
    even = is_even("col")
    slot, lane = slots(), lanes()

    def columns(j):
        a, b = recv_a[j], recv_b[j]
        return jnp.where(even, b, a), jnp.where(even, a, b)

    for h in range(2):
        for f in range(8):
            from_left, from_right = columns(2 * (f // 4) + h)
            u = f % 4
            own = edge_ref[f, h]
            strip[f, h] = jnp.where(slot < 8, roll_y(from_left, 4 - 4 * u), own)
            strip[f, 2 + h] = jnp.where(slot < 8, own, roll_y(from_right, 8 - 4 * u))
        from_left, from_right = columns(4 + h)
        for f in range(8, 28):
            i = f - 9
            if f == 8:
                own = edge_ref[8, h]
            elif i in near:
                own = edge_ref[9 + near.index(i), h]
            else:
                own = far_ref[far.index(i), h]
            left = right = own
            if f == 8 or i in y_up:
                s = 0 if f == 8 else 1 + y_up.index(i)
                left = jnp.where(slot == 7, roll_y(from_left, 7 - s), left)
            if f == 8 or i in y_down:
                s = 0 if f == 8 else 1 + y_down.index(i)
                right = jnp.where(slot == 8, roll_y(from_right, 8 - s), right)
            strip[f, h] = left
            strip[f, 2 + h] = right

    def neighbours(source, unit):
        other = unit ^ 1

        def load(k):
            me, that = source[k, unit], source[k, other]
            ahead = jnp.where(lane >= 112, roll_y(that, -16), roll_y(me, -16))
            behind = jnp.where(lane < 16, roll_y(that, 16), roll_y(me, 16))
            return me, ahead, behind

        return load

    def relax(source, target):
        def step(unit, carry):
            q, around, dx, dy, dz = gather_stencil(neighbours(source, unit))
            field = molecular_field(q, around, dx, dy, dz)
            return updated(q, field, dx, dy, dz, [strip[5 + a, unit] for a in range(3)])

        results = [step(unit, 0) for unit in range(4)]
        for unit in range(4):
            for k in range(5):
                target[k, unit] = results[unit][k]

    relax(strip, q_one)
    relax(q_one, q_two)

    edge_lane = jnp.logical_or(lane < 4, lane >= 124)

    def merge(field, units, load, shift_x, shift_y, target):
        halves = [jnp.where(slot < 8 - shift_y, units[2 + h], units[h]) for h in range(2)]
        rows = []
        for x in range(8):
            row = x + 4 - shift_x
            pair = roll_y(halves[row // 8], shift_y - (SLOTS * (row % 8) + 8))
            rows.append(jnp.where(edge_lane, pair, load(x)))
        for x in range(8):
            target[field, pl.ds(x, 8, stride=8), :] = rows[x]

    copies = [pltpu.make_async_copy(order_out, new_order, sems.at[0])]
    bounds = CHUNKS + (19,)
    for n, first in enumerate(CHUNKS):
        rows = pl.ds(first, bounds[n + 1] - first)
        copies.append(pltpu.make_async_copy(pop_out.at[rows], new_pop.at[rows], sems.at[n + 1]))

    relaxed, moving = [], []
    for unit in range(4):
        q, around, dx, dy, dz = gather_stencil(neighbours(q_two, unit))
        field = molecular_field(q, around, dx, dy, dz)
        velocity = [strip[5 + a, unit] for a in range(3)]
        relaxed.append(updated(q, field, dx, dy, dz, velocity))
        force = force_of(field, dx, dy, dz)
        moving.append(
            collide(
                range(19),
                lambda i, unit=unit: strip[9 + i, unit],
                strip[8, unit],
                velocity,
                force,
            )
        )
    for k in range(5):
        merge(k, [new[k] for new in relaxed], lambda x, k=k: order_ref[k, x], 0, 0, order_out)
    copies[0].start()
    for items in zip(*moving):
        i = items[0][0]
        a, b, c = (int(v) for v in lattice[i])
        units = [roll_z(value, c) for _, value in items]
        merge(i, units, lambda x, i=i: moved_ref[i, x + 1], a, b, pop_out)
        if i + 1 in bounds:
            copies[bounds.index(i + 1)].start()
    for copy in copies:
        copy.wait()


def call(kernel, out_shapes, scratch, flops, *args, hbm_args=(), to_hbm=False, aliases=None):
    whole, outside = (pl.BlockSpec(memory_space=m) for m in (pltpu.VMEM, pltpu.HBM))
    return pl.pallas_call(
        kernel,
        out_shape=[jax.ShapeDtypeStruct(s, f32) for s in out_shapes],
        in_specs=[outside if n in hbm_args else whole for n in range(len(args))],
        out_specs=[outside if to_hbm else whole] * len(out_shapes),
        scratch_shapes=[pltpu.VMEM(s, f32) if isinstance(s, tuple) else s for s in scratch],
        cost_estimate=pl.CostEstimate(
            flops=flops,
            bytes_accessed=4 * sum(math.prod(s) for s in out_shapes) + sum(4 * a.size for a in args),
            transcendentals=0,
        ),
        input_output_aliases=aliases or {},
        compiler_params=pltpu.CompilerParams(vmem_limit_bytes=12 * 1024 * 1024),
    )(*args)


def swap(size, first):
    return [
        (i, (i + 1) % size if i % 2 == first else (i - 1) % size) for i in range(size)
    ]


def crossing(size):
    down = [(i, (i + 1) % size if i % 2 else i - 1) for i in range(size) if i % 4 >= 2]
    return down, [(target, source) for source, target in down]


def part(size, late):
    return [(i, i ^ 1) for i in range(size) if (i % 4 >= 2) == late]


def body(rows, cols, populations, order_tensor):
    face, side, strip = (FACE, 8, 128), (6, 8, 128), (STRIPS, 8, 128)
    base, own_edges, first_rows, second_rows, first_strip, second_strip, pops = call(
        moments_kernel,
        [(9, 8, 8, 128), (NEAR, 2, 8, 128), face, face, strip, strip, (19, 64, 128)],
        [(5, 64, 128), pltpu.SemaphoreType.DMA((2,))],
        2_000_000,
        pltpu.with_memory_space_constraint(populations.reshape(19, 64, 128), pltpu.HBM),
        pltpu.with_memory_space_constraint(order_tensor.reshape(5, 64, 128), pltpu.HBM),
        hbm_args=(0, 1),
    )
    late = lax.rem(lax.axis_index("col"), 4) >= 2

    def swap_rows(second, first):
        return lax.ppermute(second, "row", swap(rows, 1)), lax.ppermute(first, "row", swap(rows, 0))

    recv_b, recv_a, strip_b, strip_a = lax.cond(
        late,
        lambda b, a, sb, sa: (b, a, *swap_rows(sb, sa)),
        lambda b, a, sb, sa: (*swap_rows(b, a), sb, sa),
        second_rows,
        first_rows,
        second_strip,
        first_strip,
    )
    edges, first, second, third, fourth = call(
        column_message_kernel,
        [(NEAR, 2, 8, 128), side, side, side, side],
        [],
        1_000_000,
        own_edges,
        recv_b,
        recv_a,
        strip_b,
        strip_a,
    )
    down, up = crossing(cols)
    recv_down = lax.ppermute(second, "col", down)
    recv_first = lax.cond(
        late, lambda m: m, lambda m: lax.ppermute(m, "col", part(cols, False)), first
    )
    blocks = [(19, 10, 8, 128), (5, 8, 8, 128), (FAR, 2, 8, 128)]
    scratch = [(5, 16, 8, 128)] * 3 + [(3, 14, 8, 128), (10, 8, 128)]
    *half_done, third_again, fourth_again = call(
        early_main_kernel,
        [*blocks, side, side],
        scratch,
        20_000_000,
        base,
        recv_b,
        recv_a,
        pops,
        third,
        fourth,
        recv_first,
    )
    recv_up = lax.ppermute(fourth_again, "col", up)
    recv_last, recv_b, recv_a = lax.cond(
        late,
        lambda m, b, a: (lax.ppermute(m, "col", part(cols, True)), *swap_rows(b, a)),
        lambda m, b, a: (m, b, a),
        third_again,
        recv_b,
        recv_a,
    )
    moved, relaxed, far_edges = call(
        late_main_kernel,
        blocks,
        scratch,
        20_000_000,
        base,
        recv_b,
        recv_a,
        pops,
        *half_done,
    )
    results = [(19, 64, 128), (5, 64, 128)]
    scratch = [
        (28, 4, 8, 128),
        (5, 4, 8, 128),
        (5, 4, 8, 128),
        *results,
        pltpu.SemaphoreType.DMA((len(CHUNKS) + 1,)),
    ]
    half_done = call(
        early_edge_kernel,
        results,
        scratch,
        8_000_000,
        edges,
        far_edges,
        recv_down,
        recv_first,
        moved,
        relaxed,
        to_hbm=True,
    )
    new_pops, new_order = call(
        late_edge_kernel,
        results,
        scratch,
        8_000_000,
        edges,
        far_edges,
        recv_up,
        recv_last,
        moved,
        relaxed,
        *half_done,
        hbm_args=(6, 7),
        to_hbm=True,
        aliases={6: 0, 7: 1},
    )
    return new_pops.reshape(populations.shape), new_order.reshape(order_tensor.shape)


def solution(mesh):
    spec = P(None, None, "row", "col")
    return jax.shard_map(
        functools.partial(body, mesh.shape["row"], mesh.shape["col"]),
        mesh=mesh,
        in_specs=(spec, spec),
        out_specs=(spec, spec),
        check_vma=False,
    )
```

```python
import functools
import math

import jax
import jax.numpy as jnp
import numpy as np
from jax import lax
from jax.experimental import pallas as pl
from jax.experimental.pallas import tpu as pltpu
from jax.sharding import PartitionSpec as P

lattice = np.array(
    [
        [0, 0, 0],
        [1, 0, 0],
        [-1, 0, 0],
        [0, 1, 0],
        [0, -1, 0],
        [0, 0, 1],
        [0, 0, -1],
        [1, 1, 0],
        [-1, -1, 0],
        [1, -1, 0],
        [-1, 1, 0],
        [1, 0, 1],
        [-1, 0, -1],
        [1, 0, -1],
        [-1, 0, 1],
        [0, 1, 1],
        [0, -1, -1],
        [0, 1, -1],
        [0, -1, 1],
    ]
)
tau_rate = 1.25
a_zero = 0.1
gamma_bulk = 3.0
stiffness = 0.4
pitch_wave = math.pi / 8.0
mobility_dt = 0.3

x_up = [i for i in range(19) if lattice[i][0] == 1]
x_down = [i + 1 for i in x_up]
y_up = [i for i in range(19) if lattice[i][1] == 1]
y_down = [i for i in range(19) if lattice[i][1] == -1]

VEL, DEN, POP, FACE = 20, 29, 30, 35
SLOTS = 16
near = sorted(y_up + y_down)
far = [i for i in range(19) if i not in near]
NEAR, FAR = 9 + len(near), len(far)
CHUNKS = (0, 7, 13)
f32 = jnp.float32


def lanes():
    return lax.broadcasted_iota(jnp.int32, (8, 128), 1)


def slots():
    return lax.rem(lanes(), SLOTS)


def roll_y(value, shift):
    shift = shift % 128
    return value if shift == 0 else pltpu.roll(value, shift, 1)


def roll_z(value, shift):
    shift = shift % 8
    return value if shift == 0 else pltpu.roll(value, shift, 0)


def is_even(axis):
    return lax.rem(lax.axis_index(axis), 2) == 0


def stencil(center, x_ahead, x_behind):
    y_ahead, y_behind = roll_y(center, -1), roll_y(center, 1)
    z_ahead, z_behind = roll_z(center, -1), roll_z(center, 1)
    around = (x_ahead + x_behind) + (y_ahead + y_behind) + (z_ahead + z_behind)
    return around, (x_ahead - x_behind, y_ahead - y_behind, z_ahead - z_behind)


def molecular_field(q, around, dx, dy, dz):
    q0, q1, q2, q3, q4 = q
    qzz = -(q0 + q3)
    s0, s1, s2, s3, s4 = q0 * q0, q1 * q1, q2 * q2, q3 * q3, q4 * q4
    square = s0 + s3 + qzz * qzz + 2.0 * (s1 + s2 + s4)
    third = square * (1.0 / 3.0)
    bulk = a_zero * gamma_bulk
    product = (
        s0 + s1 + s2 - third,
        q2 * q4 - q1 * qzz,
        q1 * q4 - q2 * q3,
        s1 + s3 + s4 - third,
        q1 * q2 - q4 * q0,
    )
    chiral = (
        2.0 * (dy[2] - dz[1]),
        (dy[4] - dx[2]) + (dz[0] - dz[3]),
        (dx[1] - dz[4]) - (2.0 * dy[0] + dy[3]),
        2.0 * (dz[1] - dx[4]),
        (dz[2] - dy[1]) + (dx[0] + 2.0 * dx[3]),
    )
    linear = a_zero * (gamma_bulk / 3.0 - 1.0) - stiffness * (4.0 * pitch_wave**2 + 6.0)
    factor = linear - bulk * square
    return [
        bulk * product[k]
        + factor * q[k]
        + stiffness * around[k]
        - (stiffness * pitch_wave) * chiral[k]
        for k in range(5)
    ]


def gather_stencil(load):
    q, around, dx, dy, dz = [], [], [], [], []
    for k in range(5):
        center, ahead, behind = load(k)
        total, (a, b, c) = stencil(center, ahead, behind)
        q.append(center)
        around.append(total)
        dx.append(a)
        dy.append(b)
        dz.append(c)
    return q, around, dx, dy, dz


def updated(q, field, dx, dy, dz, velocity):
    hx, hy, hz = (0.5 * v for v in velocity)
    return [
        q[k] + mobility_dt * field[k] - (hx * dx[k] + hy * dy[k] + hz * dz[k]) for k in range(5)
    ]


def force_of(field, dx, dy, dz):
    first = field[0] + 0.5 * field[3]
    second = field[3] + 0.5 * field[0]
    return [
        first * d[0] + second * d[3] + field[1] * d[1] + field[2] * d[2] + field[4] * d[4]
        for d in (dx, dy, dz)
    ]


def collide(which, load, density, velocity, force):
    half = 0.5 / density
    u = [velocity[a] + force[a] * half for a in range(3)]
    speed = u[0] * u[0] + u[1] * u[1] + u[2] * u[2]
    along = u[0] * force[0] + u[1] * force[1] + u[2] * force[2]
    keep = 1.0 - 0.5 * tau_rate
    base = (tau_rate * density) * (1.0 - 1.5 * speed) - (3.0 * keep) * along
    odd = [(3.0 * tau_rate) * density * u[a] + (3.0 * keep) * force[a] for a in range(3)]
    even = [(4.5 * tau_rate) * density * u[a] + (9.0 * keep) * force[a] for a in range(3)]

    def dot(c, vector):
        total = None
        for a in range(3):
            if c[a]:
                term = vector[a]
                if total is None:
                    total = term if c[a] > 0 else -term
                else:
                    total = total + term if c[a] > 0 else total - term
        return total

    rest = 1.0 - tau_rate
    done = set()
    for i in which:
        if i in done:
            continue
        if i == 0:
            yield 0, rest * load(0) + (1.0 / 3.0) * base
            continue
        low = i if i % 2 else i - 1
        c = [int(v) for v in lattice[low]]
        weight = 1.0 / 18.0 if low < 7 else 1.0 / 36.0
        first = weight * (base + dot(c, u) * dot(c, even))
        second = weight * dot(c, odd)
        for j, sign in ((low, 1), (low + 1, -1)):
            if j in which:
                done.add(j)
                yield j, rest * load(j) + (first + second if sign > 0 else first - second)


def moments_kernel(
    pop_hbm, order_hbm, base_ref, first_ref, second_ref, pop_ref, order_ref, sems
):
    copies = [
        pltpu.make_async_copy(order_hbm, order_ref, sems.at[0]),
        pltpu.make_async_copy(pop_hbm, pop_ref, sems.at[1]),
    ]
    for copy in copies:
        copy.start()
    for copy in copies:
        copy.wait()

    def row(x, carry):
        p = [pop_ref[i, pl.ds(x, 8, stride=8), :] for i in range(19)]
        density = p[0]
        for i in range(1, 19):
            density = density + p[i]
        inverse = 1.0 / density
        for a in range(3):
            plus = [p[i] for i in range(19) if lattice[i][a] == 1]
            minus = [p[i] for i in range(19) if lattice[i][a] == -1]
            momentum = functools.reduce(lambda s, t: s + t, plus) - functools.reduce(
                lambda s, t: s + t, minus
            )
            base_ref[5 + a, x] = momentum * inverse
        base_ref[8, x] = density
        for k in range(5):
            base_ref[k, x] = order_ref[k, pl.ds(x, 8, stride=8), :]
        return carry

    lax.fori_loop(0, 8, row, 0, unroll=8)
    even = is_even("row")
    for out, high in ((first_ref, even), (second_ref, jnp.logical_not(even))):

        @pl.when(high)
        def _():
            for k in range(5):
                out[4 * k : 4 * k + 4] = base_ref[k, 4:8]
            for a in range(3):
                out[VEL + 3 * a : VEL + 3 * a + 3] = base_ref[5 + a, 5:8]
            out[DEN] = base_ref[8, 7]
            for j, i in enumerate(x_up):
                out[POP + j] = pop_ref[i, pl.ds(7, 8, stride=8), :]

        @pl.when(jnp.logical_not(high))
        def _():
            for k in range(5):
                out[4 * k : 4 * k + 4] = base_ref[k, 0:4]
            for a in range(3):
                out[VEL + 3 * a : VEL + 3 * a + 3] = base_ref[5 + a, 0:3]
            out[DEN] = base_ref[8, 0]
            for j, i in enumerate(x_down):
                out[POP + j] = pop_ref[i, pl.ds(0, 8, stride=8), :]


def placed(value, row, into):
    q = row % 8
    lane = lanes()
    mask = jnp.logical_and(lane >= SLOTS * q, lane < SLOTS * q + SLOTS)
    return jnp.where(mask, roll_y(value, 8 + SLOTS * q), into)


def own_edges_kernel(base_ref, pop_ref, edge_ref):
    def pack(load, fill, field):
        low = high = jnp.full((8, 128), fill, f32)
        for x in range(4):
            low = placed(load(x), x + 4, low)
            high = placed(load(x + 4), x + 8, high)
        edge_ref[field, 0] = low
        edge_ref[field, 1] = high

    for f in range(9):
        pack(lambda x, f=f: base_ref[f, x], 1.0 if f == 8 else 0.0, f)
    for n, i in enumerate(near):
        pack(lambda x, i=i: pop_ref[i, pl.ds(x, 8, stride=8), :], 0.0, 9 + n)


def column_message_kernel(
    own_ref, recv_b, recv_a, edge_ref, first_ref, second_ref, third_ref, fourth_ref
):
    even = is_even("row")
    slot = slots()

    def halo(j):
        a, b = recv_a[j], recv_b[j]
        return jnp.where(even, b, a), jnp.where(even, a, b)

    def widen(field, rows):
        low, high = own_ref[field, 0], own_ref[field, 1]
        for j, row_low, row_high in rows:
            below, above = halo(j)
            low, high = placed(below, row_low, low), placed(above, row_high, high)
        edge_ref[field, 0] = low
        edge_ref[field, 1] = high

    for k in range(5):
        widen(k, [(4 * k + r, r, 12 + r) for r in range(4)])
    for a in range(3):
        widen(5 + a, [(VEL + 3 * a + r, 1 + r, 12 + r) for r in range(3)])
    widen(8, [(DEN, 3, 12)])
    for n, i in enumerate(near):
        low, high = own_ref[9 + n, 0], own_ref[9 + n, 1]
        if i in x_up:
            low = placed(halo(POP + x_up.index(i))[0], 3, low)
        if i in x_down:
            high = placed(halo(POP + x_down.index(i))[1], 12, high)
        edge_ref[9 + n, 0] = low
        edge_ref[9 + n, 1] = high

    col_even = is_even("col")
    for h in range(2):
        for g, parts in enumerate(((0, 1, 2, 3), (4, 5, 6, 7))):
            to_left = to_right = jnp.zeros((8, 128), f32)
            for u, f in enumerate(parts):
                value = edge_ref[f, h]
                mask = jnp.logical_and(slot >= 4 * u, slot < 4 * u + 4)
                to_left = jnp.where(mask, roll_y(value, 4 * u - 8), to_left)
                to_right = jnp.where(mask, roll_y(value, 4 * u - 4), to_right)
            first_ref[2 * g + h] = third_ref[2 * g + h] = jnp.where(col_even, to_right, to_left)
            second_ref[2 * g + h] = fourth_ref[2 * g + h] = jnp.where(col_even, to_left, to_right)
        to_left = to_right = jnp.zeros((8, 128), f32)
        for s in range(6):
            left_field = 8 if s == 0 else 9 + near.index(y_down[s - 1])
            right_field = 8 if s == 0 else 9 + near.index(y_up[s - 1])
            to_left = jnp.where(slot == s, roll_y(edge_ref[left_field, h], s - 8), to_left)
            to_right = jnp.where(slot == s, roll_y(edge_ref[right_field, h], s - 7), to_right)
        first_ref[4 + h] = third_ref[4 + h] = jnp.where(col_even, to_right, to_left)
        second_ref[4 + h] = fourth_ref[4 + h] = jnp.where(col_even, to_left, to_right)


def is_late():
    return lax.rem(lax.axis_index("col"), 4) >= 2


def early_main_kernel(base_ref, recv_b, recv_a, pop_ref, third_ref, fourth_ref, _, *rest):
    outputs, scratch = rest[:3], rest[5:]
    rest[3][...] = third_ref[...]
    rest[4][...] = fourth_ref[...]

    @pl.when(jnp.logical_not(is_late()))
    def _():
        main_block(base_ref, recv_b, recv_a, pop_ref, *outputs, *scratch)


def late_main_kernel(base_ref, recv_b, recv_a, pop_ref, *rest):
    done, outputs, scratch = rest[:3], rest[3:6], rest[6:]

    @pl.when(is_late())
    def _():
        main_block(base_ref, recv_b, recv_a, pop_ref, *outputs, *scratch)

    @pl.when(jnp.logical_not(is_late()))
    def _():
        for source, target in zip(done, outputs):
            target[...] = source[...]


def main_block(
    base_ref,
    recv_b,
    recv_a,
    pop_ref,
    moved_ref,
    order_ref,
    far_ref,
    q_zero,
    q_one,
    q_two,
    vel,
    den,
):
    even = is_even("row")

    def halo(j):
        a, b = recv_a[j], recv_b[j]
        return jnp.where(even, b, a), jnp.where(even, a, b)

    for k in range(5):
        q_zero[k, 4:12] = base_ref[k]
        for r in range(4):
            q_zero[k, r], q_zero[k, 12 + r] = halo(4 * k + r)
    for a in range(3):
        vel[a, 3:11] = base_ref[5 + a]
        for r in range(3):
            vel[a, r], vel[a, 11 + r] = halo(VEL + 3 * a + r)
    den[0], den[9] = halo(DEN)

    def relax(source, target):
        def row(r, carry):
            q, around, dx, dy, dz = gather_stencil(
                lambda k: (source[k, r], source[k, r + 1], source[k, r - 1])
            )
            field = molecular_field(q, around, dx, dy, dz)
            new = updated(q, field, dx, dy, dz, [vel[a, r - 1] for a in range(3)])
            for k in range(5):
                target[k, r] = new[k]
            return carry

        return row

    lax.fori_loop(1, 15, relax(q_zero, q_one), 0, unroll=7)
    lax.fori_loop(2, 14, relax(q_one, q_two), 0, unroll=6)

    def last(x):
        q, around, dx, dy, dz = gather_stencil(
            lambda k: (q_two[k, x + 4], q_two[k, x + 5], q_two[k, x + 3])
        )
        field = molecular_field(q, around, dx, dy, dz)
        velocity = [vel[a, x + 3] for a in range(3)]
        return q, field, dx, dy, dz, velocity, force_of(field, dx, dy, dz)

    def stream(i, value, row):
        a, b, c = (int(v) for v in lattice[i])
        moved_ref[i, row + a] = roll_y(roll_z(value, c), b)

    def own_row(x, carry):
        q, field, dx, dy, dz, velocity, force = last(x)
        new = updated(q, field, dx, dy, dz, velocity)
        for k in range(5):
            order_ref[k, x] = new[k]
        for i, value in collide(
            range(19),
            lambda i: pop_ref[i, pl.ds(x, 8, stride=8), :],
            base_ref[8, x],
            velocity,
            force,
        ):
            stream(i, value, x + 1)
        return carry

    lax.fori_loop(0, 8, own_row, 0, unroll=8)

    for n, i in enumerate(far):
        low = high = jnp.zeros((8, 128), f32)
        for x in range(4):
            low = placed(pop_ref[i, pl.ds(x, 8, stride=8), :], x + 4, low)
            high = placed(pop_ref[i, pl.ds(x + 4, 8, stride=8), :], x + 8, high)
        if i in x_up:
            low = placed(halo(POP + x_up.index(i))[0], 3, low)
        if i in x_down:
            high = placed(halo(POP + x_down.index(i))[1], 12, high)
        far_ref[n, 0] = low
        far_ref[n, 1] = high

    for x, which, side in ((-1, x_up, 0), (8, x_down, 1)):
        _, _, _, _, _, velocity, force = last(x)
        for i, value in collide(
            which,
            lambda i, which=which, side=side: halo(POP + which.index(i))[side],
            den[9 * side],
            velocity,
            force,
        ):
            stream(i, value, x + 1)


def early_edge_kernel(edge_ref, far_ref, recv_down, recv_first, moved_ref, order_ref, *rest):
    @pl.when(jnp.logical_not(is_late()))
    def _():
        edge_block(edge_ref, far_ref, recv_down, recv_first, moved_ref, order_ref, *rest)


def late_edge_kernel(edge_ref, far_ref, recv_up, recv_last, moved_ref, order_ref, *rest):
    @pl.when(is_late())
    def _():
        edge_block(edge_ref, far_ref, recv_up, recv_last, moved_ref, order_ref, *rest[2:])


def edge_block(
    edge_ref,
    far_ref,
    recv_b,
    recv_a,
    moved_ref,
    order_ref,
    new_pop,
    new_order,
    strip,
    q_one,
    q_two,
    pop_out,
    order_out,
    sems,
):
    even = is_even("col")
    slot, lane = slots(), lanes()

    def columns(j):
        a, b = recv_a[j], recv_b[j]
        return jnp.where(even, b, a), jnp.where(even, a, b)

    for h in range(2):
        for f in range(8):
            from_left, from_right = columns(2 * (f // 4) + h)
            u = f % 4
            own = edge_ref[f, h]
            strip[f, h] = jnp.where(slot < 8, roll_y(from_left, 4 - 4 * u), own)
            strip[f, 2 + h] = jnp.where(slot < 8, own, roll_y(from_right, 8 - 4 * u))
        from_left, from_right = columns(4 + h)
        for f in range(8, 28):
            i = f - 9
            if f == 8:
                own = edge_ref[8, h]
            elif i in near:
                own = edge_ref[9 + near.index(i), h]
            else:
                own = far_ref[far.index(i), h]
            left = right = own
            if f == 8 or i in y_up:
                s = 0 if f == 8 else 1 + y_up.index(i)
                left = jnp.where(slot == 7, roll_y(from_left, 7 - s), left)
            if f == 8 or i in y_down:
                s = 0 if f == 8 else 1 + y_down.index(i)
                right = jnp.where(slot == 8, roll_y(from_right, 8 - s), right)
            strip[f, h] = left
            strip[f, 2 + h] = right

    def neighbours(source, unit):
        other = unit ^ 1

        def load(k):
            me, that = source[k, unit], source[k, other]
            ahead = jnp.where(lane >= 112, roll_y(that, -16), roll_y(me, -16))
            behind = jnp.where(lane < 16, roll_y(that, 16), roll_y(me, 16))
            return me, ahead, behind

        return load

    def relax(source, target):
        def step(unit, carry):
            q, around, dx, dy, dz = gather_stencil(neighbours(source, unit))
            field = molecular_field(q, around, dx, dy, dz)
            return updated(q, field, dx, dy, dz, [strip[5 + a, unit] for a in range(3)])

        results = [step(unit, 0) for unit in range(4)]
        for unit in range(4):
            for k in range(5):
                target[k, unit] = results[unit][k]

    relax(strip, q_one)
    relax(q_one, q_two)

    edge_lane = jnp.logical_or(lane < 4, lane >= 124)

    def merge(field, units, load, shift_x, shift_y, target):
        halves = [jnp.where(slot < 8 - shift_y, units[2 + h], units[h]) for h in range(2)]
        rows = []
        for x in range(8):
            row = x + 4 - shift_x
            pair = roll_y(halves[row // 8], shift_y - (SLOTS * (row % 8) + 8))
            rows.append(jnp.where(edge_lane, pair, load(x)))
        for x in range(8):
            target[field, pl.ds(x, 8, stride=8), :] = rows[x]

    copies = [pltpu.make_async_copy(order_out, new_order, sems.at[0])]
    bounds = CHUNKS + (19,)
    for n, first in enumerate(CHUNKS):
        rows = pl.ds(first, bounds[n + 1] - first)
        copies.append(pltpu.make_async_copy(pop_out.at[rows], new_pop.at[rows], sems.at[n + 1]))

    relaxed, moving = [], []
    for unit in range(4):
        q, around, dx, dy, dz = gather_stencil(neighbours(q_two, unit))
        field = molecular_field(q, around, dx, dy, dz)
        velocity = [strip[5 + a, unit] for a in range(3)]
        relaxed.append(updated(q, field, dx, dy, dz, velocity))
        force = force_of(field, dx, dy, dz)
        moving.append(
            collide(
                range(19),
                lambda i, unit=unit: strip[9 + i, unit],
                strip[8, unit],
                velocity,
                force,
            )
        )
    for k in range(5):
        merge(k, [new[k] for new in relaxed], lambda x, k=k: order_ref[k, x], 0, 0, order_out)
    copies[0].start()
    for items in zip(*moving):
        i = items[0][0]
        a, b, c = (int(v) for v in lattice[i])
        units = [roll_z(value, c) for _, value in items]
        merge(i, units, lambda x, i=i: moved_ref[i, x + 1], a, b, pop_out)
        if i + 1 in bounds:
            copies[bounds.index(i + 1)].start()
    for copy in copies:
        copy.wait()


def call(kernel, out_shapes, scratch, flops, *args, hbm_args=(), to_hbm=False, aliases=None):
    whole, outside = (pl.BlockSpec(memory_space=m) for m in (pltpu.VMEM, pltpu.HBM))
    return pl.pallas_call(
        kernel,
        out_shape=[jax.ShapeDtypeStruct(s, f32) for s in out_shapes],
        in_specs=[outside if n in hbm_args else whole for n in range(len(args))],
        out_specs=[outside if to_hbm else whole] * len(out_shapes),
        scratch_shapes=[pltpu.VMEM(s, f32) if isinstance(s, tuple) else s for s in scratch],
        cost_estimate=pl.CostEstimate(
            flops=flops,
            bytes_accessed=4 * sum(math.prod(s) for s in out_shapes) + sum(4 * a.size for a in args),
            transcendentals=0,
        ),
        input_output_aliases=aliases or {},
        compiler_params=pltpu.CompilerParams(vmem_limit_bytes=12 * 1024 * 1024),
    )(*args)


def swap(size, first):
    return [
        (i, (i + 1) % size if i % 2 == first else (i - 1) % size) for i in range(size)
    ]


def crossing(size):
    down = [(i, (i + 1) % size if i % 2 else i - 1) for i in range(size) if i % 4 >= 2]
    return down, [(target, source) for source, target in down]


def part(size, late):
    return [(i, i ^ 1) for i in range(size) if (i % 4 >= 2) == late]


def body(rows, cols, populations, order_tensor):
    face, side = (FACE, 8, 128), (6, 8, 128)
    base, first, second, pops = call(
        moments_kernel,
        [(9, 8, 8, 128), face, face, (19, 64, 128)],
        [(5, 64, 128), pltpu.SemaphoreType.DMA((2,))],
        2_000_000,
        pltpu.with_memory_space_constraint(populations.reshape(19, 64, 128), pltpu.HBM),
        pltpu.with_memory_space_constraint(order_tensor.reshape(5, 64, 128), pltpu.HBM),
        hbm_args=(0, 1),
    )
    recv_b = lax.ppermute(second, "row", swap(rows, 1))
    recv_a = lax.ppermute(first, "row", swap(rows, 0))
    own_edges = call(own_edges_kernel, [(NEAR, 2, 8, 128)], [], 2_000_000, base, pops)[0]
    edges, first, second, third, fourth = call(
        column_message_kernel,
        [(NEAR, 2, 8, 128), side, side, side, side],
        [],
        1_000_000,
        own_edges,
        recv_b,
        recv_a,
    )
    down, up = crossing(cols)
    recv_down = lax.ppermute(second, "col", down)
    late = lax.rem(lax.axis_index("col"), 4) >= 2
    recv_first = lax.cond(
        late, lambda m: m, lambda m: lax.ppermute(m, "col", part(cols, False)), first
    )
    blocks = [(19, 10, 8, 128), (5, 8, 8, 128), (FAR, 2, 8, 128)]
    scratch = [(5, 16, 8, 128)] * 3 + [(3, 14, 8, 128), (10, 8, 128)]
    *half_done, third_again, fourth_again = call(
        early_main_kernel,
        [*blocks, side, side],
        scratch,
        20_000_000,
        base,
        recv_b,
        recv_a,
        pops,
        third,
        fourth,
        recv_first,
    )
    recv_up = lax.ppermute(fourth_again, "col", up)
    recv_last = lax.cond(
        late, lambda m: lax.ppermute(m, "col", part(cols, True)), lambda m: m, third_again
    )
    moved, relaxed, far_edges = call(
        late_main_kernel,
        blocks,
        scratch,
        20_000_000,
        base,
        recv_b,
        recv_a,
        pops,
        *half_done,
    )
    results = [(19, 64, 128), (5, 64, 128)]
    scratch = [
        (28, 4, 8, 128),
        (5, 4, 8, 128),
        (5, 4, 8, 128),
        *results,
        pltpu.SemaphoreType.DMA((len(CHUNKS) + 1,)),
    ]
    half_done = call(
        early_edge_kernel,
        results,
        scratch,
        8_000_000,
        edges,
        far_edges,
        recv_down,
        recv_first,
        moved,
        relaxed,
        to_hbm=True,
    )
    new_pops, new_order = call(
        late_edge_kernel,
        results,
        scratch,
        8_000_000,
        edges,
        far_edges,
        recv_up,
        recv_last,
        moved,
        relaxed,
        *half_done,
        hbm_args=(6, 7),
        to_hbm=True,
        aliases={6: 0, 7: 1},
    )
    return new_pops.reshape(populations.shape), new_order.reshape(order_tensor.shape)


def solution(mesh):
    spec = P(None, None, "row", "col")
    return jax.shard_map(
        functools.partial(body, mesh.shape["row"], mesh.shape["col"]),
        mesh=mesh,
        in_specs=(spec, spec),
        out_specs=(spec, spec),
        check_vma=False,
    )
```
